128 devices in a mesh: gx: 8 (over x, z_hi), gy: 16 (over y, z_lo, core).
Axes of the slice: x: 4, y: 4, z: 4 (z_hi: 2, z_lo: 2; z = z_hi * 2 + z_lo), core: 2. Of those that a mesh axis runs over, the one named last changes fastest.
Arguments:
- pre_act: bfloat16 [64, 64, 16, 512], P('gy', 'gx'), may hold values from -6 to 6
- cot: bfloat16 [64, 64, 16, 512], P('gy', 'gx'), may hold values from -6 to 6
- weight: bfloat16 [27, 512, 512], P(None, 'gy'), may hold values from -0.0546875 to 0.0546875
Outputs:
- grad_pre: bfloat16 [64, 64, 16, 512], P('gy', 'gx')
- grad_weight: float32 [27, 512, 512], P(None, 'gy')
The draws below stay inside these ranges and needn't reach their ends.
All inputs are finite; a program needn't handle non-finite values.
Results may differ from the reference program's by a relative error of at most 0.0029.
Values may be sent and summed in bfloat16 or wider, within the bound.
No kernel may reach another device: no remote copies, remote signals or barrier semaphores. Data moves between devices by JAX's collectives and lax.ppermute only.
A program may use at most 192 MiB of HBM per device.

```python
import math
import jax
import jax.numpy as jnp

CH = 512
ZS = 16
NX = 64
NY = 64


def steps_of(own_key, extent, shards, low, top_value):
    def one(axis_at, parts):
        draws = jax.random.uniform(jax.random.fold_in(jax.random.fold_in(own_key, 6), axis_at), (parts,), jnp.float32, low / len(shards), top_value / len(shards))
        return jnp.repeat(jnp.exp(draws), extent[axis_at] // parts).reshape((-1,) + (1,) * (len(extent) - axis_at - 1))

    level = one(*shards[0])
    for cut in shards[1:]:
        level = level * one(*cut)
    return level


def centred(key, dims, spread, bound, pieces=(), kind=jnp.bfloat16):
    values = spread * jax.random.normal(key, dims, jnp.float32)
    if pieces:
        values = values * steps_of(key, dims, pieces, -0.22, 0.18)
    return jnp.clip(values, -bound, bound).astype(kind)


def setup_inputs(seed: int = 0) -> dict:
    streams_of = jax.random.split(jax.random.key(seed), 4)
    pre_act = centred(streams_of[0], (NY, NX, ZS, CH), 1.5, 6.0, ((0, 16), (1, 8)))
    cot = centred(streams_of[1], (NY, NX, ZS, CH), 1.0, 6.0, ((0, 16), (1, 8)))
    weight = centred(streams_of[2], (27, CH, CH), (27 * CH) ** -0.5, 0.0546875, ((1, 16),))
    return dict(pre_act=pre_act, cot=cot, weight=weight)


def tap_offsets():
    return [(a, b, c) for a in (-1, 0, 1) for b in (-1, 0, 1) for c in (-1, 0, 1)]

def shifted(field, a, b, c):
    padded = jnp.pad(field, ((1, 1), (1, 1), (1, 1), (0, 0)))
    rows, width, depth = (field.shape[0], field.shape[1], field.shape[2])
    return padded[1 - a:1 - a + rows, 1 - b:1 - b + width, 1 - c:1 - c + depth, :]

def reference(pre_act, cot, weight):
    pre32 = pre_act.astype(jnp.float32)
    sig = jax.nn.sigmoid(pre32)
    act = (pre32 * sig).astype(jnp.bfloat16)
    act_flat = act.reshape(-1, CH)
    grad_act = jnp.zeros(pre_act.shape, jnp.float32)
    grads = []
    for index, (a, b, c) in enumerate(tap_offsets()):
        moved = shifted(cot, a, b, c)
        grad_act = grad_act + jnp.dot(moved, weight[index], preferred_element_type=jnp.float32)
        grads.append(jnp.dot(moved.reshape(-1, CH).T, act_flat, preferred_element_type=jnp.float32))
    norm = 1.0 / math.sqrt(NY * NX * ZS)
    grad_weight = jnp.stack(grads) * norm
    grad_pre = (grad_act * sig * (1.0 + pre32 * (1.0 - sig))).astype(jnp.bfloat16)
    return (grad_pre, grad_weight)
```

```python
import functools
import math

import jax
import jax.numpy as jnp
from jax import lax
from jax.experimental import pallas as pl
from jax.experimental.pallas import tpu as pltpu
from jax.sharding import PartitionSpec as P

QUAD = 4
RING = 4
F32 = jnp.float32
BF16 = jnp.bfloat16
ANY = pl.BlockSpec(memory_space=pl.ANY)
VMEM = pl.BlockSpec(memory_space=pltpu.VMEM)
LIMIT = 56 * 1024 * 1024


def params():
    return pltpu.CompilerParams(vmem_limit_bytes=LIMIT)


def quad_place():
    return lax.rem(lax.axis_index("gy"), QUAD)


def x_place():
    return lax.div(lax.axis_index("gx"), 2)


def swap(block, k):
    count = lax.axis_size("gy")
    return lax.ppermute(block, "gy", [(g, g ^ k) for g in range(count)])


def swap_far(block, k):
    nx, ny = lax.axis_size("gx"), lax.axis_size("gy")
    far = (k >> 1) & 1
    pairs = [(g * ny + h, (g ^ far) * ny + (h ^ k)) for g in range(nx) for h in range(ny)]
    return lax.ppermute(block, ("gx", "gy"), pairs)


def along_y(block, step, ring):
    count = lax.axis_size("gy")
    pairs = [(g, g + QUAD * step) for g in range(count)]
    if ring:
        pairs = [(s, t % count) for s, t in pairs]
    return lax.ppermute(block, "gy", [(s, t) for s, t in pairs if 0 <= t < count])


def along_x(block, step):
    count = lax.axis_size("gx")
    return lax.ppermute(block, "gx", [(g, (g + 2 * step) % count) for g in range(count)])


def zero_at(value, z, edge):
    return jnp.where(z == edge, 0.0, value)


def act_kernel(p0, p1, p2, p3, out):
    j = quad_place()
    for k, p in enumerate((p0, p1, p2, p3)):
        rows, width, depth, q = p.shape
        cells = rows * width * depth
        pre = p[...].reshape(cells, q).astype(F32)
        act = pre * jax.nn.sigmoid(pre)
        z = lax.rem(lax.broadcasted_iota(jnp.int32, (cells, q), 0), depth)
        low = zero_at(pltpu.roll(act, 1, 0), z, 0)
        high = zero_at(pltpu.roll(act, cells - 1, 0), z, depth - 1)
        at = pl.multiple_of((j ^ k) * cells, cells)
        for c, moved in enumerate((low, act, high)):
            out[c * q:(c + 1) * q, pl.ds(at, cells)] = moved.T.astype(BF16)


def load_cot(pieces, rims, edges, held, sem):
    j = quad_place()
    rows, width = pieces[0].shape[:2]
    copies = []

    def copy(src, dst):
        copies.append(pltpu.make_async_copy(src, dst, sem.at[len(copies)]))
        copies[-1].start()

    for k in range(QUAD):
        at = 1 + (j ^ k) * rows
        copy(pieces[k], held.at[pl.ds(at, rows), pl.ds(1, width)])
        copy(rims[k].at[0], held.at[pl.ds(at, rows), 0])
        copy(rims[k].at[1], held.at[pl.ds(at, rows), width + 1])
    for side, edge in zip((0, held.shape[0] - 1), edges):
        copy(edge, held.at[side])
    for c in copies:
        c.wait()


def weight_kernel(first, count, norm, *refs):
    pieces, rims = refs[:4], refs[4:8]
    refs = refs[8:]
    edges, refs = ((), refs) if (first, count) == (0, 1) else (refs[:2], refs[2:])
    act, right, left, keep_right, keep_left, own, held, turned, sem = refs
    load_cot(pieces, rims, edges, held, sem)
    x = x_place()
    rows, width, depth, chan = held.shape
    rows, width = rows - 2, width - 2
    q = act.shape[0] // 3
    groups, _, small, _ = turned.shape
    half = groups // 2

    def step(n, carry):
        a = first + 2 * lax.div(n, 3) if count == 2 else first + lax.div(n, 3)
        b = lax.rem(n, 3) - 1
        moved = held[pl.ds(1 - a, rows), pl.ds(1 - b, width)].reshape(rows * width * depth, chan)
        term = jnp.dot(act[...], moved, preferred_element_type=F32) * norm
        for c in range(3):
            turned[...] = term[c * q:(c + 1) * q].T.reshape(turned.shape)
            tap = 3 * n + c

            def block(r):
                at = lax.rem(x + r, RING)
                v = turned[:, pl.ds(at, 1)].reshape(groups, small, q)
                return v[:half].reshape(half * small, q), v[half:].reshape(half * small, q)

            v0, v1 = block(2)
            right[0, tap] = v0.astype(BF16)
            left[0, tap] = v1.astype(BF16)
            v0, v1 = block(1)
            keep_right[tap] = v0
            right[1, tap] = v1.astype(BF16)
            v0, v1 = block(3)
            left[1, tap] = v0.astype(BF16)
            keep_left[tap] = v1
            v0, v1 = block(0)
            own[0, tap] = v0
            own[1, tap] = v1
        return carry

    lax.fori_loop(0, 3 * count, step, 0)


def weight_terms(first, count, norm, pieces, rims, edges, act):
    rows, width, depth, chan = pieces[0].shape
    q = chan // QUAD
    taps = 9 * count
    half = chan // RING // 2
    small = chan // 16 // RING
    cells = QUAD * rows * width * depth
    ins = (*pieces, *rims, *edges, act)
    shapes = [
        jax.ShapeDtypeStruct((2, taps, half, q), BF16),
        jax.ShapeDtypeStruct((2, taps, half, q), BF16),
        jax.ShapeDtypeStruct((taps, half, q), F32),
        jax.ShapeDtypeStruct((taps, half, q), F32),
        jax.ShapeDtypeStruct((2, taps, half, q), F32),
    ]
    return pl.pallas_call(
        functools.partial(weight_kernel, first, count, norm),
        out_shape=shapes,
        in_specs=[ANY] * (len(ins) - 1) + [VMEM],
        out_specs=[VMEM] * 5,
        scratch_shapes=[
            pltpu.VMEM((QUAD * rows + 2, width + 2, depth, chan), BF16),
            pltpu.VMEM((16, RING, small, q), F32),
            pltpu.SemaphoreType.DMA((14,)),
        ],
        compiler_params=params(),
        cost_estimate=pl.CostEstimate(
            flops=2 * taps * cells * chan * q, bytes_accessed=10_000_000, transcendentals=0
        ),
    )(*ins)


def input_kernel(*refs):
    pieces, rims, edges = refs[:4], refs[4:8], refs[8:10]
    parts = refs[10:14]
    pres = refs[14:18]
    outs = refs[18:22]
    held, weights, sem, wsem = refs[22:]
    j = quad_place()
    y = lax.div(lax.axis_index("gy"), QUAD)
    copies = []
    for s, part in enumerate(parts):
        own = part.shape[2]
        for k in range(QUAD):
            at = (lax.rem(y + s, RING) * QUAD + (j ^ k)) * own
            at = pl.multiple_of(at, own)
            copies.append(
                pltpu.make_async_copy(
                    part.at[k], weights.at[:, pl.ds(at, own)], wsem.at[s * QUAD + k]
                )
            )
            copies[-1].start()
    load_cot(pieces, rims, edges, held, sem)
    for c in copies:
        c.wait()
    rows, width, depth, q = pres[0].shape
    cells = rows * width * depth
    chan = held.shape[3]
    for k in range(QUAD):
        at = (j ^ k) * rows
        total = jnp.zeros((cells, 3 * q), F32)
        for n in range(9):
            a, b = n // 3 - 1, n % 3 - 1
            moved = held[pl.ds(at + 1 - a, rows), 1 - b:1 - b + width].reshape(cells, chan)
            total = total + jnp.dot(moved, weights[n], preferred_element_type=F32)
        z = lax.rem(lax.broadcasted_iota(jnp.int32, (cells, q), 0), depth)
        grad = total[:, q:2 * q]
        grad = grad + zero_at(pltpu.roll(total[:, :q], cells - 1, 0), z, depth - 1)
        grad = grad + zero_at(pltpu.roll(total[:, 2 * q:], 1, 0), z, 0)
        pre = pres[k][...].reshape(cells, q).astype(F32)
        s = jax.nn.sigmoid(pre)
        grad = grad * s * (1.0 + pre * (1.0 - s))
        outs[k][...] = grad.astype(BF16).reshape(outs[k].shape)


def input_terms(pieces, rims, edges, parts, pres):
    rows, width, depth, chan = pieces[0].shape
    q = chan // QUAD
    cells = QUAD * rows * width * depth
    return pl.pallas_call(
        input_kernel,
        out_shape=[jax.ShapeDtypeStruct((rows, width, depth, q), BF16)] * QUAD,
        in_specs=[ANY] * 14 + [VMEM] * 4,
        out_specs=[VMEM] * QUAD,
        scratch_shapes=[
            pltpu.VMEM((QUAD * rows + 2, width + 2, depth, chan), BF16),
            pltpu.VMEM((9, chan, 3 * q), BF16),
            pltpu.SemaphoreType.DMA((14,)),
            pltpu.SemaphoreType.DMA((16,)),
        ],
        compiler_params=params(),
        cost_estimate=pl.CostEstimate(
            flops=2 * 27 * cells * chan * q, bytes_accessed=10_000_000, transcendentals=0
        ),
    )(*pieces, *rims, *edges, *parts, *pres)


def join_kernel(axis, place, *refs):
    pieces, out, sem = refs[:-2], refs[-2], refs[-1]
    size = pieces[0].shape[axis]
    copies = []
    for k, piece in enumerate(pieces):
        at = pl.multiple_of(place(k) * size, size)
        spot = out.at[(slice(None),) * axis + (pl.ds(at, size),)]
        copies.append(pltpu.make_async_copy(piece, spot, sem.at[k]))
        copies[-1].start()
    for c in copies:
        c.wait()


def join(pieces, axis, place):
    shape = list(pieces[0].shape)
    shape[axis] *= len(pieces)
    return pl.pallas_call(
        functools.partial(join_kernel, axis, place),
        out_shape=jax.ShapeDtypeStruct(tuple(shape), pieces[0].dtype),
        in_specs=[ANY] * len(pieces),
        out_specs=ANY,
        scratch_shapes=[pltpu.SemaphoreType.DMA((len(pieces),))],
        compiler_params=params(),
    )(*pieces)


def reduce_x(right, left, keep_right, keep_left, own):
    from_left = along_x(right, 1)
    from_right = along_x(left, -1)
    next_right = (from_left[0].astype(F32) + keep_right).astype(BF16)
    next_left = (from_right[0].astype(F32) + keep_left).astype(BF16)
    last_left = along_x(next_right, 1)
    last_right = along_x(next_left, -1)
    low = own[0] + from_right[1].astype(F32) + last_left.astype(F32)
    high = own[1] + from_left[1].astype(F32) + last_right.astype(F32)
    return jnp.concatenate([low, high], axis=1)


def reduce_rest(total, owned):
    y = lax.div(lax.axis_index("gy"), QUAD)
    j = quad_place()
    size = total.shape[1] // RING

    def block(r):
        return lax.dynamic_slice_in_dim(total, lax.rem(y + r, RING) * size, size, axis=1)

    mine = block(0)
    for r in (1, 2, 3):
        mine = mine + along_y(block(r).astype(BF16), r, True).astype(F32)
    count = lax.axis_size("gx")
    other = lax.ppermute(mine.astype(BF16), "gx", [(g, g ^ 1) for g in range(count)])
    mine = mine + other.astype(F32)
    small = size // QUAD

    def part(k):
        return lax.dynamic_slice_in_dim(mine, (j ^ k) * small, small, axis=1)

    pieces = [part(0)] + [swap(part(k), k) for k in (1, 2, 3)]
    whole = join(pieces, 2, lambda k: quad_place() ^ k)
    parts = [whole, along_x(whole, 1), along_x(whole, 2), along_x(whole, -1)]
    return join(parts, 1, lambda k: lax.rem(x_place() + RING - k, RING))


def body(pre_act, cot, weight):
    rows, width, depth, chan = pre_act.shape
    owned = weight.shape[1]
    q = chan // QUAD
    norm = 1.0 / math.sqrt(rows * lax.axis_size("gy") * width * lax.axis_size("gx") * depth)
    j = quad_place()
    nx = lax.axis_size("gx")

    from_low = lax.ppermute(cot[:, width - 1], "gx", [(g, g + 1) for g in range(nx - 1)])
    from_high = lax.ppermute(cot[:, 0], "gx", [(g + 1, g) for g in range(nx - 1)])
    far = swap(cot, 2)
    pieces = [cot, swap(cot, 1), far, swap(far, 1)]
    rim = jnp.stack([from_low, from_high])
    rim_far = swap(rim, 2)
    rims = [rim, swap(rim, 1), rim_far, swap(rim_far, 1)]

    def edge_row(owner, row):
        k = j ^ owner
        parts = [
            jnp.concatenate([r[0, row][None], p[row], r[1, row][None]], axis=0)
            for p, r in zip(pieces, rims)
        ]
        return jnp.where(
            k < 2, jnp.where(k == 0, parts[0], parts[1]), jnp.where(k == 2, parts[2], parts[3])
        )

    edges = [
        along_y(edge_row(QUAD - 1, rows - 1), 1, False),
        along_y(edge_row(0, 0), -1, False),
    ]

    def quarter(k):
        return lax.dynamic_slice_in_dim(pre_act, (j ^ k) * q, q, axis=3)

    pres = [quarter(0)] + [swap(quarter(k), k) for k in (1, 2, 3)]

    taps = weight.reshape(9, 3, owned, chan)

    def weight_quarter(k):
        part = lax.dynamic_slice_in_dim(taps, (j ^ k) * q, q, axis=3)
        return part.transpose(0, 2, 1, 3).reshape(9, owned, 3 * q)

    near = jnp.stack([weight_quarter(0)] + [swap_far(weight_quarter(k), k) for k in (1, 2, 3)])
    above = along_y(near, -1, True)
    below = along_y(near, 1, True)
    across = jnp.concatenate([along_y(below[:2], 1, True), along_y(above[2:], -1, True)])
    parts = [near, above, across, below]

    act = pl.pallas_call(
        act_kernel,
        out_shape=jax.ShapeDtypeStruct((3 * q, QUAD * rows * width * depth), BF16),
        in_specs=[VMEM] * QUAD,
        out_specs=VMEM,
        compiler_params=params(),
    )(*pres)

    mid = reduce_x(*weight_terms(0, 1, norm, pieces, rims, [], act))
    rest = reduce_x(*weight_terms(-1, 2, norm, pieces, rims, edges, act))
    total = jnp.concatenate([rest[:9], mid, rest[9:]])
    grad_weight = reduce_rest(total, owned)

    outs = input_terms(pieces, rims, edges, parts, pres)
    outs = [outs[0]] + [swap(outs[k], k) for k in (1, 2, 3)]
    grad_pre = join(outs, 3, lambda k: quad_place() ^ k)
    return (grad_pre, grad_weight)


def solution(mesh):
    return jax.shard_map(
        body,
        mesh=mesh,
        in_specs=(P("gy", "gx", None, None), P("gy", "gx", None, None), P(None, "gy", None)),
        out_specs=(P("gy", "gx", None, None), P(None, "gy", None)),
        check_vma=False,
    )
```

```python
import functools
import math

import jax
import jax.numpy as jnp
from jax import lax
from jax.experimental import pallas as pl
from jax.experimental.pallas import tpu as pltpu
from jax.sharding import PartitionSpec as P

QUAD = 4
RING = 4
F32 = jnp.float32
BF16 = jnp.bfloat16
ANY = pl.BlockSpec(memory_space=pl.ANY)
VMEM = pl.BlockSpec(memory_space=pltpu.VMEM)
LIMIT = 40 * 1024 * 1024


def params():
    return pltpu.CompilerParams(vmem_limit_bytes=LIMIT)


def quad_place():
    return lax.rem(lax.axis_index("gy"), QUAD)


def x_place():
    return lax.div(lax.axis_index("gx"), 2)


def swap(block, k):
    count = lax.axis_size("gy")
    return lax.ppermute(block, "gy", [(g, g ^ k) for g in range(count)])


def along_y(block, step, ring):
    count = lax.axis_size("gy")
    pairs = [(g, g + QUAD * step) for g in range(count)]
    if ring:
        pairs = [(s, t % count) for s, t in pairs]
    return lax.ppermute(block, "gy", [(s, t) for s, t in pairs if 0 <= t < count])


def along_x(block, step):
    count = lax.axis_size("gx")
    return lax.ppermute(block, "gx", [(g, (g + 2 * step) % count) for g in range(count)])


def rims_x(first, last):
    count = lax.axis_size("gx")
    low = lax.ppermute(last, "gx", [(g, g + 1) for g in range(count - 1)])
    high = lax.ppermute(first, "gx", [(g + 1, g) for g in range(count - 1)])
    return low, high


def zero_at(value, z, edge):
    return jnp.where(z == edge, 0.0, value)


def pick_kernel(cot, extra, low, high, *quarters):
    rows, width, depth, chan = cot.shape
    j = quad_place()
    q = chan // QUAD
    part = q // RING
    source = lax.broadcasted_iota(jnp.int32, (chan, q), 0)
    place = lax.broadcasted_iota(jnp.int32, (chan, q), 1)
    base = lax.div(place, part) * q + lax.rem(place, part)

    def take(block, pick):
        shape = block.shape
        flat = block[...].reshape(-1, chan)
        got = jnp.dot(flat, pick, preferred_element_type=F32)
        return got.astype(BF16).reshape(shape[:-1] + (q,))

    for k, out in enumerate(quarters):
        pick = jnp.where(source == base + (j ^ k) * part, 1.0, 0.0).astype(BF16)
        out[0:rows, 1:width + 1] = take(cot, pick)
        out[rows, 1:width + 1] = take(extra, pick)
        out[:, 0] = take(low, pick)
        out[:, width + 1] = take(high, pick)


def pick_channels(cot, extra, low, high):
    rows, width, depth, chan = cot.shape
    quarter = jax.ShapeDtypeStruct((rows + 1, width + 2, depth, chan // QUAD), BF16)
    return pl.pallas_call(
        pick_kernel,
        out_shape=[quarter] * QUAD,
        in_specs=[VMEM] * 4,
        out_specs=[VMEM] * QUAD,
        compiler_params=params(),
    )(cot, extra, low, high)


def turn_kernel(p0, p1, p2, p3, held, out):
    j, x = quad_place(), x_place()
    for k, p in enumerate((p0, p1, p2, p3)):
        rows = p.shape[0] - 1
        held[pl.ds(1 + (j ^ k) * rows, rows)] = p[0:rows]

        @pl.when((j ^ k) == 0)
        def _():
            held[0] = p[rows]

        @pl.when((j ^ k) == QUAD - 1)
        def _():
            held[held.shape[0] - 1] = p[rows]

    tall, width, depth, q = held.shape
    width -= 2
    cells = tall * width * depth
    part = q // RING
    small = part // RING
    place = lax.broadcasted_iota(jnp.int32, (q, q), 0)
    source = lax.broadcasted_iota(jnp.int32, (q, q), 1)
    xpart = lax.rem(lax.div(place, part) + x, RING)
    base = lax.div(lax.rem(place, part), small) * part + xpart * small + lax.rem(place, small)
    order = jnp.where(source == base, 1.0, 0.0).astype(BF16)
    z = lax.rem(lax.broadcasted_iota(jnp.int32, (q, cells), 1), depth)
    for b in (-1, 0, 1):
        moved = held[:, 1 - b:1 - b + width].reshape(cells, q)
        value = lax.dot_general(
            order, moved, (((1,), (1,)), ((), ())), preferred_element_type=F32
        )
        high = zero_at(pltpu.roll(value, cells - 1, 1), z, depth - 1)
        low = zero_at(pltpu.roll(value, 1, 1), z, 0)
        for c, v in enumerate((high, value, low)):
            at = ((b + 1) * 3 + c) * q
            out[at:at + q] = v.astype(BF16)


def turn(quarters):
    rows, width, depth, q = quarters[0].shape
    tall = QUAD * (rows - 1) + 2
    return pl.pallas_call(
        turn_kernel,
        out_shape=[
            jax.ShapeDtypeStruct((tall, width, depth, q), BF16),
            jax.ShapeDtypeStruct((9 * q, tall * (width - 2) * depth), BF16),
        ],
        in_specs=[VMEM] * QUAD,
        out_specs=[VMEM] * 2,
        compiler_params=params(),
    )(*quarters)


def run_copies(pairs, sem):
    copies = [pltpu.make_async_copy(s, d, sem.at[n]) for n, (s, d) in enumerate(pairs)]
    for c in copies:
        c.start()
    return copies


def weight_kernel(offsets, norm, own_act, near, far, across, cot, *refs):
    right, left, keep_right, keep_left, own, held, sem = refs
    j = quad_place()
    rows, width, depth, chan = own_act.shape
    pairs = []
    for k, piece in enumerate((own_act, near, far, across)):
        pairs.append((piece, held.at[pl.ds((j ^ k) * rows, rows)]))
    for c in run_copies(pairs, sem):
        c.wait()
    row = width * depth
    cells = QUAD * rows * row
    act = held[...].reshape(cells, chan)
    q = cot.shape[0] // 9
    part = q // RING
    half = part // 2
    for n in range(3 * len(offsets)):
        a, b = offsets[n // 3], n % 3
        moved = cot[3 * b * q:3 * (b + 1) * q, (1 - a) * row:(1 - a) * row + cells]
        term = jnp.dot(moved, act, preferred_element_type=F32) * norm
        for c in range(3):
            tap = 3 * n + c

            def block(r, h):
                at = c * q + r * part + h * half
                return term[at:at + half]

            right[0, tap] = block(2, 0).astype(BF16)
            left[0, tap] = block(2, 1).astype(BF16)
            keep_right[tap] = block(1, 0)
            right[1, tap] = block(1, 1).astype(BF16)
            left[1, tap] = block(3, 0).astype(BF16)
            keep_left[tap] = block(3, 1)
            own[0, tap] = block(0, 0)
            own[1, tap] = block(0, 1)


def weight_terms(offsets, norm, acts, cot):
    rows, width, depth, chan = acts[0].shape
    taps = 9 * len(offsets)
    q = chan // QUAD
    half = q // RING // 2
    held_cells = QUAD * rows * width * depth
    shapes = [
        jax.ShapeDtypeStruct((2, taps, half, chan), BF16),
        jax.ShapeDtypeStruct((2, taps, half, chan), BF16),
        jax.ShapeDtypeStruct((taps, half, chan), F32),
        jax.ShapeDtypeStruct((taps, half, chan), F32),
        jax.ShapeDtypeStruct((2, taps, half, chan), F32),
    ]
    return pl.pallas_call(
        functools.partial(weight_kernel, offsets, norm),
        out_shape=shapes,
        in_specs=[ANY] * 4 + [VMEM],
        out_specs=[VMEM] * 5,
        scratch_shapes=[
            pltpu.VMEM((QUAD * rows, width, depth, chan), BF16),
            pltpu.SemaphoreType.DMA((4,)),
        ],
        compiler_params=params(),
        cost_estimate=pl.CostEstimate(
            flops=2 * taps * q * held_cells * chan, bytes_accessed=10_000_000, transcendentals=0
        ),
    )(*acts, cot)


def input_kernel(held, own, above, across_low, across_high, below, *refs):
    send, keep, pass_on, weights, sem = refs
    j = quad_place()
    y = lax.div(lax.axis_index("gy"), QUAD)
    part = own.shape[1]
    low = across_low.shape[0]

    def at(s):
        return pl.ds(pl.multiple_of(lax.rem(y + s, RING) * part, part), part)

    pairs = [
        (own, weights.at[:, at(0)]),
        (above, weights.at[:, at(1)]),
        (across_low, weights.at[pl.ds(0, low), at(2)]),
        (across_high, weights.at[pl.ds(low, 27 - low), at(2)]),
        (below, weights.at[:, at(3)]),
    ]
    for c in run_copies(pairs, sem):
        c.wait()
    rows, width, depth, chan = keep.shape
    cells = rows * width * depth
    q = held.shape[3]
    taps = weights[...].reshape(9, 3, q, chan)
    for k, out in ((1, send.at[0]), (3, send.at[1]), (2, pass_on), (0, keep)):
        first = (j ^ k) * rows
        moved = []
        for n in range(9):
            a, b = n // 3 - 1, n % 3 - 1
            block = held[pl.ds(first + 1 - a, rows), 1 - b:1 - b + width]
            moved.append(block.reshape(cells, q))
        moved = jnp.concatenate(moved, axis=1)
        z = lax.rem(lax.broadcasted_iota(jnp.int32, (cells, chan), 0), depth)

        def term(c):
            return jnp.dot(moved, taps[:, c].reshape(9 * q, chan), preferred_element_type=F32)

        grad = term(1)
        grad = grad + zero_at(pltpu.roll(term(0), cells - 1, 0), z, depth - 1)
        grad = grad + zero_at(pltpu.roll(term(2), 1, 0), z, 0)
        out[...] = grad.reshape(rows, width, depth, chan)


def input_terms(held, parts):
    tall, width, depth, q = held.shape
    chan = QUAD * q
    block = ((tall - 2) // QUAD, width - 2, depth, chan)
    return pl.pallas_call(
        input_kernel,
        out_shape=[
            jax.ShapeDtypeStruct((2,) + block, F32),
            jax.ShapeDtypeStruct(block, F32),
            jax.ShapeDtypeStruct(block, F32),
        ],
        in_specs=[VMEM] + [ANY] * 5,
        out_specs=[VMEM] * 3,
        scratch_shapes=[pltpu.VMEM((27, q, chan), BF16), pltpu.SemaphoreType.DMA((5,))],
        compiler_params=params(),
        cost_estimate=pl.CostEstimate(
            flops=2 * 27 * tall * width * depth * q * chan, bytes_accessed=10_000_000, transcendentals=0
        ),
    )(held, *parts)


def finish_kernel(pre, keep, near, far, out):
    value = pre[...].astype(F32)
    s = jax.nn.sigmoid(value)
    grad = keep[...] + near[0] + far[...]
    out[...] = (grad * s * (1.0 + value * (1.0 - s))).astype(BF16)


def finish(pre_act, keep, near, far):
    return pl.pallas_call(
        finish_kernel,
        out_shape=jax.ShapeDtypeStruct(pre_act.shape, BF16),
        in_specs=[VMEM] * 4,
        out_specs=VMEM,
        compiler_params=params(),
    )(pre_act, keep, near, far)


def join_kernel(*refs):
    out = refs[-1]
    x = x_place()
    size = refs[0].shape[1]

    def put(first, piece, k):
        at = pl.ds(pl.multiple_of(lax.rem(x + k, RING) * size, size), size)
        out[first:first + piece.shape[0], at] = piece[...]

    first = 0
    for chunk in (refs[:5], refs[5:10]):
        own, below, above, low, high = chunk
        put(first, own, 0)
        put(first, below, 3)
        put(first, above, 1)
        put(first, low, 2)
        put(first + low.shape[0], high, 2)
        first += own.shape[0]


def join(first, second):
    _, size, chan = first[0].shape
    return pl.pallas_call(
        join_kernel,
        out_shape=jax.ShapeDtypeStruct((27, RING * size, chan), F32),
        in_specs=[VMEM] * 10,
        out_specs=VMEM,
        compiler_params=params(),
    )(*first, *second)


def reduce_x_first(right, left, *kept):
    return along_x(right, 1), along_x(left, -1), *kept


def reduce_x_last(from_left, from_right, keep_right, keep_left, own):
    next_right = (from_left[0].astype(F32) + keep_right).astype(BF16)
    next_left = (from_right[0].astype(F32) + keep_left).astype(BF16)
    last_left = along_x(next_right, 1)
    last_right = along_x(next_left, -1)
    low = own[0] + from_right[1].astype(F32) + last_left.astype(F32)
    high = own[1] + from_left[1].astype(F32) + last_right.astype(F32)
    return jnp.concatenate([low, high], axis=1)


def reduce_rest(total, beside=()):
    y = lax.div(lax.axis_index("gy"), QUAD)
    size = total.shape[1] // RING

    def block(r):
        return lax.dynamic_slice_in_dim(total, lax.rem(y + r, RING) * size, size, axis=1)

    others = [along_y(block(r).astype(BF16), r, True) for r in (1, 2, 3)]
    others, beside = lax.optimization_barrier((others, beside))
    mine = block(0)
    for other in others:
        mine = mine + other.astype(F32)
    count = lax.axis_size("gx")
    other = lax.ppermute(mine.astype(BF16), "gx", [(g, g ^ 1) for g in range(count)])
    whole = mine + other.astype(F32)
    below, above = along_x(whole, 1), along_x(whole, -1)
    taps = whole.shape[0] // 2
    return [whole, below, above, along_x(below[:taps], 1), along_x(above[taps:], -1)], beside


def body(pre_act, cot, weight):
    rows, width, depth, chan = pre_act.shape
    norm = 1.0 / math.sqrt(rows * lax.axis_size("gy") * width * lax.axis_size("gx") * depth)
    j = quad_place()

    count = lax.axis_size("gy")
    pairs = [(g, g + 1) for g in range(QUAD - 1, count - 1, QUAD)]
    pairs = pairs + [(t, s) for s, t in pairs]
    extra = lax.ppermute(jnp.where(j == 0, cot[0], cot[rows - 1]), "gy", pairs)
    act = jax.nn.silu(pre_act.astype(F32)).astype(BF16)
    far = swap(act, 2)
    near = swap(act, 1)
    above = along_y(weight, -1, True)
    below = along_y(weight, 1, True)
    sides = [jnp.concatenate([cot[:, x], extra[x][None]]) for x in (0, width - 1)]
    low, high = rims_x(*sides)
    quarters = pick_channels(cot, extra, low, high)
    quarters, near, far = lax.optimization_barrier((quarters, near, far))
    quarters = [quarters[0]] + [swap(quarters[k], k) for k in (1, 2, 3)]
    acts = [act, near, far, swap(far, 1)]
    held, turned = turn(quarters)

    turned, above, below = lax.optimization_barrier((turned, above, below))
    taps = 13
    parts = [weight, above, along_y(below[:taps], 1, True), along_y(above[taps:], -1, True), below]
    first = weight_terms((-1,), norm, acts, turned)
    turned, first = lax.optimization_barrier((turned, first))
    first = reduce_x_first(*first)
    second = weight_terms((0, 1), norm, acts, turned)
    held, first, second = lax.optimization_barrier((held, first, second))
    second = reduce_x_first(*second)
    grads = input_terms(held, parts)
    second, grads = lax.optimization_barrier((second, grads))
    send, keep, pass_on = grads
    got = swap(send, 1)
    far_grad = swap(pass_on + got[1], 2)
    first, _ = reduce_rest(reduce_x_last(*first))
    second, far_grad = reduce_rest(reduce_x_last(*second), far_grad)
    grad_weight = join(first, second)
    grad_pre = finish(pre_act, keep, got, far_grad)
    return (grad_pre, grad_weight)


def solution(mesh):
    return jax.shard_map(
        body,
        mesh=mesh,
        in_specs=(P("gy", "gx", None, None), P("gy", "gx", None, None), P(None, "gy", None)),
        out_specs=(P("gy", "gx", None, None), P(None, "gy", None)),
        check_vma=False,
    )
```

```python
import functools
import math

import jax
import jax.numpy as jnp
from jax import lax
from jax.experimental import pallas as pl
from jax.experimental.pallas import tpu as pltpu
from jax.sharding import PartitionSpec as P

QUAD = 4
RING = 4
F32 = jnp.float32
BF16 = jnp.bfloat16
ANY = pl.BlockSpec(memory_space=pl.ANY)
VMEM = pl.BlockSpec(memory_space=pltpu.VMEM)
LIMIT = 60 * 1024 * 1024


def params():
    return pltpu.CompilerParams(vmem_limit_bytes=LIMIT)


def quad_place():
    return lax.rem(lax.axis_index("gy"), QUAD)


def x_place():
    return lax.div(lax.axis_index("gx"), 2)


def swap(block, k):
    count = lax.axis_size("gy")
    return lax.ppermute(block, "gy", [(g, g ^ k) for g in range(count)])


def along_y(block, step, ring):
    count = lax.axis_size("gy")
    pairs = [(g, g + QUAD * step) for g in range(count)]
    if ring:
        pairs = [(s, t % count) for s, t in pairs]
    return lax.ppermute(block, "gy", [(s, t) for s, t in pairs if 0 <= t < count])


def along_x(block, step):
    count = lax.axis_size("gx")
    return lax.ppermute(block, "gx", [(g, (g + 2 * step) % count) for g in range(count)])


def rims_x(first, last, pairs=None):
    nx, ny = lax.axis_size("gx"), lax.axis_size("gy")
    pairs = pairs or [(h, h) for h in range(ny)]
    up = [(g * ny + s, (g + 1) * ny + t) for g in range(nx - 1) for s, t in pairs]
    down = [((g + 1) * ny + s, g * ny + t) for g in range(nx - 1) for s, t in pairs]
    return lax.ppermute(last, ("gx", "gy"), up), lax.ppermute(first, ("gx", "gy"), down)


def zero_at(value, z, edge):
    return jnp.where(z == edge, 0.0, value)


def pick_kernel(cot, extra, low, high, extra_low, extra_high, *quarters):
    rows, width, depth, chan = cot.shape
    j = quad_place()
    q = chan // QUAD
    part = q // RING
    source = lax.broadcasted_iota(jnp.int32, (chan, q), 0)
    place = lax.broadcasted_iota(jnp.int32, (chan, q), 1)
    base = lax.div(place, part) * q + lax.rem(place, part)

    def take(block, pick):
        shape = block.shape
        flat = block[...].reshape(-1, chan)
        got = jnp.dot(flat, pick, preferred_element_type=F32)
        return got.astype(BF16).reshape(shape[:-1] + (q,))

    for k, out in enumerate(quarters):
        pick = jnp.where(source == base + (j ^ k) * part, 1.0, 0.0).astype(BF16)
        out[0:rows, 1:width + 1] = take(cot, pick)
        out[rows, 1:width + 1] = take(extra, pick)
        out[0:rows, 0] = take(low, pick)
        out[0:rows, width + 1] = take(high, pick)
        out[rows, 0] = take(extra_low, pick)
        out[rows, width + 1] = take(extra_high, pick)


def pick_channels(cot, *rims):
    rows, width, depth, chan = cot.shape
    quarter = jax.ShapeDtypeStruct((rows + 1, width + 2, depth, chan // QUAD), BF16)
    return pl.pallas_call(
        pick_kernel,
        out_shape=[quarter] * QUAD,
        in_specs=[VMEM] * 6,
        out_specs=[VMEM] * QUAD,
        compiler_params=params(),
    )(cot, *rims)


def turn_kernel(p0, p1, p2, p3, held, out):
    j, x = quad_place(), x_place()
    for k, p in enumerate((p0, p1, p2, p3)):
        rows = p.shape[0] - 1
        held[pl.ds(1 + (j ^ k) * rows, rows)] = p[0:rows]

        @pl.when((j ^ k) == 0)
        def _():
            held[0] = p[rows]

        @pl.when((j ^ k) == QUAD - 1)
        def _():
            held[held.shape[0] - 1] = p[rows]

    tall, width, depth, q = held.shape
    width -= 2
    cells = tall * width * depth
    part = q // RING
    small = part // RING
    place = lax.broadcasted_iota(jnp.int32, (q, q), 0)
    source = lax.broadcasted_iota(jnp.int32, (q, q), 1)
    xpart = lax.rem(lax.div(place, part) + x, RING)
    base = lax.div(lax.rem(place, part), small) * part + xpart * small + lax.rem(place, small)
    order = jnp.where(source == base, 1.0, 0.0).astype(BF16)
    z = lax.rem(lax.broadcasted_iota(jnp.int32, (q, cells), 1), depth)
    for b in (-1, 0, 1):
        moved = held[:, 1 - b:1 - b + width].reshape(cells, q)
        value = lax.dot_general(
            order, moved, (((1,), (1,)), ((), ())), preferred_element_type=F32
        )
        high = zero_at(pltpu.roll(value, cells - 1, 1), z, depth - 1)
        low = zero_at(pltpu.roll(value, 1, 1), z, 0)
        for c, v in enumerate((high, value, low)):
            at = ((b + 1) * 3 + c) * q
            out[at:at + q] = v.astype(BF16)


def turn(quarters):
    rows, width, depth, q = quarters[0].shape
    tall = QUAD * (rows - 1) + 2
    return pl.pallas_call(
        turn_kernel,
        out_shape=[
            jax.ShapeDtypeStruct((tall, width, depth, q), BF16),
            jax.ShapeDtypeStruct((9 * q, tall * (width - 2) * depth), BF16),
        ],
        in_specs=[VMEM] * QUAD,
        out_specs=[VMEM] * 2,
        compiler_params=params(),
    )(*quarters)


def run_copies(pairs, sem):
    copies = [pltpu.make_async_copy(s, d, sem.at[n]) for n, (s, d) in enumerate(pairs)]
    for c in copies:
        c.start()
    return copies


def weight_kernel(low, norm, own_act, near, far, across, cot, *refs):
    right, left, keep_right, keep_left, own, held, sem = refs
    j = quad_place()
    rows, width, depth, chan = own_act.shape

    @pl.when((pl.program_id(0) == 0) & (pl.program_id(1) == 0))
    def _():
        pairs = []
        for k, piece in enumerate((own_act, near, far, across)):
            pairs.append((piece, held.at[pl.ds((j ^ k) * rows, rows)]))
        for c in run_copies(pairs, sem):
            c.wait()

    row = width * depth
    cells = QUAD * rows * row
    q = cot.shape[0] // 3
    part = q // RING
    half = part // 2
    a = low + pl.program_id(1)
    moved = cot[:, pl.ds(pl.multiple_of((1 - a) * row, row), cells)]
    act = held[...].reshape(cells, chan)
    term = jnp.dot(moved, act, preferred_element_type=F32) * norm
    for c in range(3):

        def block(r, h):
            at = c * q + r * part + h * half
            return term[at:at + half]

        right[0, c] = block(2, 0).astype(BF16)
        left[0, c] = block(2, 1).astype(BF16)
        keep_right[c] = block(1, 0)
        right[1, c] = block(1, 1).astype(BF16)
        left[1, c] = block(3, 0).astype(BF16)
        keep_left[c] = block(3, 1)
        own[0, c] = block(0, 0)
        own[1, c] = block(0, 1)


def weight_terms(low, count, norm, acts, cot):
    rows, width, depth, chan = acts[0].shape
    taps = 9 * count
    q = chan // QUAD
    half = q // RING // 2
    cells = QUAD * rows * width * depth

    def pair(dtype):
        spec = pl.BlockSpec((2, 3, half, chan), lambda b, a: (0, 3 * a + b, 0, 0))
        return jax.ShapeDtypeStruct((2, taps, half, chan), dtype), spec

    def single(dtype):
        spec = pl.BlockSpec((3, half, chan), lambda b, a: (3 * a + b, 0, 0))
        return jax.ShapeDtypeStruct((taps, half, chan), dtype), spec

    outs = [pair(BF16), pair(BF16), single(F32), single(F32), pair(F32)]
    return pl.pallas_call(
        functools.partial(weight_kernel, low, norm),
        grid=(3, count),
        out_shape=[shape for shape, _ in outs],
        in_specs=[ANY] * 4 + [pl.BlockSpec((3 * q, cot.shape[1]), lambda b, a: (b, 0))],
        out_specs=[spec for _, spec in outs],
        scratch_shapes=[
            pltpu.VMEM((QUAD * rows, width, depth, chan), BF16),
            pltpu.SemaphoreType.DMA((4,)),
        ],
        compiler_params=params(),
        cost_estimate=pl.CostEstimate(
            flops=2 * taps * q * cells * chan, bytes_accessed=10_000_000, transcendentals=0
        ),
    )(*acts, cot)


def input_kernel(held, own, above, across_low, across_high, below, send, keep, weights, sem):
    j = quad_place()
    y = lax.div(lax.axis_index("gy"), QUAD)
    part = own.shape[1]
    low = across_low.shape[0]

    @pl.when(pl.program_id(0) == 0)
    def _():
        def at(s):
            return pl.ds(pl.multiple_of(lax.rem(y + s, RING) * part, part), part)

        pairs = [
            (own, weights.at[:, at(0)]),
            (above, weights.at[:, at(1)]),
            (across_low, weights.at[pl.ds(0, low), at(2)]),
            (across_high, weights.at[pl.ds(low, 27 - low), at(2)]),
            (below, weights.at[:, at(3)]),
        ]
        for c in run_copies(pairs, sem):
            c.wait()

    _, rows, width, depth, chan = send.shape
    cells = rows * width * depth
    q = held.shape[3]
    taps = weights[...].reshape(9, 3, q, chan)
    n = pl.program_id(0)
    first = (j ^ jnp.where(n == 0, 1, jnp.where(n == 1, 3, jnp.where(n == 2, 2, 0)))) * rows
    moved = []
    for tap in range(9):
        a, b = tap // 3 - 1, tap % 3 - 1
        block = held[pl.ds(first + 1 - a, rows), 1 - b:1 - b + width]
        moved.append(block.reshape(cells, q))
    moved = jnp.concatenate(moved, axis=1)
    z = lax.rem(lax.broadcasted_iota(jnp.int32, (cells, chan), 0), depth)

    def term(c):
        return jnp.dot(moved, taps[:, c].reshape(9 * q, chan), preferred_element_type=F32)

    grad = term(1)
    grad = grad + zero_at(pltpu.roll(term(0), cells - 1, 0), z, depth - 1)
    grad = grad + zero_at(pltpu.roll(term(2), 1, 0), z, 0)

    @pl.when(n < 2)
    def _():
        send[0] = grad.reshape(rows, width, depth, chan)

    @pl.when(n >= 2)
    def _():
        keep[0] = grad.reshape(rows, width, depth, chan)


def input_terms(held, parts):
    tall, width, depth, q = held.shape
    chan = QUAD * q
    block = ((tall - 2) // QUAD, width - 2, depth, chan)
    return pl.pallas_call(
        input_kernel,
        grid=(4,),
        out_shape=[jax.ShapeDtypeStruct((2,) + block, F32)] * 2,
        in_specs=[pl.BlockSpec(held.shape, lambda n: (0, 0, 0, 0))] + [ANY] * 5,
        out_specs=[
            pl.BlockSpec((1,) + block, lambda n: (jnp.minimum(n, 1), 0, 0, 0, 0)),
            pl.BlockSpec((1,) + block, lambda n: (jnp.maximum(n - 2, 0), 0, 0, 0, 0)),
        ],
        scratch_shapes=[pltpu.VMEM((27, q, chan), BF16), pltpu.SemaphoreType.DMA((5,))],
        compiler_params=params(),
        cost_estimate=pl.CostEstimate(
            flops=2 * 27 * tall * width * depth * q * chan, bytes_accessed=10_000_000, transcendentals=0
        ),
    )(held, *parts)


def finish_kernel(pre, keep, near, far_low, far_high, out):
    rows = far_low.shape[0]
    for at, far in ((0, far_low), (rows, far_high)):
        value = pre[at:at + rows].astype(F32)
        s = jax.nn.sigmoid(value)
        grad = keep[1, at:at + rows] + near[0, at:at + rows] + far[...]
        out[at:at + rows] = (grad * s * (1.0 + value * (1.0 - s))).astype(BF16)


def finish(pre_act, keep, near, *far):
    return pl.pallas_call(
        finish_kernel,
        out_shape=jax.ShapeDtypeStruct(pre_act.shape, BF16),
        in_specs=[VMEM] * 5,
        out_specs=VMEM,
        compiler_params=params(),
    )(pre_act, keep, near, *far)


def join_kernel(*refs):
    out = refs[-1]
    x = x_place()
    size = refs[0].shape[1]

    def put(first, piece, k):
        at = pl.ds(pl.multiple_of(lax.rem(x + k, RING) * size, size), size)
        out[first:first + piece.shape[0], at] = piece[...]

    first = 0
    for chunk in (refs[:5], refs[5:10]):
        own, below, above, low, high = chunk
        put(first, own, 0)
        put(first, below, 3)
        put(first, above, 1)
        put(first, low, 2)
        put(first + low.shape[0], high, 2)
        first += own.shape[0]


def join(first, second):
    _, size, chan = first[0].shape
    return pl.pallas_call(
        join_kernel,
        out_shape=jax.ShapeDtypeStruct((27, RING * size, chan), F32),
        in_specs=[VMEM] * 10,
        out_specs=VMEM,
        compiler_params=params(),
    )(*first, *second)


def reduce_x_first(right, left, *kept):
    return along_x(right, 1), along_x(left, -1), *kept


def reduce_x_next(from_left, from_right, keep_right, keep_left, own):
    next_right = (from_left[0].astype(F32) + keep_right).astype(BF16)
    next_left = (from_right[0].astype(F32) + keep_left).astype(BF16)
    return next_right, next_left, from_left[1], from_right[1], own


def reduce_x_last(next_right, next_left, from_left, from_right, own):
    last_left = along_x(next_right, 1)
    last_right = along_x(next_left, -1)
    low = own[0] + from_right.astype(F32) + last_left.astype(F32)
    high = own[1] + from_left.astype(F32) + last_right.astype(F32)
    return jnp.concatenate([low, high], axis=1)


def reduce_y_first(total):
    y = lax.div(lax.axis_index("gy"), QUAD)
    size = total.shape[1] // RING

    def block(r):
        return lax.dynamic_slice_in_dim(total, lax.rem(y + r, RING) * size, size, axis=1)

    return block(0), [along_y(block(r).astype(BF16), r, True) for r in (1, 2, 3)]


def reduce_y_last(mine, others):
    for other in others:
        mine = mine + other.astype(F32)
    return mine


def reduce_z(mine):
    count = lax.axis_size("gx")
    other = lax.ppermute(mine.astype(BF16), "gx", [(g, g ^ 1) for g in range(count)])
    return mine + other.astype(F32)


def gather_x(whole):
    below, above = along_x(whole, 1), along_x(whole, -1)
    taps = whole.shape[0] // 2
    return [whole, below, above, along_x(below[:taps], 1), along_x(above[taps:], -1)]


def body(pre_act, cot, weight):
    rows, width, depth, chan = pre_act.shape
    norm = 1.0 / math.sqrt(rows * lax.axis_size("gy") * width * lax.axis_size("gx") * depth)
    j = quad_place()
    barrier = lax.optimization_barrier

    count = lax.axis_size("gy")
    pairs = [(g, g + 1) for g in range(QUAD - 1, count - 1, QUAD)]
    pairs = pairs + [(t, s) for s, t in pairs]
    edge = jnp.where(j == 0, cot[0], cot[rows - 1])
    extra = lax.ppermute(edge, "gy", pairs)
    rims = [extra, *rims_x(cot[:, 0], cot[:, width - 1]), *rims_x(edge[0], edge[-1], pairs)]
    act = jax.nn.silu(pre_act.astype(F32)).astype(BF16)
    rims, act, weight = barrier((rims, act, weight))

    far = swap(act, 2)
    near = swap(act, 1)
    above = along_y(weight, -1, True)
    below = along_y(weight, 1, True)
    quarters = pick_channels(cot, *rims)
    quarters = [quarters[0]] + [swap(quarters[k], k) for k in (1, 2, 3)]
    quarters, near, far = barrier((quarters, near, far))
    acts = [act, near, far, swap(far, 1)]
    held, turned = turn(quarters)

    turned, above, below = barrier((turned, above, below))
    first = weight_terms(-1, 1, norm, acts, turned)
    turned, first = barrier((turned, first))
    taps = 13
    parts = [weight, above, along_y(below[:taps], 1, True), along_y(above[taps:], -1, True), below]
    first = reduce_x_first(*first)
    second = weight_terms(0, 2, norm, acts, turned)
    held, first, second = barrier((held, first, second))
    second = reduce_x_first(*second)
    first = reduce_x_last(*reduce_x_next(*first))
    send, keep = input_terms(held, parts)
    send, keep, first, second = barrier((send, keep, first, second))
    got = swap(send, 1)
    second = reduce_x_next(*second)
    first, second = barrier((first, second))
    second = reduce_x_last(*second)
    first = reduce_y_last(*reduce_y_first(first))
    second, first, got = barrier((second, first, got))
    half = rows // 2
    far_low = swap(keep[0, :half] + got[1, :half], 2)
    second = reduce_y_last(*reduce_y_first(second))
    first = reduce_z(first)
    second, first, far_low = barrier((second, first, far_low))
    first = gather_x(first)
    second = reduce_z(second)
    second, keep, got = barrier((second, keep, got))
    far_high = swap(keep[0, half:] + got[1, half:], 2)
    second = gather_x(second)
    grad_weight = join(first, second)
    grad_pre = finish(pre_act, keep, got, far_low, far_high)
    return (grad_pre, grad_weight)


def solution(mesh):
    return jax.shard_map(
        body,
        mesh=mesh,
        in_specs=(P("gy", "gx", None, None), P("gy", "gx", None, None), P(None, "gy", None)),
        out_specs=(P("gy", "gx", None, None), P(None, "gy", None)),
        check_vma=False,
    )
```

```python
import functools
import math

import jax
import jax.numpy as jnp
from jax import lax
from jax.experimental import pallas as pl
from jax.experimental.pallas import tpu as pltpu
from jax.sharding import PartitionSpec as P

QUAD = 4
RING = 4
F32 = jnp.float32
BF16 = jnp.bfloat16
ANY = pl.BlockSpec(memory_space=pl.ANY)
VMEM = pl.BlockSpec(memory_space=pltpu.VMEM)
LIMIT = 24 * 1024 * 1024


def params():
    return pltpu.CompilerParams(vmem_limit_bytes=LIMIT)


def quad_place():
    return lax.rem(lax.axis_index("gy"), QUAD)


def x_place():
    return lax.div(lax.axis_index("gx"), 2)


def swap(block, k):
    count = lax.axis_size("gy")
    return lax.ppermute(block, "gy", [(g, g ^ k) for g in range(count)])


def along_y(block, step, ring):
    count = lax.axis_size("gy")
    pairs = [(g, g + QUAD * step) for g in range(count)]
    if ring:
        pairs = [(s, t % count) for s, t in pairs]
    return lax.ppermute(block, "gy", [(s, t) for s, t in pairs if 0 <= t < count])


def along_x(block, step):
    count = lax.axis_size("gx")
    return lax.ppermute(block, "gx", [(g, (g + 2 * step) % count) for g in range(count)])


def rims_x(first, last):
    count = lax.axis_size("gx")
    low = lax.ppermute(last, "gx", [(g, g + 1) for g in range(count - 1)])
    high = lax.ppermute(first, "gx", [(g + 1, g) for g in range(count - 1)])
    return low, high


def zero_at(value, z, edge):
    return jnp.where(z == edge, 0.0, value)


def pick_kernel(cot, extra, low, high, *quarters):
    rows, width, depth, chan = cot.shape
    j = quad_place()
    q = chan // QUAD
    part = q // RING
    source = lax.broadcasted_iota(jnp.int32, (chan, q), 0)
    place = lax.broadcasted_iota(jnp.int32, (chan, q), 1)
    base = lax.div(place, part) * q + lax.rem(place, part)

    def take(block, pick):
        shape = block.shape
        flat = block[...].reshape(-1, chan)
        got = jnp.dot(flat, pick, preferred_element_type=F32)
        return got.astype(BF16).reshape(shape[:-1] + (q,))

    for k, out in enumerate(quarters):
        pick = jnp.where(source == base + (j ^ k) * part, 1.0, 0.0).astype(BF16)
        out[0:rows, 1:width + 1] = take(cot, pick)
        out[rows, 1:width + 1] = take(extra, pick)
        out[:, 0] = take(low, pick)
        out[:, width + 1] = take(high, pick)


def pick_channels(cot, extra, low, high):
    rows, width, depth, chan = cot.shape
    quarter = jax.ShapeDtypeStruct((rows + 1, width + 2, depth, chan // QUAD), BF16)
    return pl.pallas_call(
        pick_kernel,
        out_shape=[quarter] * QUAD,
        in_specs=[VMEM] * 4,
        out_specs=[VMEM] * QUAD,
        compiler_params=params(),
    )(cot, extra, low, high)


def turn_kernel(p0, p1, p2, p3, held, out):
    j, x = quad_place(), x_place()
    for k, p in enumerate((p0, p1, p2, p3)):
        rows = p.shape[0] - 1
        held[pl.ds(1 + (j ^ k) * rows, rows)] = p[0:rows]

        @pl.when((j ^ k) == 0)
        def _():
            held[0] = p[rows]

        @pl.when((j ^ k) == QUAD - 1)
        def _():
            held[held.shape[0] - 1] = p[rows]

    tall, width, depth, q = held.shape
    width -= 2
    cells = tall * width * depth
    part = q // RING
    small = part // RING
    place = lax.broadcasted_iota(jnp.int32, (q, q), 0)
    source = lax.broadcasted_iota(jnp.int32, (q, q), 1)
    xpart = lax.rem(lax.div(place, part) + x, RING)
    base = lax.div(lax.rem(place, part), small) * part + xpart * small + lax.rem(place, small)
    order = jnp.where(source == base, 1.0, 0.0).astype(BF16)
    z = lax.rem(lax.broadcasted_iota(jnp.int32, (q, cells), 1), depth)
    for b in (-1, 0, 1):
        moved = held[:, 1 - b:1 - b + width].reshape(cells, q)
        value = lax.dot_general(
            order, moved, (((1,), (1,)), ((), ())), preferred_element_type=F32
        )
        high = zero_at(pltpu.roll(value, cells - 1, 1), z, depth - 1)
        low = zero_at(pltpu.roll(value, 1, 1), z, 0)
        for c, v in enumerate((high, value, low)):
            at = ((b + 1) * 3 + c) * q
            out[at:at + q] = v.astype(BF16)


def turn(quarters):
    rows, width, depth, q = quarters[0].shape
    tall = QUAD * (rows - 1) + 2
    return pl.pallas_call(
        turn_kernel,
        out_shape=[
            jax.ShapeDtypeStruct((tall, width, depth, q), BF16),
            jax.ShapeDtypeStruct((9 * q, tall * (width - 2) * depth), BF16),
        ],
        in_specs=[VMEM] * QUAD,
        out_specs=[VMEM] * 2,
        compiler_params=params(),
    )(*quarters)


def run_copies(pairs, sem):
    copies = [pltpu.make_async_copy(s, d, sem.at[n]) for n, (s, d) in enumerate(pairs)]
    for c in copies:
        c.start()
    return copies


def weight_kernel(offsets, norm, own_act, near, far, across, cot, *refs):
    right, left, keep_right, keep_left, own, held, sem = refs
    j = quad_place()
    rows, width, depth, chan = own_act.shape
    pairs = []
    for k, piece in enumerate((own_act, near, far, across)):
        pairs.append((piece, held.at[pl.ds((j ^ k) * rows, rows)]))
    for c in run_copies(pairs, sem):
        c.wait()
    row = width * depth
    cells = QUAD * rows * row
    act = held[...].reshape(cells, chan)
    q = cot.shape[0] // 9
    part = q // RING
    half = part // 2
    for n in range(3 * len(offsets)):
        a, b = offsets[n // 3], n % 3
        moved = cot[3 * b * q:3 * (b + 1) * q, (1 - a) * row:(1 - a) * row + cells]
        term = jnp.dot(moved, act, preferred_element_type=F32) * norm
        for c in range(3):
            tap = 3 * n + c

            def block(r, h):
                at = c * q + r * part + h * half
                return term[at:at + half]

            right[0, tap] = block(2, 0).astype(BF16)
            left[0, tap] = block(2, 1).astype(BF16)
            keep_right[tap] = block(1, 0)
            right[1, tap] = block(1, 1).astype(BF16)
            left[1, tap] = block(3, 0).astype(BF16)
            keep_left[tap] = block(3, 1)
            own[0, tap] = block(0, 0)
            own[1, tap] = block(0, 1)


def weight_terms(offsets, norm, acts, cot):
    rows, width, depth, chan = acts[0].shape
    taps = 9 * len(offsets)
    q = chan // QUAD
    half = q // RING // 2
    held_cells = QUAD * rows * width * depth
    shapes = [
        jax.ShapeDtypeStruct((2, taps, half, chan), BF16),
        jax.ShapeDtypeStruct((2, taps, half, chan), BF16),
        jax.ShapeDtypeStruct((taps, half, chan), F32),
        jax.ShapeDtypeStruct((taps, half, chan), F32),
        jax.ShapeDtypeStruct((2, taps, half, chan), F32),
    ]
    return pl.pallas_call(
        functools.partial(weight_kernel, offsets, norm),
        out_shape=shapes,
        in_specs=[ANY] * 4 + [VMEM],
        out_specs=[VMEM] * 5,
        scratch_shapes=[
            pltpu.VMEM((QUAD * rows, width, depth, chan), BF16),
            pltpu.SemaphoreType.DMA((4,)),
        ],
        compiler_params=params(),
        cost_estimate=pl.CostEstimate(
            flops=2 * taps * q * held_cells * chan, bytes_accessed=10_000_000, transcendentals=0
        ),
    )(*acts, cot)


def input_kernel(held, own, above, across_low, across_high, below, *refs):
    send, keep, pass_on, weights, sem = refs
    j = quad_place()
    y = lax.div(lax.axis_index("gy"), QUAD)
    part = own.shape[1]
    low = across_low.shape[0]

    def at(s):
        return pl.ds(pl.multiple_of(lax.rem(y + s, RING) * part, part), part)

    pairs = [
        (own, weights.at[:, at(0)]),
        (above, weights.at[:, at(1)]),
        (across_low, weights.at[pl.ds(0, low), at(2)]),
        (across_high, weights.at[pl.ds(low, 27 - low), at(2)]),
        (below, weights.at[:, at(3)]),
    ]
    for c in run_copies(pairs, sem):
        c.wait()
    rows, width, depth, chan = keep.shape
    cells = rows * width * depth
    q = held.shape[3]
    taps = weights[...].reshape(9, 3, q, chan)
    for k, out in ((1, send.at[0]), (3, send.at[1]), (2, pass_on), (0, keep)):
        first = (j ^ k) * rows
        moved = []
        for n in range(9):
            a, b = n // 3 - 1, n % 3 - 1
            block = held[pl.ds(first + 1 - a, rows), 1 - b:1 - b + width]
            moved.append(block.reshape(cells, q))
        moved = jnp.concatenate(moved, axis=1)
        z = lax.rem(lax.broadcasted_iota(jnp.int32, (cells, chan), 0), depth)

        def term(c):
            return jnp.dot(moved, taps[:, c].reshape(9 * q, chan), preferred_element_type=F32)

        grad = term(1)
        grad = grad + zero_at(pltpu.roll(term(0), cells - 1, 0), z, depth - 1)
        grad = grad + zero_at(pltpu.roll(term(2), 1, 0), z, 0)
        out[...] = grad.reshape(rows, width, depth, chan)


def input_terms(held, parts):
    tall, width, depth, q = held.shape
    chan = QUAD * q
    block = ((tall - 2) // QUAD, width - 2, depth, chan)
    return pl.pallas_call(
        input_kernel,
        out_shape=[
            jax.ShapeDtypeStruct((2,) + block, F32),
            jax.ShapeDtypeStruct(block, F32),
            jax.ShapeDtypeStruct(block, F32),
        ],
        in_specs=[VMEM] + [ANY] * 5,
        out_specs=[VMEM] * 3,
        scratch_shapes=[pltpu.VMEM((27, q, chan), BF16), pltpu.SemaphoreType.DMA((5,))],
        compiler_params=params(),
        cost_estimate=pl.CostEstimate(
            flops=2 * 27 * tall * width * depth * q * chan, bytes_accessed=10_000_000, transcendentals=0
        ),
    )(held, *parts)


def finish_kernel(pre, keep, near, far, out):
    value = pre[...].astype(F32)
    s = jax.nn.sigmoid(value)
    grad = keep[...] + near[0] + far[...]
    out[...] = (grad * s * (1.0 + value * (1.0 - s))).astype(BF16)


def finish(pre_act, keep, near, far):
    return pl.pallas_call(
        finish_kernel,
        out_shape=jax.ShapeDtypeStruct(pre_act.shape, BF16),
        in_specs=[VMEM] * 4,
        out_specs=VMEM,
        compiler_params=params(),
    )(pre_act, keep, near, far)


def split_kernel(*refs):
    parts, outs, total = refs[:10], refs[10:14], refs[14]
    y = lax.div(lax.axis_index("gy"), QUAD)
    taps = 0
    for own, from_left, from_right, last_left, last_right in (parts[:5], parts[5:]):
        count, rows = own.shape[1:3]
        low = own[0] + from_right[1].astype(F32) + last_left[...].astype(F32)
        high = own[1] + from_left[1].astype(F32) + last_right[...].astype(F32)
        at = slice(taps, taps + count)
        for half, value in enumerate((low, high)):
            for sub in range(2):
                total[2 * half + sub, at] = value[:, sub * (rows // 2):(sub + 1) * (rows // 2)]
        taps += count
    for r, out in enumerate(outs):
        out[...] = total[lax.rem(y + r, RING)].astype(out.dtype)


def split(first, second):
    _, count, rows, chan = first[0].shape
    shape = (3 * count, rows // 2, chan)
    return pl.pallas_call(
        split_kernel,
        out_shape=[jax.ShapeDtypeStruct(shape, F32)] + [jax.ShapeDtypeStruct(shape, BF16)] * 3,
        in_specs=[VMEM] * 10,
        out_specs=[VMEM] * 4,
        scratch_shapes=[pltpu.VMEM((RING,) + shape, F32)],
        compiler_params=params(),
    )(*first, *second)


def join_kernel(own, below, above, low, high, out):
    x = x_place()
    size = own.shape[1]

    def put(first, piece, k):
        at = pl.ds(pl.multiple_of(lax.rem(x + k, RING) * size, size), size)
        out[first:first + piece.shape[0], at] = piece[...]

    put(0, own, 0)
    put(0, below, 3)
    put(0, above, 1)
    put(0, low, 2)
    put(low.shape[0], high, 2)


def join(pieces):
    taps, size, chan = pieces[0].shape
    return pl.pallas_call(
        join_kernel,
        out_shape=jax.ShapeDtypeStruct((taps, RING * size, chan), F32),
        in_specs=[VMEM] * 5,
        out_specs=VMEM,
        compiler_params=params(),
    )(*pieces)


def reduce_x_first(right, left, *kept):
    return along_x(right, 1), along_x(left, -1), *kept


def reduce_x_last(from_left, from_right, keep_right, keep_left, own):
    next_right = (from_left[0].astype(F32) + keep_right).astype(BF16)
    next_left = (from_right[0].astype(F32) + keep_left).astype(BF16)
    return own, from_left, from_right, along_x(next_right, 1), along_x(next_left, -1)


def gather_x(whole):
    below, above = along_x(whole, 1), along_x(whole, -1)
    taps = whole.shape[0] // 2
    return [whole, below, above, along_x(below[:taps], 1), along_x(above[taps:], -1)]


def body(pre_act, cot, weight):
    rows, width, depth, chan = pre_act.shape
    norm = 1.0 / math.sqrt(rows * lax.axis_size("gy") * width * lax.axis_size("gx") * depth)
    j = quad_place()
    barrier = lax.optimization_barrier

    count = lax.axis_size("gy")
    pairs = [(g, g + 1) for g in range(QUAD - 1, count - 1, QUAD)]
    pairs = pairs + [(t, s) for s, t in pairs]
    extra = lax.ppermute(jnp.where(j == 0, cot[0], cot[rows - 1]), "gy", pairs)
    extra, weight = barrier((extra, weight))
    act = jax.nn.silu(pre_act.astype(F32)).astype(BF16)
    far = swap(act, 2)
    near = swap(act, 1)
    above = along_y(weight, -1, True)
    below = along_y(weight, 1, True)
    sides = [jnp.concatenate([cot[:, x], extra[x][None]]) for x in (0, width - 1)]
    sides = barrier(sides)
    low, high = rims_x(*sides)
    quarters = pick_channels(cot, extra, low, high)
    quarters, near, far = barrier((quarters, near, far))
    quarters = [quarters[0]] + [swap(quarters[k], k) for k in (1, 2, 3)]
    acts = [act, near, far, swap(far, 1)]
    held, turned = turn(quarters)

    turned, above, below = barrier((turned, above, below))
    first = weight_terms((-1,), norm, acts, turned)
    turned, first = barrier((turned, first))
    taps = 13
    parts = [weight, above, along_y(below[:taps], 1, True), along_y(above[taps:], -1, True), below]
    first = reduce_x_first(*first)
    second = weight_terms((0, 1), norm, acts, turned)
    held, first, second = barrier((held, first, second))
    second = reduce_x_first(*second)
    first = reduce_x_last(*first)
    grads = input_terms(held, parts)
    grads, first, second = barrier((grads, first, second))
    second = reduce_x_last(*second)
    send, keep, pass_on = grads
    got = swap(send, 1)
    far_grad = swap(pass_on + got[1], 2)
    mine, *others = split(first, second)
    others = [along_y(block, r, True) for r, block in zip((1, 2, 3), others)]
    others, far_grad = barrier((others, far_grad))
    for other in others:
        mine = mine + other.astype(F32)
    count = lax.axis_size("gx")
    other = lax.ppermute(mine.astype(BF16), "gx", [(g, g ^ 1) for g in range(count)])
    grad_weight = join(gather_x(mine + other.astype(F32)))
    grad_pre = finish(pre_act, keep, got, far_grad)
    return (grad_pre, grad_weight)


def solution(mesh):
    return jax.shard_map(
        body,
        mesh=mesh,
        in_specs=(P("gy", "gx", None, None), P("gy", "gx", None, None), P(None, "gy", None)),
        out_specs=(P("gy", "gx", None, None), P(None, "gy", None)),
        check_vma=False,
    )
```

```python
import functools
import math

import jax
import jax.numpy as jnp
from jax import lax
from jax.experimental import pallas as pl
from jax.experimental.pallas import tpu as pltpu
from jax.sharding import PartitionSpec as P

QUAD = 4
RING = 4
F32 = jnp.float32
BF16 = jnp.bfloat16
ANY = pl.BlockSpec(memory_space=pl.ANY)
VMEM = pl.BlockSpec(memory_space=pltpu.VMEM)
LIMIT = 24 * 1024 * 1024


def params():
    return pltpu.CompilerParams(vmem_limit_bytes=LIMIT)


def quad_place():
    return lax.rem(lax.axis_index("gy"), QUAD)


def x_place():
    return lax.div(lax.axis_index("gx"), 2)


def swap(block, k):
    count = lax.axis_size("gy")
    return lax.ppermute(block, "gy", [(g, g ^ k) for g in range(count)])


def along_y(block, step, ring):
    count = lax.axis_size("gy")
    pairs = [(g, g + QUAD * step) for g in range(count)]
    if ring:
        pairs = [(s, t % count) for s, t in pairs]
    return lax.ppermute(block, "gy", [(s, t) for s, t in pairs if 0 <= t < count])


def along_x(block, step):
    count = lax.axis_size("gx")
    return lax.ppermute(block, "gx", [(g, (g + 2 * step) % count) for g in range(count)])


def swap_x(block, first):
    count = lax.axis_size("gx")
    pairs = [(g, g + 1) for g in range(first, count - 1, 2)]
    return lax.ppermute(block, "gx", pairs + [(t, s) for s, t in pairs])


def zero_at(value, z, edge):
    return jnp.where(z == edge, 0.0, value)


def start_kernel(pre, cot, act, edge):
    value = pre[...].astype(F32)
    act[...] = (value * jax.nn.sigmoid(value)).astype(BF16)
    edge[...] = jnp.where(quad_place() == 0, cot[0], cot[cot.shape[0] - 1])


def start(pre_act, cot):
    return pl.pallas_call(
        start_kernel,
        out_shape=[
            jax.ShapeDtypeStruct(pre_act.shape, BF16),
            jax.ShapeDtypeStruct(cot.shape[1:], BF16),
        ],
        in_specs=[VMEM] * 2,
        out_specs=[VMEM] * 2,
        compiler_params=params(),
    )(pre_act, cot)


def side_kernel(cot, extra, even, odd):
    rows, width = cot.shape[:2]
    is_odd = lax.rem(lax.axis_index("gx"), 2) == 1

    def put(out, upper):
        out[0:rows] = jnp.where(upper, cot[:, width - 1], cot[:, 0])
        out[rows] = jnp.where(upper, extra[width - 1], extra[0])

    put(even, jnp.logical_not(is_odd))
    put(odd, is_odd)


def sides(cot, extra):
    rows, width, depth, chan = cot.shape
    return pl.pallas_call(
        side_kernel,
        out_shape=[jax.ShapeDtypeStruct((rows + 1, depth, chan), BF16)] * 2,
        in_specs=[VMEM] * 2,
        out_specs=[VMEM] * 2,
        compiler_params=params(),
    )(cot, extra)


def pick_kernel(cot, extra, even, odd, *quarters):
    rows, width, depth, chan = cot.shape
    j = quad_place()
    is_odd = lax.rem(lax.axis_index("gx"), 2) == 1
    q = chan // QUAD
    part = q // RING
    source = lax.broadcasted_iota(jnp.int32, (chan, q), 0)
    place = lax.broadcasted_iota(jnp.int32, (chan, q), 1)
    base = lax.div(place, part) * q + lax.rem(place, part)
    low = jnp.where(is_odd, even[...], odd[...])
    high = jnp.where(is_odd, odd[...], even[...])

    def take(block, pick):
        got = jnp.dot(block.reshape(-1, chan), pick, preferred_element_type=F32)
        return got.astype(BF16).reshape(block.shape[:-1] + (q,))

    for k, out in enumerate(quarters):
        pick = jnp.where(source == base + (j ^ k) * part, 1.0, 0.0).astype(BF16)
        out[0:rows, 1:width + 1] = take(cot[...], pick)
        out[rows, 1:width + 1] = take(extra[...], pick)
        out[:, 0] = take(low, pick)
        out[:, width + 1] = take(high, pick)


def pick_channels(cot, *rims):
    rows, width, depth, chan = cot.shape
    quarter = jax.ShapeDtypeStruct((rows + 1, width + 2, depth, chan // QUAD), BF16)
    return pl.pallas_call(
        pick_kernel,
        out_shape=[quarter] * QUAD,
        in_specs=[VMEM] * 4,
        out_specs=[VMEM] * QUAD,
        compiler_params=params(),
    )(cot, *rims)


def turn_kernel(p0, p1, p2, p3, held, out):
    j, x = quad_place(), x_place()
    for k, p in enumerate((p0, p1, p2, p3)):
        rows = p.shape[0] - 1
        held[pl.ds(1 + (j ^ k) * rows, rows)] = p[0:rows]

        @pl.when((j ^ k) == 0)
        def _():
            held[0] = p[rows]

        @pl.when((j ^ k) == QUAD - 1)
        def _():
            held[held.shape[0] - 1] = p[rows]

    tall, width, depth, q = held.shape
    width -= 2
    cells = tall * width * depth
    part = q // RING
    small = part // RING
    place = lax.broadcasted_iota(jnp.int32, (q, q), 0)
    source = lax.broadcasted_iota(jnp.int32, (q, q), 1)
    xpart = lax.rem(lax.div(place, part) + x, RING)
    base = lax.div(lax.rem(place, part), small) * part + xpart * small + lax.rem(place, small)
    order = jnp.where(source == base, 1.0, 0.0).astype(BF16)
    z = lax.rem(lax.broadcasted_iota(jnp.int32, (q, cells), 1), depth)
    for b in (-1, 0, 1):
        moved = held[:, 1 - b:1 - b + width].reshape(cells, q)
        value = lax.dot_general(
            order, moved, (((1,), (1,)), ((), ())), preferred_element_type=F32
        )
        high = zero_at(pltpu.roll(value, cells - 1, 1), z, depth - 1)
        low = zero_at(pltpu.roll(value, 1, 1), z, 0)
        for c, v in enumerate((high, value, low)):
            at = ((b + 1) * 3 + c) * q
            out[at:at + q] = v.astype(BF16)


def turn(quarters):
    rows, width, depth, q = quarters[0].shape
    tall = QUAD * (rows - 1) + 2
    return pl.pallas_call(
        turn_kernel,
        out_shape=[
            jax.ShapeDtypeStruct((tall, width, depth, q), BF16),
            jax.ShapeDtypeStruct((9 * q, tall * (width - 2) * depth), BF16),
        ],
        in_specs=[VMEM] * QUAD,
        out_specs=[VMEM] * 2,
        compiler_params=params(),
    )(*quarters)


def run_copies(pairs, sem):
    copies = [pltpu.make_async_copy(s, d, sem.at[n]) for n, (s, d) in enumerate(pairs)]
    for c in copies:
        c.start()
    return copies


def weight_kernel(norm, own_act, near, far, across, cot, *refs):
    right, left, keep_right, keep_left, own, held, sem = refs
    j = quad_place()
    rows, width, depth, chan = own_act.shape
    pairs = []
    for k, piece in enumerate((own_act, near, far, across)):
        pairs.append((piece, held.at[pl.ds((j ^ k) * rows, rows)]))
    for c in run_copies(pairs, sem):
        c.wait()
    row = width * depth
    cells = QUAD * rows * row
    act = held[...].reshape(cells, chan)
    q = cot.shape[0] // 9
    part = q // RING
    half = part // 2
    for n in range(9):
        a, b = n // 3 - 1, n % 3
        moved = cot[3 * b * q:3 * (b + 1) * q, (1 - a) * row:(1 - a) * row + cells]
        term = jnp.dot(moved, act, preferred_element_type=F32) * norm
        for c in range(3):
            tap = 3 * n + c

            def block(r, h):
                at = c * q + r * part + h * half
                return term[at:at + half]

            right[0, tap] = block(2, 0).astype(BF16)
            left[0, tap] = block(2, 1).astype(BF16)
            keep_right[tap] = block(1, 0)
            right[1, tap] = block(1, 1).astype(BF16)
            left[1, tap] = block(3, 0).astype(BF16)
            keep_left[tap] = block(3, 1)
            own[0, tap] = block(0, 0)
            own[1, tap] = block(0, 1)


def weight_terms(norm, acts, cot):
    rows, width, depth, chan = acts[0].shape
    q = chan // QUAD
    shape = (27, q // RING // 2, chan)
    cells = QUAD * rows * width * depth
    return pl.pallas_call(
        functools.partial(weight_kernel, norm),
        out_shape=[jax.ShapeDtypeStruct((2,) + shape, BF16)] * 2
        + [jax.ShapeDtypeStruct(shape, F32)] * 2
        + [jax.ShapeDtypeStruct((2,) + shape, F32)],
        in_specs=[ANY] * 4 + [VMEM],
        out_specs=[VMEM] * 5,
        scratch_shapes=[
            pltpu.VMEM((QUAD * rows, width, depth, chan), BF16),
            pltpu.SemaphoreType.DMA((4,)),
        ],
        compiler_params=params(),
        cost_estimate=pl.CostEstimate(
            flops=2 * 27 * q * cells * chan, bytes_accessed=10_000_000, transcendentals=0
        ),
    )(*acts, cot)


def input_kernel(held, own, above, across_low, across_high, below, *refs):
    send, keep, pass_on, weights, sem = refs
    j = quad_place()
    y = lax.div(lax.axis_index("gy"), QUAD)
    part = own.shape[1]
    low = across_low.shape[0]

    def at(s):
        return pl.ds(pl.multiple_of(lax.rem(y + s, RING) * part, part), part)

    pairs = [
        (own, weights.at[:, at(0)]),
        (above, weights.at[:, at(1)]),
        (across_low, weights.at[pl.ds(0, low), at(2)]),
        (across_high, weights.at[pl.ds(low, 27 - low), at(2)]),
        (below, weights.at[:, at(3)]),
    ]
    for c in run_copies(pairs, sem):
        c.wait()
    rows, width, depth, chan = keep.shape
    cells = rows * width * depth
    q = held.shape[3]
    taps = weights[...].reshape(9, 3, q, chan)
    for k, out in ((1, send.at[0]), (3, send.at[1]), (2, pass_on), (0, keep)):
        first = (j ^ k) * rows
        moved = []
        for n in range(9):
            a, b = n // 3 - 1, n % 3 - 1
            block = held[pl.ds(first + 1 - a, rows), 1 - b:1 - b + width]
            moved.append(block.reshape(cells, q))
        moved = jnp.concatenate(moved, axis=1)
        z = lax.rem(lax.broadcasted_iota(jnp.int32, (cells, chan), 0), depth)

        def term(c):
            return jnp.dot(moved, taps[:, c].reshape(9 * q, chan), preferred_element_type=F32)

        grad = term(1)
        grad = grad + zero_at(pltpu.roll(term(0), cells - 1, 0), z, depth - 1)
        grad = grad + zero_at(pltpu.roll(term(2), 1, 0), z, 0)
        out[...] = grad.reshape(rows, width, depth, chan)


def input_terms(held, parts):
    tall, width, depth, q = held.shape
    chan = QUAD * q
    block = ((tall - 2) // QUAD, width - 2, depth, chan)
    return pl.pallas_call(
        input_kernel,
        out_shape=[
            jax.ShapeDtypeStruct((2,) + block, F32),
            jax.ShapeDtypeStruct(block, F32),
            jax.ShapeDtypeStruct(block, F32),
        ],
        in_specs=[VMEM] + [ANY] * 5,
        out_specs=[VMEM] * 3,
        scratch_shapes=[pltpu.VMEM((27, q, chan), BF16), pltpu.SemaphoreType.DMA((5,))],
        compiler_params=params(),
        cost_estimate=pl.CostEstimate(
            flops=2 * 27 * tall * width * depth * q * chan, bytes_accessed=10_000_000, transcendentals=0
        ),
    )(held, *parts)


def finish_kernel(pre, keep, near, far, out):
    value = pre[...].astype(F32)
    s = jax.nn.sigmoid(value)
    grad = keep[...] + near[0] + far[...]
    out[...] = (grad * s * (1.0 + value * (1.0 - s))).astype(BF16)


def finish(pre_act, keep, near, far):
    return pl.pallas_call(
        finish_kernel,
        out_shape=jax.ShapeDtypeStruct(pre_act.shape, BF16),
        in_specs=[VMEM] * 4,
        out_specs=VMEM,
        compiler_params=params(),
    )(pre_act, keep, near, far)


def split_kernel(own, from_left, from_right, last_left, last_right, *refs):
    outs, total = refs[:-1], refs[-1]
    y = lax.div(lax.axis_index("gy"), QUAD)
    size = own.shape[2] // 2
    low = own[0] + from_right[1].astype(F32) + last_left[...].astype(F32)
    high = own[1] + from_left[1].astype(F32) + last_right[...].astype(F32)
    for half, value in enumerate((low, high)):
        for sub in range(2):
            total[2 * half + sub] = value[:, sub * size:(sub + 1) * size]
    for r, out in enumerate(outs):
        out[...] = total[lax.rem(y + r, RING)].astype(out.dtype)


def split(*parts):
    _, taps, rows, chan = parts[0].shape
    shape = (taps, rows // 2, chan)
    return pl.pallas_call(
        split_kernel,
        out_shape=[jax.ShapeDtypeStruct(shape, F32)] + [jax.ShapeDtypeStruct(shape, BF16)] * 3,
        in_specs=[VMEM] * 5,
        out_specs=[VMEM] * 4,
        scratch_shapes=[pltpu.VMEM((RING,) + shape, F32)],
        compiler_params=params(),
    )(*parts)


def join_kernel(*refs):
    out = refs[-1]
    x = x_place()
    size = refs[0].shape[1]
    low = refs[0].shape[0]
    for piece, part, k in zip(refs, (0, 1) * RING, (0, 0, 3, 3, 1, 1, 2, 2)):
        at = pl.ds(pl.multiple_of(lax.rem(x + k, RING) * size, size), size)
        first = part * low
        out[first:first + piece.shape[0], at] = piece[...]


def gather_x(low, high):
    low_below, high_above = along_x(low, 1), along_x(high, -1)
    high_below, low_above = along_x(high, 1), along_x(low, -1)
    low_far, high_far = along_x(low_below, 1), along_x(high_above, -1)
    _, size, chan = low.shape
    pieces = (low, high, low_below, high_below, low_above, high_above, low_far, high_far)
    return pl.pallas_call(
        join_kernel,
        out_shape=jax.ShapeDtypeStruct((27, RING * size, chan), F32),
        in_specs=[VMEM] * 8,
        out_specs=VMEM,
        compiler_params=params(),
    )(*pieces)


def body(pre_act, cot, weight):
    rows, width, depth, chan = pre_act.shape
    norm = 1.0 / math.sqrt(rows * lax.axis_size("gy") * width * lax.axis_size("gx") * depth)
    j = quad_place()
    barrier = lax.optimization_barrier

    count = lax.axis_size("gy")
    pairs = [(g, g + 1) for g in range(QUAD - 1, count - 1, QUAD)]
    pairs = pairs + [(t, s) for s, t in pairs]
    act, edge = start(pre_act, cot)
    extra = lax.ppermute(edge, "gy", pairs)
    far = swap(act, 2)
    near = swap(act, 1)
    extra, near, weight = barrier((extra, near, weight))
    above = along_y(weight, -1, True)
    below = along_y(weight, 1, True)
    even, odd = sides(cot, extra)
    quarters = pick_channels(cot, extra, swap_x(even, 0), swap_x(odd, 1))
    quarters, far = barrier((quarters, far))
    quarters = [quarters[0]] + [swap(quarters[k], k) for k in (1, 2, 3)]
    quarters, far = barrier((quarters, far))
    acts = [act, near, far, swap(far, 1)]
    held, turned = turn(quarters)

    turned, above, below = barrier((turned, above, below))
    taps = 13
    parts = [weight, above, along_y(below[:taps], 1, True), along_y(above[taps:], -1, True), below]
    right, left, *kept = weight_terms(norm, acts, turned)
    held, right, left = barrier((held, right, left))
    from_left, from_right = along_x(right, 1), along_x(left, -1)
    grads = input_terms(held, parts)
    send, keep, pass_on = grads
    got = swap(send, 1)
    passed, from_left, from_right = barrier((pass_on + got[1], from_left, from_right))
    far_grad = swap(passed, 2)
    keep_right, keep_left, own = kept
    right = (from_left[0].astype(F32) + keep_right).astype(BF16)
    left = (from_right[0].astype(F32) + keep_left).astype(BF16)
    mine, *others = split(own, from_left, from_right, along_x(right, 1), along_x(left, -1))

    others = [along_y(block, r, True) for r, block in zip((1, 2, 3), others)]
    others, far_grad = barrier((others, far_grad))
    for other in others:
        mine = mine + other.astype(F32)
    count = lax.axis_size("gx")
    other = lax.ppermute(mine.astype(BF16), "gx", [(g, g ^ 1) for g in range(count)])
    low, high = [mine[s] + other[s].astype(F32) for s in (slice(0, taps), slice(taps, 27))]
    grad_weight = gather_x(low, high)
    grad_pre = finish(pre_act, keep, got, far_grad)
    return (grad_pre, grad_weight)


def solution(mesh):
    return jax.shard_map(
        body,
        mesh=mesh,
        in_specs=(P("gy", "gx", None, None), P("gy", "gx", None, None), P(None, "gy", None)),
        out_specs=(P("gy", "gx", None, None), P(None, "gy", None)),
        check_vma=False,
    )
```

```python
import functools
import math

import jax
import jax.numpy as jnp
from jax import lax
from jax.experimental import pallas as pl
from jax.experimental.pallas import tpu as pltpu
from jax.sharding import PartitionSpec as P

QUAD = 4
RING = 4
F32 = jnp.float32
BF16 = jnp.bfloat16
ANY = pl.BlockSpec(memory_space=pl.ANY)
VMEM = pl.BlockSpec(memory_space=pltpu.VMEM)
LIMIT = 24 * 1024 * 1024


def params():
    return pltpu.CompilerParams(vmem_limit_bytes=LIMIT)


def quad_place():
    return lax.rem(lax.axis_index("gy"), QUAD)


def x_place():
    return lax.div(lax.axis_index("gx"), 2)


def swap(block, k):
    count = lax.axis_size("gy")
    return lax.ppermute(block, "gy", [(g, g ^ k) for g in range(count)])


def along_y(block, step, ring):
    count = lax.axis_size("gy")
    pairs = [(g, g + QUAD * step) for g in range(count)]
    if ring:
        pairs = [(s, t % count) for s, t in pairs]
    return lax.ppermute(block, "gy", [(s, t) for s, t in pairs if 0 <= t < count])


def along_x(block, step):
    count = lax.axis_size("gx")
    return lax.ppermute(block, "gx", [(g, (g + 2 * step) % count) for g in range(count)])


def swap_x(block, first):
    count = lax.axis_size("gx")
    pairs = [(g, g + 1) for g in range(first, count - 1, 2)]
    return lax.ppermute(block, "gx", pairs + [(t, s) for s, t in pairs])


def zero_at(value, z, edge):
    return jnp.where(z == edge, 0.0, value)


def start_kernel(pre, cot, act, edge):
    value = pre[...].astype(F32)
    act[...] = (value * jax.nn.sigmoid(value)).astype(BF16)
    edge[...] = jnp.where(quad_place() == 0, cot[0], cot[cot.shape[0] - 1])


def start(pre_act, cot):
    return pl.pallas_call(
        start_kernel,
        out_shape=[
            jax.ShapeDtypeStruct(pre_act.shape, BF16),
            jax.ShapeDtypeStruct(cot.shape[1:], BF16),
        ],
        in_specs=[VMEM] * 2,
        out_specs=[VMEM] * 2,
        compiler_params=params(),
    )(pre_act, cot)


def pick_kernel(cot, extra, *quarters):
    rows, _, _, chan = cot.shape
    j = quad_place()
    q = chan // QUAD
    part = q // RING
    source = lax.broadcasted_iota(jnp.int32, (chan, q), 0)
    place = lax.broadcasted_iota(jnp.int32, (chan, q), 1)
    base = lax.div(place, part) * q + lax.rem(place, part)

    def take(block, pick):
        got = jnp.dot(block.reshape(-1, chan), pick, preferred_element_type=F32)
        return got.astype(BF16).reshape(block.shape[:-1] + (q,))

    for k, out in enumerate(quarters):
        pick = jnp.where(source == base + (j ^ k) * part, 1.0, 0.0).astype(BF16)
        out[0:rows] = take(cot[...], pick)
        out[rows] = take(extra[...], pick)


def pick_channels(cot, extra):
    rows, width, depth, chan = cot.shape
    quarter = jax.ShapeDtypeStruct((rows + 1, width, depth, chan // QUAD), BF16)
    return pl.pallas_call(
        pick_kernel,
        out_shape=[quarter] * QUAD,
        in_specs=[VMEM] * 2,
        out_specs=[VMEM] * QUAD,
        compiler_params=params(),
    )(cot, extra)


def side_kernel(p0, p1, p2, p3, even, odd):
    width = p0.shape[1]
    is_odd = lax.rem(lax.axis_index("gx"), 2) == 1
    for k, p in enumerate((p0, p1, p2, p3)):
        first, last = p[:, 0], p[:, width - 1]
        even[k] = jnp.where(is_odd, first, last)
        odd[k] = jnp.where(is_odd, last, first)


def sides(quarters):
    rows, _, depth, q = quarters[0].shape
    return pl.pallas_call(
        side_kernel,
        out_shape=[jax.ShapeDtypeStruct((QUAD, rows, depth, q), BF16)] * 2,
        in_specs=[VMEM] * QUAD,
        out_specs=[VMEM] * 2,
        compiler_params=params(),
    )(*quarters)


def turn_kernel(p0, p1, p2, p3, even, odd, held, out):
    j, x = quad_place(), x_place()
    is_odd = lax.rem(lax.axis_index("gx"), 2) == 1
    for k, p in enumerate((p0, p1, p2, p3)):
        rows, width = p.shape[0] - 1, p.shape[1]
        low = jnp.where(is_odd, even[k], odd[k])
        high = jnp.where(is_odd, odd[k], even[k])

        def put(at, part):
            held[at, 1:width + 1] = p[part]
            held[at, 0] = low[part]
            held[at, width + 1] = high[part]

        put(pl.ds(1 + (j ^ k) * rows, rows), slice(0, rows))
        pl.when((j ^ k) == 0)(functools.partial(put, 0, rows))
        pl.when((j ^ k) == QUAD - 1)(functools.partial(put, held.shape[0] - 1, rows))

    tall, width, depth, q = held.shape
    width -= 2
    cells = tall * width * depth
    part = q // RING
    small = part // RING
    place = lax.broadcasted_iota(jnp.int32, (q, q), 0)
    source = lax.broadcasted_iota(jnp.int32, (q, q), 1)
    xpart = lax.rem(lax.div(place, part) + x, RING)
    base = lax.div(lax.rem(place, part), small) * part + xpart * small + lax.rem(place, small)
    order = jnp.where(source == base, 1.0, 0.0).astype(BF16)
    z = lax.rem(lax.broadcasted_iota(jnp.int32, (q, cells), 1), depth)
    for b in (-1, 0, 1):
        moved = held[:, 1 - b:1 - b + width].reshape(cells, q)
        value = lax.dot_general(
            order, moved, (((1,), (1,)), ((), ())), preferred_element_type=F32
        )
        high = zero_at(pltpu.roll(value, cells - 1, 1), z, depth - 1)
        low = zero_at(pltpu.roll(value, 1, 1), z, 0)
        for c, v in enumerate((high, value, low)):
            at = ((b + 1) * 3 + c) * q
            out[at:at + q] = v.astype(BF16)


def turn(quarters, even, odd):
    rows, width, depth, q = quarters[0].shape
    width += 2
    tall = QUAD * (rows - 1) + 2
    return pl.pallas_call(
        turn_kernel,
        out_shape=[
            jax.ShapeDtypeStruct((tall, width, depth, q), BF16),
            jax.ShapeDtypeStruct((9 * q, tall * (width - 2) * depth), BF16),
        ],
        in_specs=[VMEM] * (QUAD + 2),
        out_specs=[VMEM] * 2,
        compiler_params=params(),
    )(*quarters, even, odd)


def run_copies(pairs, sem):
    copies = [pltpu.make_async_copy(s, d, sem.at[n]) for n, (s, d) in enumerate(pairs)]
    for c in copies:
        c.start()
    return copies


def weight_kernel(norm, own_act, near, far, across, cot, *refs):
    right, left, keep_right, keep_left, own, held, sem = refs
    j = quad_place()
    rows, width, depth, chan = own_act.shape
    pairs = []
    for k, piece in enumerate((own_act, near, far, across)):
        pairs.append((piece, held.at[pl.ds((j ^ k) * rows, rows)]))
    for c in run_copies(pairs, sem):
        c.wait()
    row = width * depth
    cells = QUAD * rows * row
    act = held[...].reshape(cells, chan)
    q = cot.shape[0] // 9
    part = q // RING
    half = part // 2
    for n in range(9):
        a, b = n // 3 - 1, n % 3
        moved = cot[3 * b * q:3 * (b + 1) * q, (1 - a) * row:(1 - a) * row + cells]
        term = jnp.dot(moved, act, preferred_element_type=F32) * norm
        for c in range(3):
            tap = 3 * n + c

            def block(r, h):
                at = c * q + r * part + h * half
                return term[at:at + half]

            right[0, tap] = block(2, 0).astype(BF16)
            left[0, tap] = block(2, 1).astype(BF16)
            keep_right[tap] = block(1, 0)
            right[1, tap] = block(1, 1).astype(BF16)
            left[1, tap] = block(3, 0).astype(BF16)
            keep_left[tap] = block(3, 1)
            own[0, tap] = block(0, 0)
            own[1, tap] = block(0, 1)


def weight_terms(norm, acts, cot):
    rows, width, depth, chan = acts[0].shape
    q = chan // QUAD
    shape = (27, q // RING // 2, chan)
    cells = QUAD * rows * width * depth
    return pl.pallas_call(
        functools.partial(weight_kernel, norm),
        out_shape=[jax.ShapeDtypeStruct((2,) + shape, BF16)] * 2
        + [jax.ShapeDtypeStruct(shape, F32)] * 2
        + [jax.ShapeDtypeStruct((2,) + shape, F32)],
        in_specs=[ANY] * 4 + [VMEM],
        out_specs=[VMEM] * 5,
        scratch_shapes=[
            pltpu.VMEM((QUAD * rows, width, depth, chan), BF16),
            pltpu.SemaphoreType.DMA((4,)),
        ],
        compiler_params=params(),
        cost_estimate=pl.CostEstimate(
            flops=2 * 27 * q * cells * chan, bytes_accessed=10_000_000, transcendentals=0
        ),
    )(*acts, cot)


def input_kernel(held, own, above, across_low, across_high, below, *refs):
    send, keep, pass_on, weights, sem = refs
    j = quad_place()
    y = lax.div(lax.axis_index("gy"), QUAD)
    part = own.shape[1]
    low = across_low.shape[0]

    def at(s):
        return pl.ds(pl.multiple_of(lax.rem(y + s, RING) * part, part), part)

    pairs = [
        (own, weights.at[:, at(0)]),
        (above, weights.at[:, at(1)]),
        (across_low, weights.at[pl.ds(0, low), at(2)]),
        (across_high, weights.at[pl.ds(low, 27 - low), at(2)]),
        (below, weights.at[:, at(3)]),
    ]
    for c in run_copies(pairs, sem):
        c.wait()
    rows, width, depth, chan = keep.shape
    cells = rows * width * depth
    q = held.shape[3]
    taps = weights[...].reshape(9, 3, q, chan)
    for k, out in ((1, send.at[0]), (3, send.at[1]), (2, pass_on), (0, keep)):
        first = (j ^ k) * rows
        moved = []
        for n in range(9):
            a, b = n // 3 - 1, n % 3 - 1
            block = held[pl.ds(first + 1 - a, rows), 1 - b:1 - b + width]
            moved.append(block.reshape(cells, q))
        moved = jnp.concatenate(moved, axis=1)
        z = lax.rem(lax.broadcasted_iota(jnp.int32, (cells, chan), 0), depth)

        def term(c):
            return jnp.dot(moved, taps[:, c].reshape(9 * q, chan), preferred_element_type=F32)

        grad = term(1)
        grad = grad + zero_at(pltpu.roll(term(0), cells - 1, 0), z, depth - 1)
        grad = grad + zero_at(pltpu.roll(term(2), 1, 0), z, 0)
        out[...] = grad.reshape(rows, width, depth, chan)


def input_terms(held, parts):
    tall, width, depth, q = held.shape
    chan = QUAD * q
    block = ((tall - 2) // QUAD, width - 2, depth, chan)
    return pl.pallas_call(
        input_kernel,
        out_shape=[
            jax.ShapeDtypeStruct((2,) + block, F32),
            jax.ShapeDtypeStruct(block, F32),
            jax.ShapeDtypeStruct(block, F32),
        ],
        in_specs=[VMEM] + [ANY] * 5,
        out_specs=[VMEM] * 3,
        scratch_shapes=[pltpu.VMEM((27, q, chan), BF16), pltpu.SemaphoreType.DMA((5,))],
        compiler_params=params(),
        cost_estimate=pl.CostEstimate(
            flops=2 * 27 * tall * width * depth * q * chan, bytes_accessed=10_000_000, transcendentals=0
        ),
    )(held, *parts)


def finish_kernel(pre, keep, near, far_low, far_high, out):
    rows = far_low.shape[0]
    for at, far in ((0, far_low), (rows, far_high)):
        value = pre[at:at + rows].astype(F32)
        s = jax.nn.sigmoid(value)
        grad = keep[at:at + rows] + near[0, at:at + rows] + far[...]
        out[at:at + rows] = (grad * s * (1.0 + value * (1.0 - s))).astype(BF16)


def finish(pre_act, keep, near, *far):
    return pl.pallas_call(
        finish_kernel,
        out_shape=jax.ShapeDtypeStruct(pre_act.shape, BF16),
        in_specs=[VMEM] * 5,
        out_specs=VMEM,
        compiler_params=params(),
    )(pre_act, keep, near, *far)


def split_kernel(own, from_left, from_right, last_left, last_right, *refs):
    outs, total = refs[:-1], refs[-1]
    y = lax.div(lax.axis_index("gy"), QUAD)
    size = own.shape[2] // 2
    low = own[0] + from_right[1].astype(F32) + last_left[...].astype(F32)
    high = own[1] + from_left[1].astype(F32) + last_right[...].astype(F32)
    for half, value in enumerate((low, high)):
        for sub in range(2):
            total[2 * half + sub] = value[:, sub * size:(sub + 1) * size]
    for r, out in enumerate(outs):
        out[...] = total[lax.rem(y + r, RING)].astype(out.dtype)


def split(*parts):
    _, taps, rows, chan = parts[0].shape
    shape = (taps, rows // 2, chan)
    return pl.pallas_call(
        split_kernel,
        out_shape=[jax.ShapeDtypeStruct(shape, F32)] + [jax.ShapeDtypeStruct(shape, BF16)] * 3,
        in_specs=[VMEM] * 5,
        out_specs=[VMEM] * 4,
        scratch_shapes=[pltpu.VMEM((RING,) + shape, F32)],
        compiler_params=params(),
    )(*parts)


def join_kernel(*refs):
    out = refs[-1]
    x = x_place()
    size = refs[0].shape[1]
    low = refs[0].shape[0]
    for piece, part, k in zip(refs, (0, 1) * RING, (0, 0, 3, 3, 1, 1, 2, 2)):
        at = pl.ds(pl.multiple_of(lax.rem(x + k, RING) * size, size), size)
        first = part * low
        out[first:first + piece.shape[0], at] = piece[...]


def gather_x(low, high):
    low_below, high_above = along_x(low, 1), along_x(high, -1)
    high_below, low_above = along_x(high, 1), along_x(low, -1)
    low_far, high_far = along_x(low_below, 1), along_x(high_above, -1)
    _, size, chan = low.shape
    pieces = (low, high, low_below, high_below, low_above, high_above, low_far, high_far)
    return pl.pallas_call(
        join_kernel,
        out_shape=jax.ShapeDtypeStruct((27, RING * size, chan), F32),
        in_specs=[VMEM] * 8,
        out_specs=VMEM,
        compiler_params=params(),
    )(*pieces)


def body(pre_act, cot, weight):
    rows, width, depth, chan = pre_act.shape
    norm = 1.0 / math.sqrt(rows * lax.axis_size("gy") * width * lax.axis_size("gx") * depth)
    j = quad_place()
    barrier = lax.optimization_barrier

    count = lax.axis_size("gy")
    pairs = [(g, g + 1) for g in range(QUAD - 1, count - 1, QUAD)]
    pairs = pairs + [(t, s) for s, t in pairs]
    act, edge = start(pre_act, cot)
    extra = lax.ppermute(edge, "gy", pairs)
    far = swap(act, 2)
    near = swap(act, 1)
    extra, near, weight = barrier((extra, near, weight))
    above = along_y(weight, -1, True)
    below = along_y(weight, 1, True)
    quarters = pick_channels(cot, extra)
    quarters = [quarters[0]] + [swap(quarters[k], k) for k in (1, 2, 3)]
    quarters, far = barrier((quarters, far))
    acts = [act, near, far, swap(far, 1)]
    even, odd = sides(quarters)
    held, turned = turn(quarters, swap_x(even, 0), swap_x(odd, 1))

    turned, above, below = barrier((turned, above, below))
    right, left, *kept = weight_terms(norm, acts, turned)
    held, right, left, above, below = barrier((held, right, left, above, below))
    taps = 13
    parts = [weight, above, along_y(below[:taps], 1, True), along_y(above[taps:], -1, True), below]
    from_left, from_right = along_x(right, 1), along_x(left, -1)
    grads = input_terms(held, parts)
    grads, from_left, from_right = barrier((grads, from_left, from_right))
    send, keep, pass_on = grads
    got = swap(send, 1)
    keep_right, keep_left, own = kept
    right = (from_left[0].astype(F32) + keep_right).astype(BF16)
    left = (from_right[0].astype(F32) + keep_left).astype(BF16)
    last_left, last_right = along_x(right, 1), along_x(left, -1)
    half = rows // 2
    passed = [pass_on[s] + got[1, s] for s in (slice(0, half), slice(half, rows))]
    last_left, last_right, passed = barrier((last_left, last_right, passed))
    far_low = swap(passed[0], 2)
    mine, *others = split(own, from_left, from_right, last_left, last_right)

    others = [along_y(block, r, True) for r, block in zip((1, 2, 3), others)]
    others, far_low = barrier((others, far_low))
    for other in others:
        mine = mine + other.astype(F32)
    count = lax.axis_size("gx")
    other = lax.ppermute(mine.astype(BF16), "gx", [(g, g ^ 1) for g in range(count)])
    other, passed = barrier((other, passed))
    far_high = swap(passed[1], 2)
    low, high = [mine[s] + other[s].astype(F32) for s in (slice(0, taps), slice(taps, 27))]
    grad_weight = gather_x(low, high)
    grad_pre = finish(pre_act, keep, got, far_low, far_high)
    return (grad_pre, grad_weight)


def solution(mesh):
    return jax.shard_map(
        body,
        mesh=mesh,
        in_specs=(P("gy", "gx", None, None), P("gy", "gx", None, None), P(None, "gy", None)),
        out_specs=(P("gy", "gx", None, None), P(None, "gy", None)),
        check_vma=False,
    )
```

```python
import functools
import math

import jax
import jax.numpy as jnp
from jax import lax
from jax.experimental import pallas as pl
from jax.experimental.pallas import tpu as pltpu
from jax.sharding import PartitionSpec as P

QUAD = 4
RING = 4
XTAPS = 13
F32 = jnp.float32
BF16 = jnp.bfloat16
ANY = pl.BlockSpec(memory_space=pl.ANY)
VMEM = pl.BlockSpec(memory_space=pltpu.VMEM)
LIMIT = 24 * 1024 * 1024


def params():
    return pltpu.CompilerParams(vmem_limit_bytes=LIMIT)


def quad_place():
    return lax.rem(lax.axis_index("gy"), QUAD)


def x_place():
    return lax.div(lax.axis_index("gx"), 2)


def y_place():
    return lax.div(lax.axis_index("gy"), QUAD)


def swap(block, k):
    count = lax.axis_size("gy")
    return lax.ppermute(block, "gy", [(g, g ^ k) for g in range(count)])


def along_y(block, step, ring):
    count = lax.axis_size("gy")
    pairs = [(g, g + QUAD * step) for g in range(count)]
    if ring:
        pairs = [(s, t % count) for s, t in pairs]
    return lax.ppermute(block, "gy", [(s, t) for s, t in pairs if 0 <= t < count])


def along_x(block, step):
    count = lax.axis_size("gx")
    return lax.ppermute(block, "gx", [(g, (g + 2 * step) % count) for g in range(count)])


def swap_x(block, first):
    count = lax.axis_size("gx")
    pairs = [(g, g + 1) for g in range(first, count - 1, 2)]
    return lax.ppermute(block, "gx", pairs + [(t, s) for s, t in pairs])


def zero_at(value, z, edge):
    return jnp.where(z == edge, 0.0, value)


def start_kernel(pre, cot, act, edge):
    value = pre[...].astype(F32)
    act[...] = (value * jax.nn.sigmoid(value)).astype(BF16)
    edge[...] = jnp.where(quad_place() == 0, cot[0], cot[cot.shape[0] - 1])


def start(pre_act, cot):
    return pl.pallas_call(
        start_kernel,
        out_shape=[
            jax.ShapeDtypeStruct(pre_act.shape, BF16),
            jax.ShapeDtypeStruct(cot.shape[1:], BF16),
        ],
        in_specs=[VMEM] * 2,
        out_specs=[VMEM] * 2,
        compiler_params=params(),
    )(pre_act, cot)


def pick_kernel(cot, extra, *quarters):
    rows, _, _, chan = cot.shape
    j = quad_place()
    q = chan // QUAD
    part = q // RING
    source = lax.broadcasted_iota(jnp.int32, (chan, q), 0)
    place = lax.broadcasted_iota(jnp.int32, (chan, q), 1)
    base = lax.div(place, part) * q + lax.rem(place, part)

    def take(block, pick):
        got = jnp.dot(block.reshape(-1, chan), pick, preferred_element_type=F32)
        return got.astype(BF16).reshape(block.shape[:-1] + (q,))

    for k, out in enumerate(quarters):
        pick = jnp.where(source == base + (j ^ k) * part, 1.0, 0.0).astype(BF16)
        out[0:rows] = take(cot[...], pick)
        out[rows] = take(extra[...], pick)


def pick_channels(cot, extra):
    rows, width, depth, chan = cot.shape
    quarter = jax.ShapeDtypeStruct((rows + 1, width, depth, chan // QUAD), BF16)
    return pl.pallas_call(
        pick_kernel,
        out_shape=[quarter] * QUAD,
        in_specs=[VMEM] * 2,
        out_specs=[VMEM] * QUAD,
        compiler_params=params(),
    )(cot, extra)


def side_kernel(p0, p1, p2, p3, even, odd):
    width = p0.shape[1]
    is_odd = lax.rem(lax.axis_index("gx"), 2) == 1
    for k, p in enumerate((p0, p1, p2, p3)):
        first, last = p[:, 0], p[:, width - 1]
        even[k] = jnp.where(is_odd, first, last)
        odd[k] = jnp.where(is_odd, last, first)


def sides(quarters):
    rows, _, depth, q = quarters[0].shape
    return pl.pallas_call(
        side_kernel,
        out_shape=[jax.ShapeDtypeStruct((QUAD, rows, depth, q), BF16)] * 2,
        in_specs=[VMEM] * QUAD,
        out_specs=[VMEM] * 2,
        compiler_params=params(),
    )(*quarters)


def turn_kernel(p0, p1, p2, p3, even, odd, held, out):
    j, x = quad_place(), x_place()
    is_odd = lax.rem(lax.axis_index("gx"), 2) == 1
    for k, p in enumerate((p0, p1, p2, p3)):
        rows, width = p.shape[0] - 1, p.shape[1]
        low = jnp.where(is_odd, even[k], odd[k])
        high = jnp.where(is_odd, odd[k], even[k])

        def put(at, part):
            held[at, 1:width + 1] = p[part]
            held[at, 0] = low[part]
            held[at, width + 1] = high[part]

        put(pl.ds(1 + (j ^ k) * rows, rows), slice(0, rows))
        pl.when((j ^ k) == 0)(functools.partial(put, 0, rows))
        pl.when((j ^ k) == QUAD - 1)(functools.partial(put, held.shape[0] - 1, rows))

    tall, width, depth, q = held.shape
    width -= 2
    cells = tall * width * depth
    part = q // RING
    small = part // RING
    place = lax.broadcasted_iota(jnp.int32, (q, q), 0)
    source = lax.broadcasted_iota(jnp.int32, (q, q), 1)
    xpart = lax.rem(lax.div(place, part) + x, RING)
    ypart = lax.rem(lax.div(lax.rem(place, part), small) + y_place(), RING)
    base = ypart * part + xpart * small + lax.rem(place, small)
    order = jnp.where(source == base, 1.0, 0.0).astype(BF16)
    z = lax.rem(lax.broadcasted_iota(jnp.int32, (q, cells), 1), depth)
    for b in (-1, 0, 1):
        moved = held[:, 1 - b:1 - b + width].reshape(cells, q)
        value = lax.dot_general(
            order, moved, (((1,), (1,)), ((), ())), preferred_element_type=F32
        )
        high = zero_at(pltpu.roll(value, cells - 1, 1), z, depth - 1)
        low = zero_at(pltpu.roll(value, 1, 1), z, 0)
        for c, v in enumerate((high, value, low)):
            at = ((b + 1) * 3 + c) * q
            out[at:at + q] = v.astype(BF16)


def turn(quarters, even, odd):
    rows, width, depth, q = quarters[0].shape
    width += 2
    tall = QUAD * (rows - 1) + 2
    return pl.pallas_call(
        turn_kernel,
        out_shape=[
            jax.ShapeDtypeStruct((tall, width, depth, q), BF16),
            jax.ShapeDtypeStruct((9 * q, tall * (width - 2) * depth), BF16),
        ],
        in_specs=[VMEM] * (QUAD + 2),
        out_specs=[VMEM] * 2,
        compiler_params=params(),
    )(*quarters, even, odd)


def run_copies(pairs, sem):
    copies = [pltpu.make_async_copy(s, d, sem.at[n]) for n, (s, d) in enumerate(pairs)]
    for c in copies:
        c.start()
    return copies


def weight_kernel(norm, own_act, near, far, across, cot, *refs):
    groups, held, sem = (refs[:5], refs[5:10]), *refs[10:]
    j = quad_place()
    rows, width, depth, chan = own_act.shape
    pairs = []
    for k, piece in enumerate((own_act, near, far, across)):
        pairs.append((piece, held.at[pl.ds((j ^ k) * rows, rows)]))
    for c in run_copies(pairs, sem):
        c.wait()
    row = width * depth
    cells = QUAD * rows * row
    act = held[...].reshape(cells, chan)
    q = cot.shape[0] // 9
    small = q // RING // RING
    for n in range(9):
        a, b = n // 3 - 1, n % 3
        moved = cot[3 * b * q:3 * (b + 1) * q, (1 - a) * row:(1 - a) * row + cells]
        term = jnp.dot(moved, act, preferred_element_type=F32) * norm
        for c in range(3):
            tap = 3 * n + c
            by_y = tap >= XTAPS
            up, down, keep_up, keep_down, own = groups[by_y]
            tap -= XTAPS * by_y

            def block(r, h):
                spots = [(2 * h, r), (2 * h + 1, r)] if by_y else [(r, 2 * h), (r, 2 * h + 1)]
                starts = [c * q + (xr * RING + yr) * small for xr, yr in spots]
                return jnp.concatenate([term[at:at + small] for at in starts], axis=0)

            up[0, tap] = block(2, 0).astype(BF16)
            down[0, tap] = block(2, 1).astype(BF16)
            keep_up[tap] = block(1, 0)
            up[1, tap] = block(1, 1).astype(BF16)
            down[1, tap] = block(3, 0).astype(BF16)
            keep_down[tap] = block(3, 1)
            own[0, tap] = block(0, 0)
            own[1, tap] = block(0, 1)


def weight_terms(norm, acts, cot):
    rows, width, depth, chan = acts[0].shape
    q = chan // QUAD
    cells = QUAD * rows * width * depth
    shapes = []
    for taps in (XTAPS, 27 - XTAPS):
        shape = (taps, q // RING // 2, chan)
        shapes += [jax.ShapeDtypeStruct((2,) + shape, BF16)] * 2
        shapes += [jax.ShapeDtypeStruct(shape, F32)] * 2
        shapes += [jax.ShapeDtypeStruct((2,) + shape, F32)]
    return pl.pallas_call(
        functools.partial(weight_kernel, norm),
        out_shape=shapes,
        in_specs=[ANY] * 4 + [VMEM],
        out_specs=[VMEM] * 10,
        scratch_shapes=[
            pltpu.VMEM((QUAD * rows, width, depth, chan), BF16),
            pltpu.SemaphoreType.DMA((4,)),
        ],
        compiler_params=params(),
        cost_estimate=pl.CostEstimate(
            flops=2 * 27 * q * cells * chan, bytes_accessed=10_000_000, transcendentals=0
        ),
    )(*acts, cot)


def input_kernel(held, own, above, across_low, across_high, below, *refs):
    send, keep, pass_on, weights, sem = refs
    j = quad_place()
    y = y_place()
    part = own.shape[1]
    low = across_low.shape[0]

    def at(s):
        return pl.ds(pl.multiple_of(lax.rem(y + s, RING) * part, part), part)

    pairs = [
        (own, weights.at[:, at(0)]),
        (above, weights.at[:, at(1)]),
        (across_low, weights.at[pl.ds(0, low), at(2)]),
        (across_high, weights.at[pl.ds(low, 27 - low), at(2)]),
        (below, weights.at[:, at(3)]),
    ]
    for c in run_copies(pairs, sem):
        c.wait()
    rows, width, depth, chan = keep.shape
    cells = rows * width * depth
    q = held.shape[3]
    taps = weights[...].reshape(9, 3, q, chan)
    for k, out in ((1, send.at[0]), (3, send.at[1]), (2, pass_on), (0, keep)):
        first = (j ^ k) * rows
        moved = []
        for n in range(9):
            a, b = n // 3 - 1, n % 3 - 1
            block = held[pl.ds(first + 1 - a, rows), 1 - b:1 - b + width]
            moved.append(block.reshape(cells, q))
        moved = jnp.concatenate(moved, axis=1)
        z = lax.rem(lax.broadcasted_iota(jnp.int32, (cells, chan), 0), depth)

        def term(c):
            return jnp.dot(moved, taps[:, c].reshape(9 * q, chan), preferred_element_type=F32)

        grad = term(1)
        grad = grad + zero_at(pltpu.roll(term(0), cells - 1, 0), z, depth - 1)
        grad = grad + zero_at(pltpu.roll(term(2), 1, 0), z, 0)
        out[...] = grad.reshape(rows, width, depth, chan)


def input_terms(held, parts):
    tall, width, depth, q = held.shape
    chan = QUAD * q
    block = ((tall - 2) // QUAD, width - 2, depth, chan)
    return pl.pallas_call(
        input_kernel,
        out_shape=[
            jax.ShapeDtypeStruct((2,) + block, F32),
            jax.ShapeDtypeStruct(block, F32),
            jax.ShapeDtypeStruct(block, F32),
        ],
        in_specs=[VMEM] + [ANY] * 5,
        out_specs=[VMEM] * 3,
        scratch_shapes=[pltpu.VMEM((27, q, chan), BF16), pltpu.SemaphoreType.DMA((5,))],
        compiler_params=params(),
        cost_estimate=pl.CostEstimate(
            flops=2 * 27 * tall * width * depth * q * chan, bytes_accessed=10_000_000, transcendentals=0
        ),
    )(held, *parts)


def finish_kernel(pre, keep, near, far, out):
    value = pre[...].astype(F32)
    s = jax.nn.sigmoid(value)
    grad = keep[...] + near[0] + far[...]
    out[...] = (grad * s * (1.0 + value * (1.0 - s))).astype(BF16)


def finish(pre_act, keep, near, far):
    return pl.pallas_call(
        finish_kernel,
        out_shape=jax.ShapeDtypeStruct(pre_act.shape, BF16),
        in_specs=[VMEM] * 4,
        out_specs=VMEM,
        compiler_params=params(),
    )(pre_act, keep, near, far)


def next_kernel(*refs):
    for n, out in enumerate(refs[8:]):
        came, keep = refs[2 * n:2 * n + 2]
        out[...] = (came[0].astype(F32) + keep[...]).astype(BF16)


def next_step(*parts):
    keeps = parts[1::2]
    return pl.pallas_call(
        next_kernel,
        out_shape=[jax.ShapeDtypeStruct(k.shape, BF16) for k in keeps],
        in_specs=[VMEM] * 8,
        out_specs=[VMEM] * 4,
        compiler_params=params(),
    )(*parts)


def split_kernel(*refs):
    for group in range(2):
        own, from_low, from_high, last_low, last_high = refs[5 * group:5 * group + 5]
        outs = refs[10 + 4 * group:14 + 4 * group]
        size = own.shape[2] // 2
        low = own[0] + from_high[1].astype(F32) + last_low[...].astype(F32)
        high = own[1] + from_low[1].astype(F32) + last_high[...].astype(F32)
        blocks = (low[:, :size], low[:, size:], high[:, :size], high[:, size:])
        for block, out in zip(blocks, outs):
            out[...] = block.astype(out.dtype)


def split(*parts):
    shapes = []
    for own in parts[::5]:
        _, taps, rows, chan = own.shape
        shape = (taps, rows // 2, chan)
        shapes += [jax.ShapeDtypeStruct(shape, F32)] + [jax.ShapeDtypeStruct(shape, BF16)] * 3
    return pl.pallas_call(
        split_kernel,
        out_shape=shapes,
        in_specs=[VMEM] * 10,
        out_specs=[VMEM] * 8,
        compiler_params=params(),
    )(*parts)


def join_kernel(*refs):
    out = refs[-1]
    x = x_place()
    size = refs[0].shape[1]
    low = refs[0].shape[0]
    for piece, part, k in zip(refs, (0, 1) * RING, (0, 0, 3, 3, 1, 1, 2, 2)):
        at = pl.ds(pl.multiple_of(lax.rem(x + k, RING) * size, size), size)
        first = part * low
        out[first:first + piece.shape[0], at] = piece[...]


def gather_x(low, high):
    low_below, high_above = along_x(low, 1), along_x(high, -1)
    high_below, low_above = along_x(high, 1), along_x(low, -1)
    low_far, high_far = along_x(low_below, 1), along_x(high_above, -1)
    _, size, chan = low.shape
    pieces = (low, high, low_below, high_below, low_above, high_above, low_far, high_far)
    return pl.pallas_call(
        join_kernel,
        out_shape=jax.ShapeDtypeStruct((27, RING * size, chan), F32),
        in_specs=[VMEM] * 8,
        out_specs=VMEM,
        compiler_params=params(),
    )(*pieces)


def body(pre_act, cot, weight):
    rows, width, depth, chan = pre_act.shape
    norm = 1.0 / math.sqrt(rows * lax.axis_size("gy") * width * lax.axis_size("gx") * depth)
    j = quad_place()
    barrier = lax.optimization_barrier

    count = lax.axis_size("gy")
    pairs = [(g, g + 1) for g in range(QUAD - 1, count - 1, QUAD)]
    pairs = pairs + [(t, s) for s, t in pairs]
    act, edge = start(pre_act, cot)
    extra = lax.ppermute(edge, "gy", pairs)
    far = swap(act, 2)
    near = swap(act, 1)
    extra, near, weight = barrier((extra, near, weight))
    above = along_y(weight, -1, True)
    below = along_y(weight, 1, True)
    quarters = pick_channels(cot, extra)
    quarters = [quarters[0]] + [swap(quarters[k], k) for k in (1, 2, 3)]
    quarters, far = barrier((quarters, far))
    acts = [act, near, far, swap(far, 1)]
    even, odd = sides(quarters)
    even, odd = swap_x(even, 0), swap_x(odd, 1)
    even, odd, above, below = barrier((even, odd, above, below))
    taps = XTAPS
    parts = [weight, above, along_y(below[:taps], 1, True), along_y(above[taps:], -1, True), below]
    held, turned = turn(quarters, even, odd)

    terms = weight_terms(norm, acts, turned)
    held, terms = barrier((held, terms))
    xup, xdown, xkeep_up, xkeep_down, xown = terms[:5]
    yup, ydown, ykeep_up, ykeep_down, yown = terms[5:]
    xlow, xhigh = along_x(xup, 1), along_x(xdown, -1)
    ylow, yhigh = along_y(yup, 1, True), along_y(ydown, -1, True)
    grads = input_terms(held, parts)
    grads, xlow, xhigh, ylow, yhigh = barrier((grads, xlow, xhigh, ylow, yhigh))
    send, keep, pass_on = grads
    got = swap(send, 1)
    xup, xdown, yup, ydown = next_step(
        xlow, xkeep_up, xhigh, xkeep_down, ylow, ykeep_up, yhigh, ykeep_down
    )
    xlast = along_x(xup, 1), along_x(xdown, -1)
    ylast = along_y(yup, 1, True), along_y(ydown, -1, True)
    xlast, ylast, got = barrier((xlast, ylast, got))
    blocks = split(xown, xlow, xhigh, *xlast, yown, ylow, yhigh, *ylast)

    low, high = blocks[0], blocks[4]
    lows = [along_y(block, r, True) for r, block in zip((1, 2, 3), blocks[1:4])]
    highs = [along_x(block, r) for r, block in zip((1, 2, 3), blocks[5:])]
    for other in lows:
        low = low + other.astype(F32)
    for other in highs:
        high = high + other.astype(F32)
    count = lax.axis_size("gx")
    mine = jnp.concatenate([low.astype(BF16), high.astype(BF16)])
    other = lax.ppermute(mine, "gx", [(g, g ^ 1) for g in range(count)])
    other, passed = barrier((other, pass_on + got[1]))
    far_grad = swap(passed, 2)
    low, high = low + other[:taps].astype(F32), high + other[taps:].astype(F32)
    grad_weight = gather_x(low, high)
    grad_pre = finish(pre_act, keep, got, far_grad)
    return (grad_pre, grad_weight)


def solution(mesh):
    return jax.shard_map(
        body,
        mesh=mesh,
        in_specs=(P("gy", "gx", None, None), P("gy", "gx", None, None), P(None, "gy", None)),
        out_specs=(P("gy", "gx", None, None), P(None, "gy", None)),
        check_vma=False,
    )
```

```python
import functools
import math

import jax
import jax.numpy as jnp
from jax import lax
from jax.experimental import pallas as pl
from jax.experimental.pallas import tpu as pltpu
from jax.sharding import PartitionSpec as P

QUAD = 4
RING = 4
XTAPS = 13
F32 = jnp.float32
BF16 = jnp.bfloat16
ANY = pl.BlockSpec(memory_space=pl.ANY)
VMEM = pl.BlockSpec(memory_space=pltpu.VMEM)
LIMIT = 24 * 1024 * 1024


def params():
    return pltpu.CompilerParams(vmem_limit_bytes=LIMIT)


def small_cost():
    return pl.CostEstimate(flops=1000, bytes_accessed=1000, transcendentals=0)


def quad_place():
    return lax.rem(lax.axis_index("gy"), QUAD)


def x_place():
    return lax.div(lax.axis_index("gx"), 2)


def y_place():
    return lax.div(lax.axis_index("gy"), QUAD)


def swap(block, k):
    count = lax.axis_size("gy")
    return lax.ppermute(block, "gy", [(g, g ^ k) for g in range(count)])


def along_y(block, step, ring):
    count = lax.axis_size("gy")
    pairs = [(g, g + QUAD * step) for g in range(count)]
    if ring:
        pairs = [(s, t % count) for s, t in pairs]
    return lax.ppermute(block, "gy", [(s, t) for s, t in pairs if 0 <= t < count])


def along_x(block, step):
    count = lax.axis_size("gx")
    return lax.ppermute(block, "gx", [(g, (g + 2 * step) % count) for g in range(count)])


def swap_x(block, first):
    count = lax.axis_size("gx")
    pairs = [(g, g + 1) for g in range(first, count - 1, 2)]
    return lax.ppermute(block, "gx", pairs + [(t, s) for s, t in pairs])


def zero_at(value, z, edge):
    return jnp.where(z == edge, 0.0, value)


def pick_kernel(cot, extra, *quarters):
    rows, _, _, chan = cot.shape
    j = quad_place()
    q = chan // QUAD
    part = q // RING
    source = lax.broadcasted_iota(jnp.int32, (chan, q), 0)
    place = lax.broadcasted_iota(jnp.int32, (chan, q), 1)
    base = lax.div(place, part) * q + lax.rem(place, part)

    def take(block, pick):
        got = jnp.dot(block.reshape(-1, chan), pick, preferred_element_type=F32)
        return got.astype(BF16).reshape(block.shape[:-1] + (q,))

    for k, out in enumerate(quarters):
        pick = jnp.where(source == base + (j ^ k) * part, 1.0, 0.0).astype(BF16)
        out[0:rows] = take(cot[...], pick)
        out[rows] = take(extra[...], pick)


def pick_channels(cot, extra):
    rows, width, depth, chan = cot.shape
    quarter = jax.ShapeDtypeStruct((rows + 1, width, depth, chan // QUAD), BF16)
    return pl.pallas_call(
        pick_kernel,
        out_shape=[quarter] * QUAD,
        in_specs=[VMEM] * 2,
        out_specs=[VMEM] * QUAD,
        compiler_params=params(),
        cost_estimate=small_cost(),
    )(cot, extra)


def side_kernel(p0, p1, p2, p3, even, odd):
    width = p0.shape[1]
    is_odd = lax.rem(lax.axis_index("gx"), 2) == 1
    for k, p in enumerate((p0, p1, p2, p3)):
        first, last = p[:, 0], p[:, width - 1]
        even[k] = jnp.where(is_odd, first, last)
        odd[k] = jnp.where(is_odd, last, first)


def sides(quarters):
    rows, _, depth, q = quarters[0].shape
    return pl.pallas_call(
        side_kernel,
        out_shape=[jax.ShapeDtypeStruct((QUAD, rows, depth, q), BF16)] * 2,
        in_specs=[VMEM] * QUAD,
        out_specs=[VMEM] * 2,
        compiler_params=params(),
        cost_estimate=small_cost(),
    )(*quarters)


def turn_kernel(p0, p1, p2, p3, even, odd, held, out):
    j, x = quad_place(), x_place()
    is_odd = lax.rem(lax.axis_index("gx"), 2) == 1
    for k, p in enumerate((p0, p1, p2, p3)):
        rows, width = p.shape[0] - 1, p.shape[1]
        low = jnp.where(is_odd, even[k], odd[k])
        high = jnp.where(is_odd, odd[k], even[k])

        def put(at, part):
            held[at, 1:width + 1] = p[part]
            held[at, 0] = low[part]
            held[at, width + 1] = high[part]

        put(pl.ds(1 + (j ^ k) * rows, rows), slice(0, rows))
        pl.when((j ^ k) == 0)(functools.partial(put, 0, rows))
        pl.when((j ^ k) == QUAD - 1)(functools.partial(put, held.shape[0] - 1, rows))

    tall, width, depth, q = held.shape
    width -= 2
    cells = tall * width * depth
    part = q // RING
    small = part // RING
    place = lax.broadcasted_iota(jnp.int32, (q, q), 0)
    source = lax.broadcasted_iota(jnp.int32, (q, q), 1)
    xpart = lax.rem(lax.div(place, part) + x, RING)
    ypart = lax.rem(lax.div(lax.rem(place, part), small) + y_place(), RING)
    base = ypart * part + xpart * small + lax.rem(place, small)
    order = jnp.where(source == base, 1.0, 0.0).astype(BF16)
    z = lax.rem(lax.broadcasted_iota(jnp.int32, (q, cells), 1), depth)
    for b in (-1, 0, 1):
        moved = held[:, 1 - b:1 - b + width].reshape(cells, q)
        value = lax.dot_general(
            order, moved, (((1,), (1,)), ((), ())), preferred_element_type=F32
        )
        high = zero_at(pltpu.roll(value, cells - 1, 1), z, depth - 1)
        low = zero_at(pltpu.roll(value, 1, 1), z, 0)
        for c, v in enumerate((high, value, low)):
            at = ((b + 1) * 3 + c) * q
            out[at:at + q] = v.astype(BF16)


def turn(quarters, even, odd):
    rows, width, depth, q = quarters[0].shape
    width += 2
    tall = QUAD * (rows - 1) + 2
    return pl.pallas_call(
        turn_kernel,
        out_shape=[
            jax.ShapeDtypeStruct((tall, width, depth, q), BF16),
            jax.ShapeDtypeStruct((9 * q, tall * (width - 2) * depth), BF16),
        ],
        in_specs=[VMEM] * (QUAD + 2),
        out_specs=[VMEM] * 2,
        compiler_params=params(),
        cost_estimate=small_cost(),
    )(*quarters, even, odd)


def run_copies(pairs, sem):
    copies = [pltpu.make_async_copy(s, d, sem.at[n]) for n, (s, d) in enumerate(pairs)]
    for c in copies:
        c.start()
    return copies


def weight_kernel(norm, own_act, near, far, across, cot, *refs):
    groups, held, sem = (refs[:5], refs[5:10]), *refs[10:]
    j = quad_place()
    rows, width, depth, chan = own_act.shape
    pairs = []
    for k, piece in enumerate((own_act, near, far, across)):
        pairs.append((piece, held.at[pl.ds((j ^ k) * rows, rows)]))
    for c in run_copies(pairs, sem):
        c.wait()
    row = width * depth
    cells = QUAD * rows * row
    act = held[...].reshape(cells, chan)
    q = cot.shape[0] // 9
    small = q // RING // RING
    for n in range(9):
        a, b = n // 3 - 1, n % 3
        moved = cot[3 * b * q:3 * (b + 1) * q, (1 - a) * row:(1 - a) * row + cells]
        term = jnp.dot(moved, act, preferred_element_type=F32) * norm
        for c in range(3):
            tap = 3 * n + c
            by_y = tap >= XTAPS
            up, down, keep_up, keep_down, own = groups[by_y]
            tap -= XTAPS * by_y

            def block(r, h):
                spots = [(2 * h, r), (2 * h + 1, r)] if by_y else [(r, 2 * h), (r, 2 * h + 1)]
                starts = [c * q + (xr * RING + yr) * small for xr, yr in spots]
                return jnp.concatenate([term[at:at + small] for at in starts], axis=0)

            up[0, tap] = block(2, 0).astype(BF16)
            down[0, tap] = block(2, 1).astype(BF16)
            keep_up[tap] = block(1, 0)
            up[1, tap] = block(1, 1).astype(BF16)
            down[1, tap] = block(3, 0).astype(BF16)
            keep_down[tap] = block(3, 1)
            own[0, tap] = block(0, 0)
            own[1, tap] = block(0, 1)


def weight_terms(norm, acts, cot):
    rows, width, depth, chan = acts[0].shape
    q = chan // QUAD
    cells = QUAD * rows * width * depth
    shapes = []
    for taps in (XTAPS, 27 - XTAPS):
        shape = (taps, q // RING // 2, chan)
        shapes += [jax.ShapeDtypeStruct((2,) + shape, BF16)] * 2
        shapes += [jax.ShapeDtypeStruct(shape, F32)] * 2
        shapes += [jax.ShapeDtypeStruct((2,) + shape, F32)]
    return pl.pallas_call(
        functools.partial(weight_kernel, norm),
        out_shape=shapes,
        in_specs=[ANY] * 4 + [VMEM],
        out_specs=[VMEM] * 10,
        scratch_shapes=[
            pltpu.VMEM((QUAD * rows, width, depth, chan), BF16),
            pltpu.SemaphoreType.DMA((4,)),
        ],
        compiler_params=params(),
        cost_estimate=pl.CostEstimate(
            flops=2 * 27 * q * cells * chan, bytes_accessed=10_000_000, transcendentals=0
        ),
    )(*acts, cot)


def input_kernel(held, own, above, across_low, across_high, below, *refs):
    send, keep, pass_on, weights, sem = refs
    j = quad_place()
    y = y_place()
    part = own.shape[1]
    low = across_low.shape[0]

    def at(s):
        return pl.ds(pl.multiple_of(lax.rem(y + s, RING) * part, part), part)

    pairs = [
        (own, weights.at[:, at(0)]),
        (above, weights.at[:, at(1)]),
        (across_low, weights.at[pl.ds(0, low), at(2)]),
        (across_high, weights.at[pl.ds(low, 27 - low), at(2)]),
        (below, weights.at[:, at(3)]),
    ]
    for c in run_copies(pairs, sem):
        c.wait()
    rows, width, depth, chan = keep.shape
    cells = rows * width * depth
    q = held.shape[3]
    taps = weights[...].reshape(9, 3, q, chan)
    for k, out in ((1, send.at[0]), (3, send.at[1]), (2, pass_on), (0, keep)):
        first = (j ^ k) * rows
        moved = []
        for n in range(9):
            a, b = n // 3 - 1, n % 3 - 1
            block = held[pl.ds(first + 1 - a, rows), 1 - b:1 - b + width]
            moved.append(block.reshape(cells, q))
        moved = jnp.concatenate(moved, axis=1)
        z = lax.rem(lax.broadcasted_iota(jnp.int32, (cells, chan), 0), depth)

        def term(c):
            return jnp.dot(moved, taps[:, c].reshape(9 * q, chan), preferred_element_type=F32)

        grad = term(1)
        grad = grad + zero_at(pltpu.roll(term(0), cells - 1, 0), z, depth - 1)
        grad = grad + zero_at(pltpu.roll(term(2), 1, 0), z, 0)
        out[...] = grad.reshape(rows, width, depth, chan)


def input_terms(held, parts):
    tall, width, depth, q = held.shape
    chan = QUAD * q
    block = ((tall - 2) // QUAD, width - 2, depth, chan)
    return pl.pallas_call(
        input_kernel,
        out_shape=[
            jax.ShapeDtypeStruct((2,) + block, F32),
            jax.ShapeDtypeStruct(block, F32),
            jax.ShapeDtypeStruct(block, F32),
        ],
        in_specs=[VMEM] + [ANY] * 5,
        out_specs=[VMEM] * 3,
        scratch_shapes=[pltpu.VMEM((27, q, chan), BF16), pltpu.SemaphoreType.DMA((5,))],
        compiler_params=params(),
        cost_estimate=pl.CostEstimate(
            flops=2 * 27 * tall * width * depth * q * chan, bytes_accessed=10_000_000, transcendentals=0
        ),
    )(held, *parts)


def finish_kernel(pre, keep, near, far, out):
    value = pre[...].astype(F32)
    s = jax.nn.sigmoid(value)
    grad = keep[...] + near[0] + far[...]
    out[...] = (grad * s * (1.0 + value * (1.0 - s))).astype(BF16)


def finish(pre_act, keep, near, far):
    return pl.pallas_call(
        finish_kernel,
        out_shape=jax.ShapeDtypeStruct(pre_act.shape, BF16),
        in_specs=[VMEM] * 4,
        out_specs=VMEM,
        compiler_params=params(),
    )(pre_act, keep, near, far)


def next_kernel(*refs):
    for n, out in enumerate(refs[8:]):
        came, keep = refs[2 * n:2 * n + 2]
        out[...] = (came[0].astype(F32) + keep[...]).astype(BF16)


def next_step(*parts):
    keeps = parts[1::2]
    return pl.pallas_call(
        next_kernel,
        out_shape=[jax.ShapeDtypeStruct(k.shape, BF16) for k in keeps],
        in_specs=[VMEM] * 8,
        out_specs=[VMEM] * 4,
        compiler_params=params(),
    )(*parts)


def split_kernel(*refs):
    for group in range(2):
        own, from_low, from_high, last_low, last_high = refs[5 * group:5 * group + 5]
        outs = refs[10 + 4 * group:14 + 4 * group]
        size = own.shape[2] // 2
        low = own[0] + from_high[1].astype(F32) + last_low[...].astype(F32)
        high = own[1] + from_low[1].astype(F32) + last_high[...].astype(F32)
        blocks = (low[:, :size], low[:, size:], high[:, :size], high[:, size:])
        for block, out in zip(blocks, outs):
            out[...] = block.astype(out.dtype)


def split(*parts):
    shapes = []
    for own in parts[::5]:
        _, taps, rows, chan = own.shape
        shape = (taps, rows // 2, chan)
        shapes += [jax.ShapeDtypeStruct(shape, F32)] + [jax.ShapeDtypeStruct(shape, BF16)] * 3
    return pl.pallas_call(
        split_kernel,
        out_shape=shapes,
        in_specs=[VMEM] * 10,
        out_specs=[VMEM] * 8,
        compiler_params=params(),
    )(*parts)


def join_kernel(*refs):
    out = refs[-1]
    x = x_place()
    size = refs[0].shape[1]
    low = refs[0].shape[0]
    for piece, part, k in zip(refs, (0, 1) * RING, (0, 0, 3, 3, 1, 1, 2, 2)):
        at = pl.ds(pl.multiple_of(lax.rem(x + k, RING) * size, size), size)
        first = part * low
        out[first:first + piece.shape[0], at] = piece[...]


def gather_x(low, high):
    low_below, high_above = along_x(low, 1), along_x(high, -1)
    high_below, low_above = along_x(high, 1), along_x(low, -1)
    low_far, high_far = along_x(low_below, 1), along_x(high_above, -1)
    _, size, chan = low.shape
    pieces = (low, high, low_below, high_below, low_above, high_above, low_far, high_far)
    return pl.pallas_call(
        join_kernel,
        out_shape=jax.ShapeDtypeStruct((27, RING * size, chan), F32),
        in_specs=[VMEM] * 8,
        out_specs=VMEM,
        compiler_params=params(),
    )(*pieces)


def body(pre_act, cot, weight):
    rows, width, depth, chan = pre_act.shape
    norm = 1.0 / math.sqrt(rows * lax.axis_size("gy") * width * lax.axis_size("gx") * depth)
    j = quad_place()
    barrier = lax.optimization_barrier

    count = lax.axis_size("gy")
    pairs = [(g, g + 1) for g in range(QUAD - 1, count - 1, QUAD)]
    pairs = pairs + [(t, s) for s, t in pairs]
    extra = lax.ppermute(jnp.where(j == 0, cot[0], cot[rows - 1]), "gy", pairs)
    act = jax.nn.silu(pre_act.astype(F32)).astype(BF16)
    near = swap(act, 1)
    extra, near, weight = barrier((extra, near, weight))
    above = along_y(weight, -1, True)
    below = along_y(weight, 1, True)
    quarters = pick_channels(cot, extra)
    quarters = [quarters[0]] + [swap(quarters[k], k) for k in (1, 2, 3)]
    quarters, act = barrier((quarters, act))
    far = swap(act, 2)
    even, odd = sides(quarters)
    even, odd = swap_x(even, 0), swap_x(odd, 1)
    even, odd, above, below, far = barrier((even, odd, above, below, far))
    acts = [act, near, far, swap(far, 1)]
    taps = XTAPS
    parts = [weight, above, along_y(below[:taps], 1, True), along_y(above[taps:], -1, True), below]
    held, turned = turn(quarters, even, odd)

    terms = weight_terms(norm, acts, turned)
    held, terms = barrier((held, terms))
    xup, xdown, xkeep_up, xkeep_down, xown = terms[:5]
    yup, ydown, ykeep_up, ykeep_down, yown = terms[5:]
    xlow, xhigh = along_x(xup, 1), along_x(xdown, -1)
    ylow, yhigh = along_y(yup, 1, True), along_y(ydown, -1, True)
    grads = input_terms(held, parts)
    grads, xlow, xhigh, ylow, yhigh = barrier((grads, xlow, xhigh, ylow, yhigh))
    send, keep, pass_on = grads
    got = swap(send, 1)
    xup, xdown, yup, ydown = next_step(
        xlow, xkeep_up, xhigh, xkeep_down, ylow, ykeep_up, yhigh, ykeep_down
    )
    xlast = along_x(xup, 1), along_x(xdown, -1)
    ylast = along_y(yup, 1, True), along_y(ydown, -1, True)
    xlast, ylast, got = barrier((xlast, ylast, got))
    blocks = split(xown, xlow, xhigh, *xlast, yown, ylow, yhigh, *ylast)

    low, high = blocks[0], blocks[4]
    lows = [along_y(block, r, True) for r, block in zip((1, 2, 3), blocks[1:4])]
    highs = [along_x(block, r) for r, block in zip((1, 2, 3), blocks[5:])]
    for other in lows:
        low = low + other.astype(F32)
    for other in highs:
        high = high + other.astype(F32)
    count = lax.axis_size("gx")
    mine = jnp.concatenate([low.astype(BF16), high.astype(BF16)])
    other = lax.ppermute(mine, "gx", [(g, g ^ 1) for g in range(count)])
    other, passed = barrier((other, pass_on + got[1]))
    far_grad = swap(passed, 2)
    low, high = low + other[:taps].astype(F32), high + other[taps:].astype(F32)
    grad_weight = gather_x(low, high)
    grad_pre = finish(pre_act, keep, got, far_grad)
    return (grad_pre, grad_weight)


def solution(mesh):
    return jax.shard_map(
        body,
        mesh=mesh,
        in_specs=(P("gy", "gx", None, None), P("gy", "gx", None, None), P(None, "gy", None)),
        out_specs=(P("gy", "gx", None, None), P(None, "gy", None)),
        check_vma=False,
    )
```

```python
import functools
import math

import jax
import jax.numpy as jnp
from jax import lax
from jax.experimental import pallas as pl
from jax.experimental.pallas import tpu as pltpu
from jax.sharding import PartitionSpec as P

QUAD = 4
RING = 4
XTAPS = 13
F32 = jnp.float32
BF16 = jnp.bfloat16
ANY = pl.BlockSpec(memory_space=pl.ANY)
VMEM = pl.BlockSpec(memory_space=pltpu.VMEM)
LIMIT = 24 * 1024 * 1024


def params():
    return pltpu.CompilerParams(vmem_limit_bytes=LIMIT)


def small_cost():
    return pl.CostEstimate(flops=1000, bytes_accessed=1000, transcendentals=0)


def quad_place():
    return lax.rem(lax.axis_index("gy"), QUAD)


def x_place():
    return lax.div(lax.axis_index("gx"), 2)


def y_place():
    return lax.div(lax.axis_index("gy"), QUAD)


def swap(block, k):
    count = lax.axis_size("gy")
    return lax.ppermute(block, "gy", [(g, g ^ k) for g in range(count)])


def along_y(block, step, ring):
    count = lax.axis_size("gy")
    pairs = [(g, g + QUAD * step) for g in range(count)]
    if ring:
        pairs = [(s, t % count) for s, t in pairs]
    return lax.ppermute(block, "gy", [(s, t) for s, t in pairs if 0 <= t < count])


def along_x(block, step):
    count = lax.axis_size("gx")
    return lax.ppermute(block, "gx", [(g, (g + 2 * step) % count) for g in range(count)])


def swap_x(block, first):
    count = lax.axis_size("gx")
    pairs = [(g, g + 1) for g in range(first, count - 1, 2)]
    return lax.ppermute(block, "gx", pairs + [(t, s) for s, t in pairs])


def swap_y(block, first):
    count = lax.axis_size("gy")
    pairs = [(g, g + QUAD) for g in range(count - QUAD) if (g // QUAD - first) % 2 == 0]
    return lax.ppermute(block, "gy", pairs + [(t, s) for s, t in pairs])


def zero_at(value, z, edge):
    return jnp.where(z == edge, 0.0, value)


def pick_kernel(cot, *quarters):
    chan = cot.shape[3]
    j = quad_place()
    q = chan // QUAD
    part = q // RING
    source = lax.broadcasted_iota(jnp.int32, (chan, q), 0)
    place = lax.broadcasted_iota(jnp.int32, (chan, q), 1)
    base = lax.div(place, part) * q + lax.rem(place, part)
    flat = cot[...].reshape(-1, chan)
    for k, out in enumerate(quarters):
        pick = jnp.where(source == base + (j ^ k) * part, 1.0, 0.0).astype(BF16)
        got = jnp.dot(flat, pick, preferred_element_type=F32)
        out[...] = got.astype(BF16).reshape(out.shape)


def pick_channels(cot):
    rows, width, depth, chan = cot.shape
    quarter = jax.ShapeDtypeStruct((rows, width, depth, chan // QUAD), BF16)
    return pl.pallas_call(
        pick_kernel,
        out_shape=[quarter] * QUAD,
        in_specs=[VMEM],
        out_specs=[VMEM] * QUAD,
        compiler_params=params(),
        cost_estimate=small_cost(),
    )(cot)


def side_kernel(p0, p1, p2, p3, even, odd):
    width = p0.shape[1]
    is_odd = lax.rem(lax.axis_index("gx"), 2) == 1
    for k, p in enumerate((p0, p1, p2, p3)):
        first, last = p[:, 0], p[:, width - 1]
        even[k] = jnp.where(is_odd, first, last)
        odd[k] = jnp.where(is_odd, last, first)


def sides(quarters):
    rows, _, depth, q = quarters[0].shape
    return pl.pallas_call(
        side_kernel,
        out_shape=[jax.ShapeDtypeStruct((QUAD, rows, depth, q), BF16)] * 2,
        in_specs=[VMEM] * QUAD,
        out_specs=[VMEM] * 2,
        compiler_params=params(),
        cost_estimate=small_cost(),
    )(*quarters)


def rim_of(even, odd, k):
    is_odd = lax.rem(lax.axis_index("gx"), 2) == 1
    return jnp.where(is_odd, even[k], odd[k]), jnp.where(is_odd, odd[k], even[k])


def edge_kernel(p0, p1, p2, p3, even, odd, first, second):
    j = quad_place()
    is_odd = lax.rem(y_place(), 2) == 1
    rows, width = p0.shape[:2]

    def put(out, p, k, row):
        low, high = rim_of(even, odd, k)
        out[1:width + 1] = p[row]
        out[0] = low[row]
        out[width + 1] = high[row]

    for k, p in enumerate((p0, p1, p2, p3)):
        is_top, is_bottom = (j ^ k) == QUAD - 1, (j ^ k) == 0
        not_odd = jnp.logical_not(is_odd)
        pl.when(is_top & not_odd)(functools.partial(put, first, p, k, rows - 1))
        pl.when(is_top & is_odd)(functools.partial(put, second, p, k, rows - 1))
        pl.when(is_bottom & not_odd)(functools.partial(put, second, p, k, 0))
        pl.when(is_bottom & is_odd)(functools.partial(put, first, p, k, 0))


def edge_rows(quarters, even, odd):
    _, width, depth, q = quarters[0].shape
    return pl.pallas_call(
        edge_kernel,
        out_shape=[jax.ShapeDtypeStruct((width + 2, depth, q), BF16)] * 2,
        in_specs=[VMEM] * (QUAD + 2),
        out_specs=[VMEM] * 2,
        compiler_params=params(),
        cost_estimate=small_cost(),
    )(*quarters, even, odd)


def turn_kernel(p0, p1, p2, p3, even, odd, first, second, held, out):
    j, x = quad_place(), x_place()
    is_odd = lax.rem(y_place(), 2) == 1
    held[0] = jnp.where(is_odd, first[...], second[...])
    held[held.shape[0] - 1] = jnp.where(is_odd, second[...], first[...])
    for k, p in enumerate((p0, p1, p2, p3)):
        rows, width = p.shape[:2]
        low, high = rim_of(even, odd, k)
        at = pl.ds(1 + (j ^ k) * rows, rows)
        held[at, 1:width + 1] = p[...]
        held[at, 0] = low
        held[at, width + 1] = high

    tall, width, depth, q = held.shape
    width -= 2
    cells = tall * width * depth
    part = q // RING
    small = part // RING
    place = lax.broadcasted_iota(jnp.int32, (q, q), 0)
    source = lax.broadcasted_iota(jnp.int32, (q, q), 1)
    xpart = lax.rem(lax.div(place, part) + x, RING)
    ypart = lax.rem(lax.div(lax.rem(place, part), small) + y_place(), RING)
    base = ypart * part + xpart * small + lax.rem(place, small)
    order = jnp.where(source == base, 1.0, 0.0).astype(BF16)
    z = lax.rem(lax.broadcasted_iota(jnp.int32, (q, cells), 1), depth)
    for b in (-1, 0, 1):
        moved = held[:, 1 - b:1 - b + width].reshape(cells, q)
        value = lax.dot_general(
            order, moved, (((1,), (1,)), ((), ())), preferred_element_type=F32
        )
        high = zero_at(pltpu.roll(value, cells - 1, 1), z, depth - 1)
        low = zero_at(pltpu.roll(value, 1, 1), z, 0)
        for c, v in enumerate((high, value, low)):
            at = ((b + 1) * 3 + c) * q
            out[at:at + q] = v.astype(BF16)


def turn(quarters, *rims):
    rows, width, depth, q = quarters[0].shape
    width += 2
    tall = QUAD * rows + 2
    return pl.pallas_call(
        turn_kernel,
        out_shape=[
            jax.ShapeDtypeStruct((tall, width, depth, q), BF16),
            jax.ShapeDtypeStruct((9 * q, tall * (width - 2) * depth), BF16),
        ],
        in_specs=[VMEM] * (QUAD + 4),
        out_specs=[VMEM] * 2,
        compiler_params=params(),
        cost_estimate=small_cost(),
    )(*quarters, *rims)


def run_copies(pairs, sem):
    copies = [pltpu.make_async_copy(s, d, sem.at[n]) for n, (s, d) in enumerate(pairs)]
    for c in copies:
        c.start()
    return copies


def weight_kernel(norm, own_act, near, far, across, cot, *refs):
    groups, held, sem = (refs[:5], refs[5:10]), *refs[10:]
    j = quad_place()
    rows, width, depth, chan = own_act.shape
    pairs = []
    for k, piece in enumerate((own_act, near, far, across)):
        pairs.append((piece, held.at[pl.ds((j ^ k) * rows, rows)]))
    for c in run_copies(pairs, sem):
        c.wait()
    row = width * depth
    cells = QUAD * rows * row
    act = held[...].reshape(cells, chan)
    q = cot.shape[0] // 9
    small = q // RING // RING
    for n in range(9):
        a, b = n // 3 - 1, n % 3
        moved = cot[3 * b * q:3 * (b + 1) * q, (1 - a) * row:(1 - a) * row + cells]
        term = jnp.dot(moved, act, preferred_element_type=F32) * norm
        for c in range(3):
            tap = 3 * n + c
            by_y = tap >= XTAPS
            up, down, keep_up, keep_down, own = groups[by_y]
            tap -= XTAPS * by_y

            def block(r, h):
                spots = [(2 * h, r), (2 * h + 1, r)] if by_y else [(r, 2 * h), (r, 2 * h + 1)]
                starts = [c * q + (xr * RING + yr) * small for xr, yr in spots]
                return jnp.concatenate([term[at:at + small] for at in starts], axis=0)

            up[0, tap] = block(2, 0).astype(BF16)
            down[0, tap] = block(2, 1).astype(BF16)
            keep_up[tap] = block(1, 0)
            up[1, tap] = block(1, 1).astype(BF16)
            down[1, tap] = block(3, 0).astype(BF16)
            keep_down[tap] = block(3, 1)
            own[0, tap] = block(0, 0)
            own[1, tap] = block(0, 1)


def weight_terms(norm, acts, cot):
    rows, width, depth, chan = acts[0].shape
    q = chan // QUAD
    cells = QUAD * rows * width * depth
    shapes = []
    for taps in (XTAPS, 27 - XTAPS):
        shape = (taps, q // RING // 2, chan)
        shapes += [jax.ShapeDtypeStruct((2,) + shape, BF16)] * 2
        shapes += [jax.ShapeDtypeStruct(shape, F32)] * 2
        shapes += [jax.ShapeDtypeStruct((2,) + shape, F32)]
    return pl.pallas_call(
        functools.partial(weight_kernel, norm),
        out_shape=shapes,
        in_specs=[ANY] * 4 + [VMEM],
        out_specs=[VMEM] * 10,
        scratch_shapes=[
            pltpu.VMEM((QUAD * rows, width, depth, chan), BF16),
            pltpu.SemaphoreType.DMA((4,)),
        ],
        compiler_params=params(),
        cost_estimate=pl.CostEstimate(
            flops=2 * 27 * q * cells * chan, bytes_accessed=10_000_000, transcendentals=0
        ),
    )(*acts, cot)


def input_kernel(held, own, above, across_low, across_high, below, *refs):
    send, keep, pass_on, weights, sem = refs
    j = quad_place()
    y = y_place()
    part = own.shape[1]
    low = across_low.shape[0]

    def at(s):
        return pl.ds(pl.multiple_of(lax.rem(y + s, RING) * part, part), part)

    pairs = [
        (own, weights.at[:, at(0)]),
        (above, weights.at[:, at(1)]),
        (across_low, weights.at[pl.ds(0, low), at(2)]),
        (across_high, weights.at[pl.ds(low, 27 - low), at(2)]),
        (below, weights.at[:, at(3)]),
    ]
    for c in run_copies(pairs, sem):
        c.wait()
    rows, width, depth, chan = keep.shape
    cells = rows * width * depth
    q = held.shape[3]
    taps = weights[...].reshape(9, 3, q, chan)
    for k, out in ((1, send.at[0]), (3, send.at[1]), (2, pass_on), (0, keep)):
        first = (j ^ k) * rows
        moved = []
        for n in range(9):
            a, b = n // 3 - 1, n % 3 - 1
            block = held[pl.ds(first + 1 - a, rows), 1 - b:1 - b + width]
            moved.append(block.reshape(cells, q))
        moved = jnp.concatenate(moved, axis=1)
        z = lax.rem(lax.broadcasted_iota(jnp.int32, (cells, chan), 0), depth)

        def term(c):
            return jnp.dot(moved, taps[:, c].reshape(9 * q, chan), preferred_element_type=F32)

        grad = term(1)
        grad = grad + zero_at(pltpu.roll(term(0), cells - 1, 0), z, depth - 1)
        grad = grad + zero_at(pltpu.roll(term(2), 1, 0), z, 0)
        out[...] = grad.reshape(rows, width, depth, chan)


def input_terms(held, parts):
    tall, width, depth, q = held.shape
    chan = QUAD * q
    block = ((tall - 2) // QUAD, width - 2, depth, chan)
    return pl.pallas_call(
        input_kernel,
        out_shape=[
            jax.ShapeDtypeStruct((2,) + block, F32),
            jax.ShapeDtypeStruct(block, F32),
            jax.ShapeDtypeStruct(block, F32),
        ],
        in_specs=[VMEM] + [ANY] * 5,
        out_specs=[VMEM] * 3,
        scratch_shapes=[pltpu.VMEM((27, q, chan), BF16), pltpu.SemaphoreType.DMA((5,))],
        compiler_params=params(),
        cost_estimate=pl.CostEstimate(
            flops=2 * 27 * tall * width * depth * q * chan, bytes_accessed=10_000_000, transcendentals=0
        ),
    )(held, *parts)


def finish_kernel(pre, keep, near, far, out):
    value = pre[...].astype(F32)
    s = jax.nn.sigmoid(value)
    grad = keep[...] + near[0] + far[...]
    out[...] = (grad * s * (1.0 + value * (1.0 - s))).astype(BF16)


def finish(pre_act, keep, near, far):
    return pl.pallas_call(
        finish_kernel,
        out_shape=jax.ShapeDtypeStruct(pre_act.shape, BF16),
        in_specs=[VMEM] * 4,
        out_specs=VMEM,
        compiler_params=params(),
    )(pre_act, keep, near, far)


def next_kernel(*refs):
    for n, out in enumerate(refs[8:]):
        came, keep = refs[2 * n:2 * n + 2]
        out[...] = (came[0].astype(F32) + keep[...]).astype(BF16)


def next_step(*parts):
    keeps = parts[1::2]
    return pl.pallas_call(
        next_kernel,
        out_shape=[jax.ShapeDtypeStruct(k.shape, BF16) for k in keeps],
        in_specs=[VMEM] * 8,
        out_specs=[VMEM] * 4,
        compiler_params=params(),
    )(*parts)


def split_kernel(*refs):
    for group in range(2):
        own, from_low, from_high, last_low, last_high = refs[5 * group:5 * group + 5]
        outs = refs[10 + 4 * group:14 + 4 * group]
        size = own.shape[2] // 2
        low = own[0] + from_high[1].astype(F32) + last_low[...].astype(F32)
        high = own[1] + from_low[1].astype(F32) + last_high[...].astype(F32)
        blocks = (low[:, :size], low[:, size:], high[:, :size], high[:, size:])
        for block, out in zip(blocks, outs):
            out[...] = block.astype(out.dtype)


def split(*parts):
    shapes = []
    for own in parts[::5]:
        _, taps, rows, chan = own.shape
        shape = (taps, rows // 2, chan)
        shapes += [jax.ShapeDtypeStruct(shape, F32)] + [jax.ShapeDtypeStruct(shape, BF16)] * 3
    return pl.pallas_call(
        split_kernel,
        out_shape=shapes,
        in_specs=[VMEM] * 10,
        out_specs=[VMEM] * 8,
        compiler_params=params(),
    )(*parts)


def join_kernel(*refs):
    out = refs[-1]
    x = x_place()
    size = refs[0].shape[1]
    low = refs[0].shape[0]
    for piece, part, k in zip(refs, (0, 1) * RING, (0, 0, 3, 3, 1, 1, 2, 2)):
        at = pl.ds(pl.multiple_of(lax.rem(x + k, RING) * size, size), size)
        first = part * low
        out[first:first + piece.shape[0], at] = piece[...]


def gather_x(low, high):
    low_below, high_above = along_x(low, 1), along_x(high, -1)
    high_below, low_above = along_x(high, 1), along_x(low, -1)
    low_far, high_far = along_x(low_below, 1), along_x(high_above, -1)
    _, size, chan = low.shape
    pieces = (low, high, low_below, high_below, low_above, high_above, low_far, high_far)
    return pl.pallas_call(
        join_kernel,
        out_shape=jax.ShapeDtypeStruct((27, RING * size, chan), F32),
        in_specs=[VMEM] * 8,
        out_specs=VMEM,
        compiler_params=params(),
    )(*pieces)


def body(pre_act, cot, weight):
    rows, width, depth, chan = pre_act.shape
    norm = 1.0 / math.sqrt(rows * lax.axis_size("gy") * width * lax.axis_size("gx") * depth)
    barrier = lax.optimization_barrier

    quarters = pick_channels(cot)
    quarters = [quarters[0]] + [swap(quarters[k], k) for k in (1, 2, 3)]
    act = jax.nn.silu(pre_act.astype(F32)).astype(BF16)
    near = swap(act, 1)
    above = along_y(weight, -1, True)
    below = along_y(weight, 1, True)
    even, odd = sides(quarters)
    even, odd, act = barrier((even, odd, act))
    even, odd = swap_x(even, 0), swap_x(odd, 1)
    far = swap(act, 2)
    first, second = edge_rows(quarters, even, odd)
    first, second = swap_y(first, 0), swap_y(second, 1)
    first, second, above, below, far = barrier((first, second, above, below, far))
    acts = [act, near, far, swap(far, 1)]
    taps = XTAPS
    parts = [weight, above, along_y(below[:taps], 1, True), along_y(above[taps:], -1, True), below]
    held, turned = turn(quarters, even, odd, first, second)

    terms = weight_terms(norm, acts, turned)
    held, terms = barrier((held, terms))
    xup, xdown, xkeep_up, xkeep_down, xown = terms[:5]
    yup, ydown, ykeep_up, ykeep_down, yown = terms[5:]
    xlow, xhigh = along_x(xup, 1), along_x(xdown, -1)
    ylow, yhigh = along_y(yup, 1, True), along_y(ydown, -1, True)
    grads = input_terms(held, parts)
    grads, xlow, xhigh, ylow, yhigh = barrier((grads, xlow, xhigh, ylow, yhigh))
    send, keep, pass_on = grads
    got = swap(send, 1)
    xup, xdown, yup, ydown = next_step(
        xlow, xkeep_up, xhigh, xkeep_down, ylow, ykeep_up, yhigh, ykeep_down
    )
    xlast = along_x(xup, 1), along_x(xdown, -1)
    ylast = along_y(yup, 1, True), along_y(ydown, -1, True)
    xlast, ylast, got = barrier((xlast, ylast, got))
    blocks = split(xown, xlow, xhigh, *xlast, yown, ylow, yhigh, *ylast)

    low, high = blocks[0], blocks[4]
    lows = [along_y(block, r, True) for r, block in zip((1, 2, 3), blocks[1:4])]
    highs = [along_x(block, r) for r, block in zip((1, 2, 3), blocks[5:])]
    for other in lows:
        low = low + other.astype(F32)
    for other in highs:
        high = high + other.astype(F32)
    count = lax.axis_size("gx")
    mine = jnp.concatenate([low.astype(BF16), high.astype(BF16)])
    other = lax.ppermute(mine, "gx", [(g, g ^ 1) for g in range(count)])
    other, passed = barrier((other, pass_on + got[1]))
    far_grad = swap(passed, 2)
    low, high = low + other[:taps].astype(F32), high + other[taps:].astype(F32)
    grad_weight = gather_x(low, high)
    grad_pre = finish(pre_act, keep, got, far_grad)
    return (grad_pre, grad_weight)


def solution(mesh):
    return jax.shard_map(
        body,
        mesh=mesh,
        in_specs=(P("gy", "gx", None, None), P("gy", "gx", None, None), P(None, "gy", None)),
        out_specs=(P("gy", "gx", None, None), P(None, "gy", None)),
        check_vma=False,
    )
```

```python
import functools
import math

import jax
import jax.numpy as jnp
from jax import lax
from jax.experimental import pallas as pl
from jax.experimental.pallas import tpu as pltpu
from jax.sharding import PartitionSpec as P

QUAD = 4
RING = 4
XTAPS = 13
F32 = jnp.float32
BF16 = jnp.bfloat16
ANY = pl.BlockSpec(memory_space=pl.ANY)
VMEM = pl.BlockSpec(memory_space=pltpu.VMEM)
LIMIT = 24 * 1024 * 1024


def params():
    return pltpu.CompilerParams(vmem_limit_bytes=LIMIT)


def small_cost():
    return pl.CostEstimate(flops=1000, bytes_accessed=1000, transcendentals=0)


def quad_place():
    return lax.rem(lax.axis_index("gy"), QUAD)


def x_place():
    return lax.div(lax.axis_index("gx"), 2)


def y_place():
    return lax.div(lax.axis_index("gy"), QUAD)


def swap(block, k):
    count = lax.axis_size("gy")
    return lax.ppermute(block, "gy", [(g, g ^ k) for g in range(count)])


def along_y(block, step, ring):
    count = lax.axis_size("gy")
    pairs = [(g, g + QUAD * step) for g in range(count)]
    if ring:
        pairs = [(s, t % count) for s, t in pairs]
    return lax.ppermute(block, "gy", [(s, t) for s, t in pairs if 0 <= t < count])


def along_x(block, step):
    count = lax.axis_size("gx")
    return lax.ppermute(block, "gx", [(g, (g + 2 * step) % count) for g in range(count)])


def swap_x(block, first):
    count = lax.axis_size("gx")
    pairs = [(g, g + 1) for g in range(first, count - 1, 2)]
    return lax.ppermute(block, "gx", pairs + [(t, s) for s, t in pairs])


def swap_y(block, first):
    count = lax.axis_size("gy")
    pairs = [(g, g + QUAD) for g in range(count - QUAD) if (g // QUAD - first) % 2 == 0]
    return lax.ppermute(block, "gy", pairs + [(t, s) for s, t in pairs])


def zero_at(value, z, edge):
    return jnp.where(z == edge, 0.0, value)


def pick_kernel(cot, *quarters):
    chan = cot.shape[3]
    j = quad_place()
    q = chan // QUAD
    part = q // RING
    source = lax.broadcasted_iota(jnp.int32, (chan, q), 0)
    place = lax.broadcasted_iota(jnp.int32, (chan, q), 1)
    base = lax.div(place, part) * q + lax.rem(place, part)
    flat = cot[...].reshape(-1, chan)
    for k, out in enumerate(quarters):
        pick = jnp.where(source == base + (j ^ k) * part, 1.0, 0.0).astype(BF16)
        got = jnp.dot(flat, pick, preferred_element_type=F32)
        out[...] = got.astype(BF16).reshape(out.shape)


def pick_channels(cot):
    rows, width, depth, chan = cot.shape
    quarter = jax.ShapeDtypeStruct((rows, width, depth, chan // QUAD), BF16)
    return pl.pallas_call(
        pick_kernel,
        out_shape=[quarter] * QUAD,
        in_specs=[VMEM],
        out_specs=[VMEM] * QUAD,
        compiler_params=params(),
        cost_estimate=small_cost(),
    )(cot)


def side_kernel(p0, p1, p2, p3, even, odd):
    width = p0.shape[1]
    is_odd = lax.rem(lax.axis_index("gx"), 2) == 1
    for k, p in enumerate((p0, p1, p2, p3)):
        first, last = p[:, 0], p[:, width - 1]
        even[k] = jnp.where(is_odd, first, last)
        odd[k] = jnp.where(is_odd, last, first)


def sides(quarters):
    rows, _, depth, q = quarters[0].shape
    return pl.pallas_call(
        side_kernel,
        out_shape=[jax.ShapeDtypeStruct((QUAD, rows, depth, q), BF16)] * 2,
        in_specs=[VMEM] * QUAD,
        out_specs=[VMEM] * 2,
        compiler_params=params(),
        cost_estimate=small_cost(),
    )(*quarters)


def rim_of(even, odd, k):
    is_odd = lax.rem(lax.axis_index("gx"), 2) == 1
    return jnp.where(is_odd, even[k], odd[k]), jnp.where(is_odd, odd[k], even[k])


def edge_kernel(p0, p1, p2, p3, even, odd, first, second):
    j = quad_place()
    is_odd = lax.rem(y_place(), 2) == 1
    rows, width = p0.shape[:2]

    def put(out, p, k, row):
        low, high = rim_of(even, odd, k)
        out[1:width + 1] = p[row]
        out[0] = low[row]
        out[width + 1] = high[row]

    for k, p in enumerate((p0, p1, p2, p3)):
        is_top, is_bottom = (j ^ k) == QUAD - 1, (j ^ k) == 0
        not_odd = jnp.logical_not(is_odd)
        pl.when(is_top & not_odd)(functools.partial(put, first, p, k, rows - 1))
        pl.when(is_top & is_odd)(functools.partial(put, second, p, k, rows - 1))
        pl.when(is_bottom & not_odd)(functools.partial(put, second, p, k, 0))
        pl.when(is_bottom & is_odd)(functools.partial(put, first, p, k, 0))


def edge_rows(quarters, even, odd):
    _, width, depth, q = quarters[0].shape
    return pl.pallas_call(
        edge_kernel,
        out_shape=[jax.ShapeDtypeStruct((width + 2, depth, q), BF16)] * 2,
        in_specs=[VMEM] * (QUAD + 2),
        out_specs=[VMEM] * 2,
        compiler_params=params(),
        cost_estimate=small_cost(),
    )(*quarters, even, odd)


def turn_kernel(p0, p1, p2, p3, even, odd, first, second, held, out):
    j, x = quad_place(), x_place()
    is_odd = lax.rem(y_place(), 2) == 1
    held[0] = jnp.where(is_odd, first[...], second[...])
    held[held.shape[0] - 1] = jnp.where(is_odd, second[...], first[...])
    for k, p in enumerate((p0, p1, p2, p3)):
        rows, width = p.shape[:2]
        low, high = rim_of(even, odd, k)
        at = pl.ds(1 + (j ^ k) * rows, rows)
        held[at, 1:width + 1] = p[...]
        held[at, 0] = low
        held[at, width + 1] = high

    tall, width, depth, q = held.shape
    width -= 2
    cells = tall * width * depth
    part = q // RING
    small = part // RING
    place = lax.broadcasted_iota(jnp.int32, (q, q), 0)
    source = lax.broadcasted_iota(jnp.int32, (q, q), 1)
    xpart = lax.rem(lax.div(place, part) + x, RING)
    ypart = lax.rem(lax.div(lax.rem(place, part), small) + y_place(), RING)
    base = ypart * part + xpart * small + lax.rem(place, small)
    order = jnp.where(source == base, 1.0, 0.0).astype(BF16)
    z = lax.rem(lax.broadcasted_iota(jnp.int32, (q, cells), 1), depth)
    for b in (-1, 0, 1):
        moved = held[:, 1 - b:1 - b + width].reshape(cells, q)
        value = lax.dot_general(
            order, moved, (((1,), (1,)), ((), ())), preferred_element_type=F32
        )
        high = zero_at(pltpu.roll(value, cells - 1, 1), z, depth - 1)
        low = zero_at(pltpu.roll(value, 1, 1), z, 0)
        for c, v in enumerate((high, value, low)):
            at = ((b + 1) * 3 + c) * q
            out[at:at + q] = v.astype(BF16)


def turn(quarters, *rims):
    rows, width, depth, q = quarters[0].shape
    width += 2
    tall = QUAD * rows + 2
    return pl.pallas_call(
        turn_kernel,
        out_shape=[
            jax.ShapeDtypeStruct((tall, width, depth, q), BF16),
            jax.ShapeDtypeStruct((9 * q, tall * (width - 2) * depth), BF16),
        ],
        in_specs=[VMEM] * (QUAD + 4),
        out_specs=[VMEM] * 2,
        compiler_params=params(),
        cost_estimate=small_cost(),
    )(*quarters, *rims)


def run_copies(pairs, sem):
    copies = [pltpu.make_async_copy(s, d, sem.at[n]) for n, (s, d) in enumerate(pairs)]
    for c in copies:
        c.start()
    return copies


def weight_kernel(norm, own_act, near, far_low, across_low, far_high, across_high, cot, *refs):
    groups, held, sem = (refs[:5], refs[5:10]), *refs[10:]
    j = quad_place()
    rows, width, depth, chan = own_act.shape
    pairs = [
        (piece, held.at[pl.ds((j ^ k) * rows + first, piece.shape[0])])
        for piece, k, first in (
            (own_act, 0, 0),
            (near, 1, 0),
            (far_low, 2, 0),
            (across_low, 3, 0),
            (far_high, 2, far_low.shape[0]),
            (across_high, 3, far_low.shape[0]),
        )
    ]
    for c in run_copies(pairs, sem):
        c.wait()
    row = width * depth
    cells = QUAD * rows * row
    act = held[...].reshape(cells, chan)
    q = cot.shape[0] // 9
    small = q // RING // RING
    for n in range(9):
        a, b = n // 3 - 1, n % 3
        moved = cot[3 * b * q:3 * (b + 1) * q, (1 - a) * row:(1 - a) * row + cells]
        term = jnp.dot(moved, act, preferred_element_type=F32) * norm
        for c in range(3):
            tap = 3 * n + c
            by_y = tap >= XTAPS
            up, down, keep_up, keep_down, own = groups[by_y]
            tap -= XTAPS * by_y

            def block(r, h):
                spots = [(2 * h, r), (2 * h + 1, r)] if by_y else [(r, 2 * h), (r, 2 * h + 1)]
                starts = [c * q + (xr * RING + yr) * small for xr, yr in spots]
                return jnp.concatenate([term[at:at + small] for at in starts], axis=0)

            up[0, tap] = block(2, 0).astype(BF16)
            down[0, tap] = block(2, 1).astype(BF16)
            keep_up[tap] = block(1, 0)
            up[1, tap] = block(1, 1).astype(BF16)
            down[1, tap] = block(3, 0).astype(BF16)
            keep_down[tap] = block(3, 1)
            own[0, tap] = block(0, 0)
            own[1, tap] = block(0, 1)


def weight_terms(norm, acts, cot):
    rows, width, depth, chan = acts[0].shape
    q = chan // QUAD
    cells = QUAD * rows * width * depth
    shapes = []
    for taps in (XTAPS, 27 - XTAPS):
        shape = (taps, q // RING // 2, chan)
        shapes += [jax.ShapeDtypeStruct((2,) + shape, BF16)] * 2
        shapes += [jax.ShapeDtypeStruct(shape, F32)] * 2
        shapes += [jax.ShapeDtypeStruct((2,) + shape, F32)]
    return pl.pallas_call(
        functools.partial(weight_kernel, norm),
        out_shape=shapes,
        in_specs=[ANY] * 6 + [VMEM],
        out_specs=[VMEM] * 10,
        scratch_shapes=[
            pltpu.VMEM((QUAD * rows, width, depth, chan), BF16),
            pltpu.SemaphoreType.DMA((6,)),
        ],
        compiler_params=params(),
        cost_estimate=pl.CostEstimate(
            flops=2 * 27 * q * cells * chan, bytes_accessed=10_000_000, transcendentals=0
        ),
    )(*acts, cot)


def input_kernel(held, own, above, across_low, across_high, below, *refs):
    send, keep, pass_on, weights, sem = refs
    j = quad_place()
    y = y_place()
    part = own.shape[1]
    low = across_low.shape[0]

    def at(s):
        return pl.ds(pl.multiple_of(lax.rem(y + s, RING) * part, part), part)

    pairs = [
        (own, weights.at[:, at(0)]),
        (above, weights.at[:, at(1)]),
        (across_low, weights.at[pl.ds(0, low), at(2)]),
        (across_high, weights.at[pl.ds(low, 27 - low), at(2)]),
        (below, weights.at[:, at(3)]),
    ]
    for c in run_copies(pairs, sem):
        c.wait()
    rows, width, depth, chan = keep.shape
    cells = rows * width * depth
    q = held.shape[3]
    taps = weights[...].reshape(9, 3, q, chan)
    for k, out in ((1, send.at[0]), (3, send.at[1]), (2, pass_on), (0, keep)):
        first = (j ^ k) * rows
        moved = []
        for n in range(9):
            a, b = n // 3 - 1, n % 3 - 1
            block = held[pl.ds(first + 1 - a, rows), 1 - b:1 - b + width]
            moved.append(block.reshape(cells, q))
        moved = jnp.concatenate(moved, axis=1)
        z = lax.rem(lax.broadcasted_iota(jnp.int32, (cells, chan), 0), depth)

        def term(c):
            return jnp.dot(moved, taps[:, c].reshape(9 * q, chan), preferred_element_type=F32)

        grad = term(1)
        grad = grad + zero_at(pltpu.roll(term(0), cells - 1, 0), z, depth - 1)
        grad = grad + zero_at(pltpu.roll(term(2), 1, 0), z, 0)
        out[...] = grad.reshape(rows, width, depth, chan)


def input_terms(held, parts):
    tall, width, depth, q = held.shape
    chan = QUAD * q
    block = ((tall - 2) // QUAD, width - 2, depth, chan)
    return pl.pallas_call(
        input_kernel,
        out_shape=[
            jax.ShapeDtypeStruct((2,) + block, F32),
            jax.ShapeDtypeStruct(block, F32),
            jax.ShapeDtypeStruct(block, F32),
        ],
        in_specs=[VMEM] + [ANY] * 5,
        out_specs=[VMEM] * 3,
        scratch_shapes=[pltpu.VMEM((27, q, chan), BF16), pltpu.SemaphoreType.DMA((5,))],
        compiler_params=params(),
        cost_estimate=pl.CostEstimate(
            flops=2 * 27 * tall * width * depth * q * chan, bytes_accessed=10_000_000, transcendentals=0
        ),
    )(held, *parts)


def finish_kernel(pre, keep, near, far, out):
    value = pre[...].astype(F32)
    s = jax.nn.sigmoid(value)
    grad = keep[...] + near[0] + far[...]
    out[...] = (grad * s * (1.0 + value * (1.0 - s))).astype(BF16)


def finish(pre_act, keep, near, far):
    return pl.pallas_call(
        finish_kernel,
        out_shape=jax.ShapeDtypeStruct(pre_act.shape, BF16),
        in_specs=[VMEM] * 4,
        out_specs=VMEM,
        compiler_params=params(),
    )(pre_act, keep, near, far)


def next_kernel(*refs):
    for n, out in enumerate(refs[8:]):
        came, keep = refs[2 * n:2 * n + 2]
        out[...] = (came[0].astype(F32) + keep[...]).astype(BF16)


def next_step(*parts):
    keeps = parts[1::2]
    return pl.pallas_call(
        next_kernel,
        out_shape=[jax.ShapeDtypeStruct(k.shape, BF16) for k in keeps],
        in_specs=[VMEM] * 8,
        out_specs=[VMEM] * 4,
        compiler_params=params(),
    )(*parts)


def split_kernel(*refs):
    for group in range(2):
        own, from_low, from_high, last_low, last_high = refs[5 * group:5 * group + 5]
        outs = refs[10 + 4 * group:14 + 4 * group]
        size = own.shape[2] // 2
        low = own[0] + from_high[1].astype(F32) + last_low[...].astype(F32)
        high = own[1] + from_low[1].astype(F32) + last_high[...].astype(F32)
        blocks = (low[:, :size], low[:, size:], high[:, :size], high[:, size:])
        for block, out in zip(blocks, outs):
            out[...] = block.astype(out.dtype)


def split(*parts):
    shapes = []
    for own in parts[::5]:
        _, taps, rows, chan = own.shape
        shape = (taps, rows // 2, chan)
        shapes += [jax.ShapeDtypeStruct(shape, F32)] + [jax.ShapeDtypeStruct(shape, BF16)] * 3
    return pl.pallas_call(
        split_kernel,
        out_shape=shapes,
        in_specs=[VMEM] * 10,
        out_specs=[VMEM] * 8,
        compiler_params=params(),
    )(*parts)


def join_kernel(*refs):
    out = refs[-1]
    x = x_place()
    size = refs[0].shape[1]
    low = refs[0].shape[0]
    for piece, part, k in zip(refs, (0, 1) * RING, (0, 0, 3, 3, 1, 1, 2, 2)):
        at = pl.ds(pl.multiple_of(lax.rem(x + k, RING) * size, size), size)
        first = part * low
        out[first:first + piece.shape[0], at] = piece[...]


def gather_x(low, high):
    low_below, high_above = along_x(low, 1), along_x(high, -1)
    high_below, low_above = along_x(high, 1), along_x(low, -1)
    low_far, high_far = along_x(low_below, 1), along_x(high_above, -1)
    _, size, chan = low.shape
    pieces = (low, high, low_below, high_below, low_above, high_above, low_far, high_far)
    return pl.pallas_call(
        join_kernel,
        out_shape=jax.ShapeDtypeStruct((27, RING * size, chan), F32),
        in_specs=[VMEM] * 8,
        out_specs=VMEM,
        compiler_params=params(),
    )(*pieces)


def body(pre_act, cot, weight):
    rows, width, depth, chan = pre_act.shape
    norm = 1.0 / math.sqrt(rows * lax.axis_size("gy") * width * lax.axis_size("gx") * depth)
    barrier = lax.optimization_barrier

    quarters = pick_channels(cot)
    quarters = [quarters[0]] + [swap(quarters[k], k) for k in (1, 2, 3)]
    act = jax.nn.silu(pre_act.astype(F32)).astype(BF16)
    half = rows // 2
    near = swap(act, 1)
    far_low = swap(act[:half], 2)
    above = along_y(weight, -1, True)
    below = along_y(weight, 1, True)
    quarters, far_low = barrier((quarters, far_low))
    even, odd = sides(quarters)
    even, odd = swap_x(even, 0), swap_x(odd, 1)
    even, odd, above, below, act_high = barrier((even, odd, above, below, act[half:]))
    far_high = swap(act_high, 2)
    first, second = edge_rows(quarters, even, odd)
    first, second = swap_y(first, 0), swap_y(second, 1)
    first, second, above, below, far_high = barrier((first, second, above, below, far_high))
    acts = [act, near, far_low, swap(far_low, 1), far_high, swap(far_high, 1)]
    taps = XTAPS
    parts = [weight, above, along_y(below[:taps], 1, True), along_y(above[taps:], -1, True), below]
    held, turned = turn(quarters, even, odd, first, second)

    terms = weight_terms(norm, acts, turned)
    held, terms = barrier((held, terms))
    xup, xdown, xkeep_up, xkeep_down, xown = terms[:5]
    yup, ydown, ykeep_up, ykeep_down, yown = terms[5:]
    xlow, xhigh = along_x(xup, 1), along_x(xdown, -1)
    ylow, yhigh = along_y(yup, 1, True), along_y(ydown, -1, True)
    grads = input_terms(held, parts)
    grads, xlow, xhigh, ylow, yhigh = barrier((grads, xlow, xhigh, ylow, yhigh))
    send, keep, pass_on = grads
    got = swap(send, 1)
    xup, xdown, yup, ydown = next_step(
        xlow, xkeep_up, xhigh, xkeep_down, ylow, ykeep_up, yhigh, ykeep_down
    )
    xlast = along_x(xup, 1), along_x(xdown, -1)
    ylast = along_y(yup, 1, True), along_y(ydown, -1, True)
    xlast, ylast, got = barrier((xlast, ylast, got))
    blocks = split(xown, xlow, xhigh, *xlast, yown, ylow, yhigh, *ylast)

    low, high = blocks[0], blocks[4]
    lows = [along_y(block, r, True) for r, block in zip((1, 2, 3), blocks[1:4])]
    highs = [along_x(block, r) for r, block in zip((1, 2, 3), blocks[5:])]
    for other in lows:
        low = low + other.astype(F32)
    for other in highs:
        high = high + other.astype(F32)
    count = lax.axis_size("gx")
    mine = jnp.concatenate([low.astype(BF16), high.astype(BF16)])
    other = lax.ppermute(mine, "gx", [(g, g ^ 1) for g in range(count)])
    other, passed = barrier((other, pass_on + got[1]))
    far_grad = swap(passed, 2)
    low, high = low + other[:taps].astype(F32), high + other[taps:].astype(F32)
    grad_weight = gather_x(low, high)
    grad_pre = finish(pre_act, keep, got, far_grad)
    return (grad_pre, grad_weight)


def solution(mesh):
    return jax.shard_map(
        body,
        mesh=mesh,
        in_specs=(P("gy", "gx", None, None), P("gy", "gx", None, None), P(None, "gy", None)),
        out_specs=(P("gy", "gx", None, None), P(None, "gy", None)),
        check_vma=False,
    )
```

```python
import functools
import math

import jax
import jax.numpy as jnp
from jax import lax
from jax.experimental import pallas as pl
from jax.experimental.pallas import tpu as pltpu
from jax.sharding import PartitionSpec as P

QUAD = 4
RING = 4
XTAPS = 13
F32 = jnp.float32
BF16 = jnp.bfloat16
ANY = pl.BlockSpec(memory_space=pl.ANY)
VMEM = pl.BlockSpec(memory_space=pltpu.VMEM)
LIMIT = 24 * 1024 * 1024


def params():
    return pltpu.CompilerParams(vmem_limit_bytes=LIMIT)


def small_cost():
    return pl.CostEstimate(flops=1000, bytes_accessed=1000, transcendentals=0)


def quad_place():
    return lax.rem(lax.axis_index("gy"), QUAD)


def x_place():
    return lax.div(lax.axis_index("gx"), 2)


def y_place():
    return lax.div(lax.axis_index("gy"), QUAD)


def swap(block, k):
    count = lax.axis_size("gy")
    return lax.ppermute(block, "gy", [(g, g ^ k) for g in range(count)])


def along_y(block, step, ring):
    count = lax.axis_size("gy")
    pairs = [(g, g + QUAD * step) for g in range(count)]
    if ring:
        pairs = [(s, t % count) for s, t in pairs]
    return lax.ppermute(block, "gy", [(s, t) for s, t in pairs if 0 <= t < count])


def along_x(block, step):
    count = lax.axis_size("gx")
    return lax.ppermute(block, "gx", [(g, (g + 2 * step) % count) for g in range(count)])


def swap_x(block, first):
    count = lax.axis_size("gx")
    pairs = [(g, g + 1) for g in range(first, count - 1, 2)]
    return lax.ppermute(block, "gx", pairs + [(t, s) for s, t in pairs])


def zero_at(value, z, edge):
    return jnp.where(z == edge, 0.0, value)


def pick(block, k):
    chan = block.shape[-1]
    q = chan // QUAD
    part = q // RING
    source = lax.broadcasted_iota(jnp.int32, (chan, q), 0)
    place = lax.broadcasted_iota(jnp.int32, (chan, q), 1)
    base = lax.div(place, part) * q + lax.rem(place, part) + (quad_place() ^ k) * part
    matrix = jnp.where(source == base, 1.0, 0.0).astype(BF16)
    got = jnp.dot(block.reshape(-1, chan), matrix, preferred_element_type=F32)
    return got.astype(BF16).reshape(block.shape[:-1] + (q,))


def own_kernel(cot, *quarters):
    for k, out in enumerate(quarters):
        out[...] = pick(cot[...], k)


def extra_kernel(extra, q0, q1, q2, q3, *quarters):
    for k, (own, out) in enumerate(zip((q0, q1, q2, q3), quarters)):
        rows = own.shape[0]
        out[0:rows] = own[...]
        out[rows] = pick(extra[...], k)


def quarters_of(kernel, rows, *ins):
    width, depth, chan = ins[0].shape[-3:]
    quarter = jax.ShapeDtypeStruct((rows, width, depth, chan // QUAD), BF16)
    return pl.pallas_call(
        kernel,
        out_shape=[quarter] * QUAD,
        in_specs=[VMEM] * len(ins),
        out_specs=[VMEM] * QUAD,
        compiler_params=params(),
        cost_estimate=pl.CostEstimate(
            flops=1000, bytes_accessed=40_000_000 if kernel is own_kernel else 1000, transcendentals=0
        ),
    )(*ins)


def side_kernel(p0, p1, p2, p3, even, odd):
    width = p0.shape[1]
    is_odd = lax.rem(lax.axis_index("gx"), 2) == 1
    for k, p in enumerate((p0, p1, p2, p3)):
        first, last = p[:, 0], p[:, width - 1]
        even[k] = jnp.where(is_odd, first, last)
        odd[k] = jnp.where(is_odd, last, first)


def sides(quarters):
    rows, _, depth, q = quarters[0].shape
    return pl.pallas_call(
        side_kernel,
        out_shape=[jax.ShapeDtypeStruct((QUAD, rows, depth, q), BF16)] * 2,
        in_specs=[VMEM] * QUAD,
        out_specs=[VMEM] * 2,
        compiler_params=params(),
        cost_estimate=small_cost(),
    )(*quarters)


def turn_kernel(p0, p1, p2, p3, even, odd, held, out):
    j, x = quad_place(), x_place()
    is_odd = lax.rem(lax.axis_index("gx"), 2) == 1
    for k, p in enumerate((p0, p1, p2, p3)):
        rows, width = p.shape[0] - 1, p.shape[1]
        low = jnp.where(is_odd, even[k], odd[k])
        high = jnp.where(is_odd, odd[k], even[k])

        def put(at, part):
            held[at, 1:width + 1] = p[part]
            held[at, 0] = low[part]
            held[at, width + 1] = high[part]

        put(pl.ds(1 + (j ^ k) * rows, rows), slice(0, rows))
        pl.when((j ^ k) == 0)(functools.partial(put, 0, rows))
        pl.when((j ^ k) == QUAD - 1)(functools.partial(put, held.shape[0] - 1, rows))

    tall, width, depth, q = held.shape
    width -= 2
    cells = tall * width * depth
    part = q // RING
    small = part // RING
    place = lax.broadcasted_iota(jnp.int32, (q, q), 0)
    source = lax.broadcasted_iota(jnp.int32, (q, q), 1)
    xpart = lax.rem(lax.div(place, part) + x, RING)
    ypart = lax.rem(lax.div(lax.rem(place, part), small) + y_place(), RING)
    base = ypart * part + xpart * small + lax.rem(place, small)
    order = jnp.where(source == base, 1.0, 0.0).astype(BF16)
    z = lax.rem(lax.broadcasted_iota(jnp.int32, (q, cells), 1), depth)
    for b in (-1, 0, 1):
        moved = held[:, 1 - b:1 - b + width].reshape(cells, q)
        value = lax.dot_general(
            order, moved, (((1,), (1,)), ((), ())), preferred_element_type=F32
        )
        high = zero_at(pltpu.roll(value, cells - 1, 1), z, depth - 1)
        low = zero_at(pltpu.roll(value, 1, 1), z, 0)
        for c, v in enumerate((high, value, low)):
            at = ((b + 1) * 3 + c) * q
            out[at:at + q] = v.astype(BF16)


def turn(quarters, even, odd):
    rows, width, depth, q = quarters[0].shape
    width += 2
    tall = QUAD * (rows - 1) + 2
    return pl.pallas_call(
        turn_kernel,
        out_shape=[
            jax.ShapeDtypeStruct((tall, width, depth, q), BF16),
            jax.ShapeDtypeStruct((9 * q, tall * (width - 2) * depth), BF16),
        ],
        in_specs=[VMEM] * (QUAD + 2),
        out_specs=[VMEM] * 2,
        compiler_params=params(),
        cost_estimate=small_cost(),
    )(*quarters, even, odd)


def run_copies(pairs, sem):
    copies = [pltpu.make_async_copy(s, d, sem.at[n]) for n, (s, d) in enumerate(pairs)]
    for c in copies:
        c.start()
    return copies


def weight_kernel(norm, own_act, near, far, across, cot, *refs):
    groups, held, sem = (refs[:5], refs[5:10]), *refs[10:]
    j = quad_place()
    rows, width, depth, chan = own_act.shape
    pairs = []
    for k, piece in enumerate((own_act, near, far, across)):
        pairs.append((piece, held.at[pl.ds((j ^ k) * rows, rows)]))
    for c in run_copies(pairs, sem):
        c.wait()
    row = width * depth
    cells = QUAD * rows * row
    act = held[...].reshape(cells, chan)
    q = cot.shape[0] // 9
    small = q // RING // RING
    for n in range(9):
        a, b = n // 3 - 1, n % 3
        moved = cot[3 * b * q:3 * (b + 1) * q, (1 - a) * row:(1 - a) * row + cells]
        term = jnp.dot(moved, act, preferred_element_type=F32) * norm
        for c in range(3):
            tap = 3 * n + c
            by_y = tap >= XTAPS
            up, down, keep_up, keep_down, own = groups[by_y]
            tap -= XTAPS * by_y

            def block(r, h):
                spots = [(2 * h, r), (2 * h + 1, r)] if by_y else [(r, 2 * h), (r, 2 * h + 1)]
                starts = [c * q + (xr * RING + yr) * small for xr, yr in spots]
                return jnp.concatenate([term[at:at + small] for at in starts], axis=0)

            up[0, tap] = block(2, 0).astype(BF16)
            down[0, tap] = block(2, 1).astype(BF16)
            keep_up[tap] = block(1, 0)
            up[1, tap] = block(1, 1).astype(BF16)
            down[1, tap] = block(3, 0).astype(BF16)
            keep_down[tap] = block(3, 1)
            own[0, tap] = block(0, 0)
            own[1, tap] = block(0, 1)


def weight_terms(norm, acts, cot):
    rows, width, depth, chan = acts[0].shape
    q = chan // QUAD
    cells = QUAD * rows * width * depth
    shapes = []
    for taps in (XTAPS, 27 - XTAPS):
        shape = (taps, q // RING // 2, chan)
        shapes += [jax.ShapeDtypeStruct((2,) + shape, BF16)] * 2
        shapes += [jax.ShapeDtypeStruct(shape, F32)] * 2
        shapes += [jax.ShapeDtypeStruct((2,) + shape, F32)]
    return pl.pallas_call(
        functools.partial(weight_kernel, norm),
        out_shape=shapes,
        in_specs=[ANY] * 4 + [VMEM],
        out_specs=[VMEM] * 10,
        scratch_shapes=[
            pltpu.VMEM((QUAD * rows, width, depth, chan), BF16),
            pltpu.SemaphoreType.DMA((4,)),
        ],
        compiler_params=params(),
        cost_estimate=pl.CostEstimate(
            flops=2 * 27 * q * cells * chan, bytes_accessed=10_000_000, transcendentals=0
        ),
    )(*acts, cot)


def input_kernel(held, own, above, across_low, across_high, below, *refs):
    send, keep, pass_on, weights, sem = refs
    j = quad_place()
    y = y_place()
    part = own.shape[1]
    low = across_low.shape[0]

    def at(s):
        return pl.ds(pl.multiple_of(lax.rem(y + s, RING) * part, part), part)

    pairs = [
        (own, weights.at[:, at(0)]),
        (above, weights.at[:, at(1)]),
        (across_low, weights.at[pl.ds(0, low), at(2)]),
        (across_high, weights.at[pl.ds(low, 27 - low), at(2)]),
        (below, weights.at[:, at(3)]),
    ]
    for c in run_copies(pairs, sem):
        c.wait()
    rows, width, depth, chan = keep.shape
    cells = rows * width * depth
    q = held.shape[3]
    taps = weights[...].reshape(9, 3, q, chan)
    for k, out in ((1, send.at[0]), (3, send.at[1]), (2, pass_on), (0, keep)):
        first = (j ^ k) * rows
        moved = []
        for n in range(9):
            a, b = n // 3 - 1, n % 3 - 1
            block = held[pl.ds(first + 1 - a, rows), 1 - b:1 - b + width]
            moved.append(block.reshape(cells, q))
        moved = jnp.concatenate(moved, axis=1)
        z = lax.rem(lax.broadcasted_iota(jnp.int32, (cells, chan), 0), depth)

        def term(c):
            return jnp.dot(moved, taps[:, c].reshape(9 * q, chan), preferred_element_type=F32)

        grad = term(1)
        grad = grad + zero_at(pltpu.roll(term(0), cells - 1, 0), z, depth - 1)
        grad = grad + zero_at(pltpu.roll(term(2), 1, 0), z, 0)
        out[...] = grad.reshape(rows, width, depth, chan)


def input_terms(held, parts):
    tall, width, depth, q = held.shape
    chan = QUAD * q
    block = ((tall - 2) // QUAD, width - 2, depth, chan)
    return pl.pallas_call(
        input_kernel,
        out_shape=[
            jax.ShapeDtypeStruct((2,) + block, F32),
            jax.ShapeDtypeStruct(block, F32),
            jax.ShapeDtypeStruct(block, F32),
        ],
        in_specs=[VMEM] + [ANY] * 5,
        out_specs=[VMEM] * 3,
        scratch_shapes=[pltpu.VMEM((27, q, chan), BF16), pltpu.SemaphoreType.DMA((5,))],
        compiler_params=params(),
        cost_estimate=pl.CostEstimate(
            flops=2 * 27 * tall * width * depth * q * chan, bytes_accessed=10_000_000, transcendentals=0
        ),
    )(held, *parts)


def finish_kernel(pre, keep, near, far, out):
    value = pre[...].astype(F32)
    s = jax.nn.sigmoid(value)
    grad = keep[...] + near[0] + far[...].astype(F32)
    out[...] = (grad * s * (1.0 + value * (1.0 - s))).astype(BF16)


def finish(pre_act, keep, near, far):
    return pl.pallas_call(
        finish_kernel,
        out_shape=jax.ShapeDtypeStruct(pre_act.shape, BF16),
        in_specs=[VMEM] * 4,
        out_specs=VMEM,
        compiler_params=params(),
    )(pre_act, keep, near, far)


def next_kernel(*refs):
    for n, out in enumerate(refs[8:]):
        came, keep = refs[2 * n:2 * n + 2]
        out[...] = (came[0].astype(F32) + keep[...]).astype(BF16)


def next_step(*parts):
    keeps = parts[1::2]
    return pl.pallas_call(
        next_kernel,
        out_shape=[jax.ShapeDtypeStruct(k.shape, BF16) for k in keeps],
        in_specs=[VMEM] * 8,
        out_specs=[VMEM] * 4,
        compiler_params=params(),
    )(*parts)


def split_kernel(*refs):
    for group in range(2):
        own, from_low, from_high, last_low, last_high = refs[5 * group:5 * group + 5]
        outs = refs[10 + 4 * group:14 + 4 * group]
        size = own.shape[2] // 2
        low = own[0] + from_high[1].astype(F32) + last_low[...].astype(F32)
        high = own[1] + from_low[1].astype(F32) + last_high[...].astype(F32)
        blocks = (low[:, :size], low[:, size:], high[:, :size], high[:, size:])
        for block, out in zip(blocks, outs):
            out[...] = block.astype(out.dtype)


def split(*parts):
    shapes = []
    for own in parts[::5]:
        _, taps, rows, chan = own.shape
        shape = (taps, rows // 2, chan)
        shapes += [jax.ShapeDtypeStruct(shape, F32)] + [jax.ShapeDtypeStruct(shape, BF16)] * 3
    return pl.pallas_call(
        split_kernel,
        out_shape=shapes,
        in_specs=[VMEM] * 10,
        out_specs=[VMEM] * 8,
        compiler_params=params(),
    )(*parts)


def join_kernel(*refs):
    out = refs[-1]
    x = x_place()
    size = refs[0].shape[1]
    low = refs[0].shape[0]
    for piece, part, k in zip(refs, (0, 1) * RING, (0, 0, 3, 3, 1, 1, 2, 2)):
        at = pl.ds(pl.multiple_of(lax.rem(x + k, RING) * size, size), size)
        first = part * low
        out[first:first + piece.shape[0], at] = piece[...].astype(F32)


def gather_x(low, high):
    low_below, high_above = along_x(low, 1), along_x(high, -1)
    high_below, low_above = along_x(high.astype(BF16), 1), along_x(low.astype(BF16), -1)
    low_far, high_far = along_x(low_below, 1), along_x(high_above, -1)
    return low, high, low_below, high_below, low_above, high_above, low_far, high_far


def join(pieces):
    _, size, chan = pieces[0].shape
    return pl.pallas_call(
        join_kernel,
        out_shape=jax.ShapeDtypeStruct((27, RING * size, chan), F32),
        in_specs=[VMEM] * 8,
        out_specs=VMEM,
        compiler_params=params(),
    )(*pieces)


def body(pre_act, cot, weight):
    rows, width, depth, chan = pre_act.shape
    norm = 1.0 / math.sqrt(rows * lax.axis_size("gy") * width * lax.axis_size("gx") * depth)
    j = quad_place()
    barrier = lax.optimization_barrier

    count = lax.axis_size("gy")
    pairs = [(g, g + 1) for g in range(QUAD - 1, count - 1, QUAD)]
    pairs = pairs + [(t, s) for s, t in pairs]
    extra = lax.ppermute(jnp.where(j == 0, cot[0], cot[rows - 1]), "gy", pairs)
    act = jax.nn.silu(pre_act.astype(F32)).astype(BF16)
    far = swap(act, 2)
    near = swap(act, 1)
    own_quarters = quarters_of(own_kernel, rows, cot)
    extra, near, own_quarters = barrier((extra, near, own_quarters))
    quarters = quarters_of(extra_kernel, rows + 1, extra, *own_quarters)
    quarters, weight = barrier((quarters, weight))
    above = along_y(weight, -1, True)
    below = along_y(weight, 1, True)
    quarters = [quarters[0]] + [swap(quarters[k], k) for k in (1, 2, 3)]
    quarters, far = barrier((quarters, far))
    acts = [act, near, far, swap(far, 1)]
    even, odd = sides(quarters)
    even, odd = swap_x(even, 0), swap_x(odd, 1)
    even, odd, above, below = barrier((even, odd, above, below))
    taps = XTAPS
    parts = [weight, above, along_y(below[:taps], 1, True), along_y(above[taps:], -1, True), below]
    held, turned = turn(quarters, even, odd)

    terms = weight_terms(norm, acts, turned)
    held, terms = barrier((held, terms))
    xup, xdown, xkeep_up, xkeep_down, xown = terms[:5]
    yup, ydown, ykeep_up, ykeep_down, yown = terms[5:]
    xlow, xhigh = along_x(xup, 1), along_x(xdown, -1)
    ylow, yhigh = along_y(yup, 1, True), along_y(ydown, -1, True)
    grads = input_terms(held, parts)
    grads, xlow, xhigh, ylow, yhigh = barrier((grads, xlow, xhigh, ylow, yhigh))
    send, keep, pass_on = grads
    got = swap(send, 1)
    xup, xdown, yup, ydown = next_step(
        xlow, xkeep_up, xhigh, xkeep_down, ylow, ykeep_up, yhigh, ykeep_down
    )
    xlast = along_x(xup, 1), along_x(xdown, -1)
    ylast = along_y(yup, 1, True), along_y(ydown, -1, True)
    xlast, ylast, got = barrier((xlast, ylast, got))
    blocks = split(xown, xlow, xhigh, *xlast, yown, ylow, yhigh, *ylast)

    low, high = blocks[0], blocks[4]
    lows = [along_y(block, r, True) for r, block in zip((1, 2, 3), blocks[1:4])]
    highs = [along_x(block, r) for r, block in zip((1, 2, 3), blocks[5:])]
    for other in lows:
        low = low + other.astype(F32)
    for other in highs:
        high = high + other.astype(F32)
    count = lax.axis_size("gx")
    mine = jnp.concatenate([low.astype(BF16), high.astype(BF16)])
    other = lax.ppermute(mine, "gx", [(g, g ^ 1) for g in range(count)])
    other, passed = barrier((other, (pass_on + got[1]).astype(BF16)))
    far_grad = swap(passed, 2)
    low, high = low + other[:taps].astype(F32), high + other[taps:].astype(F32)
    pieces = gather_x(low, high)
    grad_pre = finish(pre_act, keep, got, far_grad)
    grad_pre, pieces = barrier((grad_pre, pieces))
    return (grad_pre, join(pieces))


def solution(mesh):
    return jax.shard_map(
        body,
        mesh=mesh,
        in_specs=(P("gy", "gx", None, None), P("gy", "gx", None, None), P(None, "gy", None)),
        out_specs=(P("gy", "gx", None, None), P(None, "gy", None)),
        check_vma=False,
    )
```

```python
import functools
import math

import jax
import jax.numpy as jnp
from jax import lax
from jax.experimental import pallas as pl
from jax.experimental.pallas import tpu as pltpu
from jax.sharding import PartitionSpec as P

QUAD = 4
RING = 4
XTAPS = 13
F32 = jnp.float32
BF16 = jnp.bfloat16
ANY = pl.BlockSpec(memory_space=pl.ANY)
VMEM = pl.BlockSpec(memory_space=pltpu.VMEM)
LIMIT = 24 * 1024 * 1024


def params():
    return pltpu.CompilerParams(vmem_limit_bytes=LIMIT)


def small_cost():
    return pl.CostEstimate(flops=1000, bytes_accessed=1000, transcendentals=0)


def quad_place():
    return lax.rem(lax.axis_index("gy"), QUAD)


def x_place():
    return lax.div(lax.axis_index("gx"), 2)


def y_place():
    return lax.div(lax.axis_index("gy"), QUAD)


def swap(block, k):
    count = lax.axis_size("gy")
    return lax.ppermute(block, "gy", [(g, g ^ k) for g in range(count)])


def along_y(block, step, ring):
    count = lax.axis_size("gy")
    pairs = [(g, g + QUAD * step) for g in range(count)]
    if ring:
        pairs = [(s, t % count) for s, t in pairs]
    return lax.ppermute(block, "gy", [(s, t) for s, t in pairs if 0 <= t < count])


def along_x(block, step):
    count = lax.axis_size("gx")
    return lax.ppermute(block, "gx", [(g, (g + 2 * step) % count) for g in range(count)])


def swap_x(block, first):
    nx, ny = lax.axis_size("gx"), lax.axis_size("gy")
    pairs = []
    for g in range(first, nx - 1, 2):
        for h in range(ny):
            pairs += [(g * ny + h, (g + 1) * ny + (h ^ 2)), ((g + 1) * ny + h, g * ny + (h ^ 2))]
    return lax.ppermute(block, ("gx", "gy"), pairs)


def zero_at(value, z, edge):
    return jnp.where(z == edge, 0.0, value)


def pick(block, k):
    chan = block.shape[-1]
    q = chan // QUAD
    part = q // RING
    source = lax.broadcasted_iota(jnp.int32, (chan, q), 0)
    place = lax.broadcasted_iota(jnp.int32, (chan, q), 1)
    base = lax.div(place, part) * q + lax.rem(place, part) + (quad_place() ^ k) * part
    matrix = jnp.where(source == base, 1.0, 0.0).astype(BF16)
    got = jnp.dot(block.reshape(-1, chan), matrix, preferred_element_type=F32)
    return got.astype(BF16).reshape(block.shape[:-1] + (q,))


def side_kernel(cot, extra, even, odd):
    rows, width = cot.shape[:2]
    is_odd = lax.rem(lax.axis_index("gx"), 2) == 1

    def put(out, upper):
        out[0:rows] = jnp.where(upper, cot[:, width - 1], cot[:, 0])
        out[rows] = jnp.where(upper, extra[width - 1], extra[0])

    put(even, jnp.logical_not(is_odd))
    put(odd, is_odd)


def sides(cot, extra):
    rows, width, depth, chan = cot.shape
    return pl.pallas_call(
        side_kernel,
        out_shape=[jax.ShapeDtypeStruct((rows + 1, depth, chan), BF16)] * 2,
        in_specs=[VMEM] * 2,
        out_specs=[VMEM] * 2,
        compiler_params=params(),
        cost_estimate=small_cost(),
    )(cot, extra)


def pick_kernel(cot, extra, even, odd, *quarters):
    rows, width = cot.shape[:2]
    is_odd = lax.rem(lax.axis_index("gx"), 2) == 1
    low = jnp.where(is_odd, even[...], odd[...])
    high = jnp.where(is_odd, odd[...], even[...])
    for k, out in enumerate(quarters):
        out[0:rows, 1:width + 1] = pick(cot[...], k)
        out[rows, 1:width + 1] = pick(extra[...], k)
        out[:, 0] = pick(low, k)
        out[:, width + 1] = pick(high, k)


def pick_channels(cot, *rims):
    rows, width, depth, chan = cot.shape
    quarter = jax.ShapeDtypeStruct((rows + 1, width + 2, depth, chan // QUAD), BF16)
    return pl.pallas_call(
        pick_kernel,
        out_shape=[quarter] * QUAD,
        in_specs=[VMEM] * 4,
        out_specs=[VMEM] * QUAD,
        compiler_params=params(),
        cost_estimate=small_cost(),
    )(cot, *rims)


def turn_kernel(p0, p1, p2, p3, held, out):
    j, x = quad_place(), x_place()
    last = held.shape[0] - 1
    for k, p in enumerate((p0, p1, p2, p3)):
        rows, width = p.shape[0] - 1, p.shape[1] - 2

        def put_own(at, part):
            held[at, 1:width + 1] = p[part, 1:width + 1]

        def put_rims(at, part):
            held[at, 0] = p[part, 0]
            held[at, width + 1] = p[part, width + 1]

        for place, put in ((j ^ k, put_own), (j ^ k ^ 2, put_rims)):
            put(pl.ds(1 + place * rows, rows), slice(0, rows))
            pl.when(place == QUAD - 1)(functools.partial(put, 0, rows))
            pl.when(place == 0)(functools.partial(put, last, rows))

    tall, width, depth, q = held.shape
    width -= 2
    cells = tall * width * depth
    part = q // RING
    small = part // RING
    place = lax.broadcasted_iota(jnp.int32, (q, q), 0)
    source = lax.broadcasted_iota(jnp.int32, (q, q), 1)
    xpart = lax.rem(lax.div(place, part) + x, RING)
    ypart = lax.rem(lax.div(lax.rem(place, part), small) + y_place(), RING)
    base = ypart * part + xpart * small + lax.rem(place, small)
    order = jnp.where(source == base, 1.0, 0.0).astype(BF16)
    z = lax.rem(lax.broadcasted_iota(jnp.int32, (q, cells), 1), depth)
    for b in (-1, 0, 1):
        moved = held[:, 1 - b:1 - b + width].reshape(cells, q)
        value = lax.dot_general(
            order, moved, (((1,), (1,)), ((), ())), preferred_element_type=F32
        )
        high = zero_at(pltpu.roll(value, cells - 1, 1), z, depth - 1)
        low = zero_at(pltpu.roll(value, 1, 1), z, 0)
        for c, v in enumerate((high, value, low)):
            at = ((b + 1) * 3 + c) * q
            out[at:at + q] = v.astype(BF16)


def turn(quarters):
    rows, width, depth, q = quarters[0].shape
    tall = QUAD * (rows - 1) + 2
    return pl.pallas_call(
        turn_kernel,
        out_shape=[
            jax.ShapeDtypeStruct((tall, width, depth, q), BF16),
            jax.ShapeDtypeStruct((9 * q, tall * (width - 2) * depth), BF16),
        ],
        in_specs=[VMEM] * QUAD,
        out_specs=[VMEM] * 2,
        compiler_params=params(),
        cost_estimate=small_cost(),
    )(*quarters)


def run_copies(pairs, sem):
    copies = [pltpu.make_async_copy(s, d, sem.at[n]) for n, (s, d) in enumerate(pairs)]
    for c in copies:
        c.start()
    return copies


def weight_kernel(norm, own_act, near, far, across, cot, *refs):
    groups, held, sem = (refs[:5], refs[5:10]), *refs[10:]
    j = quad_place()
    rows, width, depth, chan = own_act.shape
    pairs = []
    for k, piece in enumerate((own_act, near, far, across)):
        pairs.append((piece, held.at[pl.ds((j ^ k) * rows, rows)]))
    for c in run_copies(pairs, sem):
        c.wait()
    row = width * depth
    cells = QUAD * rows * row
    act = held[...].reshape(cells, chan)
    q = cot.shape[0] // 9
    small = q // RING // RING
    for n in range(9):
        a, b = n // 3 - 1, n % 3
        moved = cot[3 * b * q:3 * (b + 1) * q, (1 - a) * row:(1 - a) * row + cells]
        term = jnp.dot(moved, act, preferred_element_type=F32) * norm
        for c in range(3):
            tap = 3 * n + c
            by_y = tap >= XTAPS
            up, down, keep_up, keep_down, own = groups[by_y]
            tap -= XTAPS * by_y

            def block(r, h):
                spots = [(2 * h, r), (2 * h + 1, r)] if by_y else [(r, 2 * h), (r, 2 * h + 1)]
                starts = [c * q + (xr * RING + yr) * small for xr, yr in spots]
                return jnp.concatenate([term[at:at + small] for at in starts], axis=0)

            up[0, tap] = block(2, 0).astype(BF16)
            down[0, tap] = block(2, 1).astype(BF16)
            keep_up[tap] = block(1, 0)
            up[1, tap] = block(1, 1).astype(BF16)
            down[1, tap] = block(3, 0).astype(BF16)
            keep_down[tap] = block(3, 1)
            own[0, tap] = block(0, 0)
            own[1, tap] = block(0, 1)


def weight_terms(norm, acts, cot):
    rows, width, depth, chan = acts[0].shape
    q = chan // QUAD
    cells = QUAD * rows * width * depth
    shapes = []
    for taps in (XTAPS, 27 - XTAPS):
        shape = (taps, q // RING // 2, chan)
        shapes += [jax.ShapeDtypeStruct((2,) + shape, BF16)] * 2
        shapes += [jax.ShapeDtypeStruct(shape, F32)] * 2
        shapes += [jax.ShapeDtypeStruct((2,) + shape, F32)]
    return pl.pallas_call(
        functools.partial(weight_kernel, norm),
        out_shape=shapes,
        in_specs=[ANY] * 4 + [VMEM],
        out_specs=[VMEM] * 10,
        scratch_shapes=[
            pltpu.VMEM((QUAD * rows, width, depth, chan), BF16),
            pltpu.SemaphoreType.DMA((4,)),
        ],
        compiler_params=params(),
        cost_estimate=pl.CostEstimate(
            flops=2 * 27 * q * cells * chan, bytes_accessed=10_000_000, transcendentals=0
        ),
    )(*acts, cot)


def input_kernel(held, own, above, across_low, across_high, below, *refs):
    send, keep, pass_on, weights, sem = refs
    j = quad_place()
    y = y_place()
    part = own.shape[1]
    low = across_low.shape[0]

    def at(s):
        return pl.ds(pl.multiple_of(lax.rem(y + s, RING) * part, part), part)

    pairs = [
        (own, weights.at[:, at(0)]),
        (above, weights.at[:, at(1)]),
        (across_low, weights.at[pl.ds(0, low), at(2)]),
        (across_high, weights.at[pl.ds(low, 27 - low), at(2)]),
        (below, weights.at[:, at(3)]),
    ]
    for c in run_copies(pairs, sem):
        c.wait()
    rows, width, depth, chan = keep.shape
    cells = rows * width * depth
    q = held.shape[3]
    taps = weights[...].reshape(9, 3, q, chan)
    for k, out in ((1, send.at[0]), (3, send.at[1]), (2, pass_on), (0, keep)):
        first = (j ^ k) * rows
        moved = []
        for n in range(9):
            a, b = n // 3 - 1, n % 3 - 1
            block = held[pl.ds(first + 1 - a, rows), 1 - b:1 - b + width]
            moved.append(block.reshape(cells, q))
        moved = jnp.concatenate(moved, axis=1)
        z = lax.rem(lax.broadcasted_iota(jnp.int32, (cells, chan), 0), depth)

        def term(c):
            return jnp.dot(moved, taps[:, c].reshape(9 * q, chan), preferred_element_type=F32)

        grad = term(1)
        grad = grad + zero_at(pltpu.roll(term(0), cells - 1, 0), z, depth - 1)
        grad = grad + zero_at(pltpu.roll(term(2), 1, 0), z, 0)
        out[...] = grad.reshape(rows, width, depth, chan)


def input_terms(held, parts):
    tall, width, depth, q = held.shape
    chan = QUAD * q
    block = ((tall - 2) // QUAD, width - 2, depth, chan)
    return pl.pallas_call(
        input_kernel,
        out_shape=[
            jax.ShapeDtypeStruct((2,) + block, F32),
            jax.ShapeDtypeStruct(block, F32),
            jax.ShapeDtypeStruct(block, F32),
        ],
        in_specs=[VMEM] + [ANY] * 5,
        out_specs=[VMEM] * 3,
        scratch_shapes=[pltpu.VMEM((27, q, chan), BF16), pltpu.SemaphoreType.DMA((5,))],
        compiler_params=params(),
        cost_estimate=pl.CostEstimate(
            flops=2 * 27 * tall * width * depth * q * chan, bytes_accessed=10_000_000, transcendentals=0
        ),
    )(held, *parts)


def finish_kernel(pre, keep, near, far, out):
    value = pre[...].astype(F32)
    s = jax.nn.sigmoid(value)
    grad = keep[...] + near[0] + far[...].astype(F32)
    out[...] = (grad * s * (1.0 + value * (1.0 - s))).astype(BF16)


def finish(pre_act, keep, near, far):
    return pl.pallas_call(
        finish_kernel,
        out_shape=jax.ShapeDtypeStruct(pre_act.shape, BF16),
        in_specs=[VMEM] * 4,
        out_specs=VMEM,
        compiler_params=params(),
    )(pre_act, keep, near, far)


def next_kernel(*refs):
    for n, out in enumerate(refs[8:]):
        came, keep = refs[2 * n:2 * n + 2]
        out[...] = (came[0].astype(F32) + keep[...]).astype(BF16)


def next_step(*parts):
    keeps = parts[1::2]
    return pl.pallas_call(
        next_kernel,
        out_shape=[jax.ShapeDtypeStruct(k.shape, BF16) for k in keeps],
        in_specs=[VMEM] * 8,
        out_specs=[VMEM] * 4,
        compiler_params=params(),
    )(*parts)


def split_kernel(*refs):
    for group in range(2):
        own, from_low, from_high, last_low, last_high = refs[5 * group:5 * group + 5]
        outs = refs[10 + 4 * group:14 + 4 * group]
        size = own.shape[2] // 2
        low = own[0] + from_high[1].astype(F32) + last_low[...].astype(F32)
        high = own[1] + from_low[1].astype(F32) + last_high[...].astype(F32)
        blocks = (low[:, :size], low[:, size:], high[:, :size], high[:, size:])
        for block, out in zip(blocks, outs):
            out[...] = block.astype(out.dtype)


def split(*parts):
    shapes = []
    for own in parts[::5]:
        _, taps, rows, chan = own.shape
        shape = (taps, rows // 2, chan)
        shapes += [jax.ShapeDtypeStruct(shape, F32)] + [jax.ShapeDtypeStruct(shape, BF16)] * 3
    return pl.pallas_call(
        split_kernel,
        out_shape=shapes,
        in_specs=[VMEM] * 10,
        out_specs=[VMEM] * 8,
        compiler_params=params(),
    )(*parts)


def join_kernel(*refs):
    out = refs[-1]
    x = x_place()
    size = refs[0].shape[1]
    low = refs[0].shape[0]
    for piece, part, k in zip(refs, (0, 1) * RING, (0, 0, 3, 3, 1, 1, 2, 2)):
        at = pl.ds(pl.multiple_of(lax.rem(x + k, RING) * size, size), size)
        first = part * low
        out[first:first + piece.shape[0], at] = piece[...].astype(F32)


def gather_x(low, high):
    low_below, high_above = along_x(low, 1), along_x(high, -1)
    high_below, low_above = along_x(high.astype(BF16), 1), along_x(low.astype(BF16), -1)
    low_far, high_far = along_x(low_below, 1), along_x(high_above, -1)
    return low, high, low_below, high_below, low_above, high_above, low_far, high_far


def join(pieces):
    _, size, chan = pieces[0].shape
    return pl.pallas_call(
        join_kernel,
        out_shape=jax.ShapeDtypeStruct((27, RING * size, chan), F32),
        in_specs=[VMEM] * 8,
        out_specs=VMEM,
        compiler_params=params(),
    )(*pieces)


def body(pre_act, cot, weight):
    rows, width, depth, chan = pre_act.shape
    norm = 1.0 / math.sqrt(rows * lax.axis_size("gy") * width * lax.axis_size("gx") * depth)
    j = quad_place()
    barrier = lax.optimization_barrier

    count = lax.axis_size("gy")
    pairs = [(g, g + QUAD) for g in range(QUAD - 1, count - QUAD, QUAD)]
    pairs = pairs + [(g + QUAD, g) for g in range(0, count - QUAD, QUAD)]
    extra = lax.ppermute(jnp.where(j == 0, cot[0], cot[rows - 1]), "gy", pairs)
    act = jax.nn.silu(pre_act.astype(F32)).astype(BF16)
    far = swap(act, 2)
    near = swap(act, 1)
    extra, near, weight = barrier((extra, near, weight))
    above = along_y(weight, -1, True)
    below = along_y(weight, 1, True)
    even, odd = sides(cot, extra)
    quarters = pick_channels(cot, extra, swap_x(even, 0), swap_x(odd, 1))
    quarters = [quarters[0]] + [swap(quarters[k], k) for k in (1, 2, 3)]
    quarters, far = barrier((quarters, far))
    acts = [act, near, far, swap(far, 1)]
    quarters, above, below = barrier((quarters, above, below))
    taps = XTAPS
    parts = [weight, above, along_y(below[:taps], 1, True), along_y(above[taps:], -1, True), below]
    held, turned = turn(quarters)

    terms = weight_terms(norm, acts, turned)
    held, terms = barrier((held, terms))
    xup, xdown, xkeep_up, xkeep_down, xown = terms[:5]
    yup, ydown, ykeep_up, ykeep_down, yown = terms[5:]
    xlow, xhigh = along_x(xup, 1), along_x(xdown, -1)
    ylow, yhigh = along_y(yup, 1, True), along_y(ydown, -1, True)
    grads = input_terms(held, parts)
    grads, xlow, xhigh, ylow, yhigh = barrier((grads, xlow, xhigh, ylow, yhigh))
    send, keep, pass_on = grads
    got = swap(send, 1)
    xup, xdown, yup, ydown = next_step(
        xlow, xkeep_up, xhigh, xkeep_down, ylow, ykeep_up, yhigh, ykeep_down
    )
    xlast = along_x(xup, 1), along_x(xdown, -1)
    ylast = along_y(yup, 1, True), along_y(ydown, -1, True)
    xlast, ylast, got = barrier((xlast, ylast, got))
    blocks = split(xown, xlow, xhigh, *xlast, yown, ylow, yhigh, *ylast)

    low, high = blocks[0], blocks[4]
    lows = [along_y(block, r, True) for r, block in zip((1, 2, 3), blocks[1:4])]
    highs = [along_x(block, r) for r, block in zip((1, 2, 3), blocks[5:])]
    for other in lows:
        low = low + other.astype(F32)
    for other in highs:
        high = high + other.astype(F32)
    count = lax.axis_size("gx")
    mine = jnp.concatenate([low.astype(BF16), high.astype(BF16)])
    other = lax.ppermute(mine, "gx", [(g, g ^ 1) for g in range(count)])
    other, passed = barrier((other, (pass_on + got[1]).astype(BF16)))
    far_grad = swap(passed, 2)
    low, high = low + other[:taps].astype(F32), high + other[taps:].astype(F32)
    pieces = gather_x(low, high)
    grad_pre = finish(pre_act, keep, got, far_grad)
    grad_pre, pieces = barrier((grad_pre, pieces))
    return (grad_pre, join(pieces))


def solution(mesh):
    return jax.shard_map(
        body,
        mesh=mesh,
        in_specs=(P("gy", "gx", None, None), P("gy", "gx", None, None), P(None, "gy", None)),
        out_specs=(P("gy", "gx", None, None), P(None, "gy", None)),
        check_vma=False,
    )
```

```python
import functools
import math

import jax
import jax.numpy as jnp
from jax import lax
from jax.experimental import pallas as pl
from jax.experimental.pallas import tpu as pltpu
from jax.sharding import PartitionSpec as P

QUAD = 4
RING = 4
XTAPS = 13
F32 = jnp.float32
BF16 = jnp.bfloat16
ANY = pl.BlockSpec(memory_space=pl.ANY)
VMEM = pl.BlockSpec(memory_space=pltpu.VMEM)
LIMIT = 24 * 1024 * 1024


def params():
    return pltpu.CompilerParams(vmem_limit_bytes=LIMIT)


def small_cost():
    return pl.CostEstimate(flops=1000, bytes_accessed=1000, transcendentals=0)


def quad_place():
    return lax.rem(lax.axis_index("gy"), QUAD)


def x_place():
    return lax.div(lax.axis_index("gx"), 2)


def y_place():
    return lax.div(lax.axis_index("gy"), QUAD)


def swap(block, k):
    count = lax.axis_size("gy")
    return lax.ppermute(block, "gy", [(g, g ^ k) for g in range(count)])


def along_y(block, step, ring):
    count = lax.axis_size("gy")
    pairs = [(g, g + QUAD * step) for g in range(count)]
    if ring:
        pairs = [(s, t % count) for s, t in pairs]
    return lax.ppermute(block, "gy", [(s, t) for s, t in pairs if 0 <= t < count])


def along_x(block, step):
    count = lax.axis_size("gx")
    return lax.ppermute(block, "gx", [(g, (g + 2 * step) % count) for g in range(count)])


def swap_x(block, first):
    count = lax.axis_size("gx")
    pairs = [(g, g + 1) for g in range(first, count - 1, 2)]
    return lax.ppermute(block, "gx", pairs + [(t, s) for s, t in pairs])


def zero_at(value, z, edge):
    return jnp.where(z == edge, 0.0, value)


def pick(block, k):
    chan = block.shape[-1]
    q = chan // QUAD
    part = q // RING
    source = lax.broadcasted_iota(jnp.int32, (chan, q), 0)
    place = lax.broadcasted_iota(jnp.int32, (chan, q), 1)
    base = lax.div(place, part) * q + lax.rem(place, part) + (quad_place() ^ k) * part
    matrix = jnp.where(source == base, 1.0, 0.0).astype(BF16)
    got = jnp.dot(block.reshape(-1, chan), matrix, preferred_element_type=F32)
    return got.astype(BF16).reshape(block.shape[:-1] + (q,))


def own_kernel(cot, *quarters):
    for k, out in enumerate(quarters):
        out[...] = pick(cot[...], k)


def extra_kernel(extra, q0, q1, q2, q3, *quarters):
    for k, (own, out) in enumerate(zip((q0, q1, q2, q3), quarters)):
        rows = own.shape[0]
        out[0:rows] = own[...]
        out[rows] = pick(extra[...], k)


def quarters_of(kernel, rows, *ins):
    width, depth, chan = ins[0].shape[-3:]
    quarter = jax.ShapeDtypeStruct((rows, width, depth, chan // QUAD), BF16)
    return pl.pallas_call(
        kernel,
        out_shape=[quarter] * QUAD,
        in_specs=[VMEM] * len(ins),
        out_specs=[VMEM] * QUAD,
        compiler_params=params(),
        cost_estimate=pl.CostEstimate(
            flops=1000, bytes_accessed=40_000_000 if kernel is own_kernel else 1000, transcendentals=0
        ),
    )(*ins)


def side_kernel(p0, p1, p2, p3, even, odd):
    width = p0.shape[1]
    is_odd = lax.rem(lax.axis_index("gx"), 2) == 1
    for k, p in enumerate((p0, p1, p2, p3)):
        first, last = p[:, 0], p[:, width - 1]
        even[k] = jnp.where(is_odd, first, last)
        odd[k] = jnp.where(is_odd, last, first)


def sides(quarters):
    rows, _, depth, q = quarters[0].shape
    return pl.pallas_call(
        side_kernel,
        out_shape=[jax.ShapeDtypeStruct((QUAD, rows, depth, q), BF16)] * 2,
        in_specs=[VMEM] * QUAD,
        out_specs=[VMEM] * 2,
        compiler_params=params(),
        cost_estimate=small_cost(),
    )(*quarters)


def turn_kernel(p0, p1, p2, p3, even, odd, held, out):
    j, x = quad_place(), x_place()
    is_odd = lax.rem(lax.axis_index("gx"), 2) == 1
    for k, p in enumerate((p0, p1, p2, p3)):
        rows, width = p.shape[0] - 1, p.shape[1]
        low = jnp.where(is_odd, even[k], odd[k])
        high = jnp.where(is_odd, odd[k], even[k])

        def put(at, part):
            held[at, 1:width + 1] = p[part]
            held[at, 0] = low[part]
            held[at, width + 1] = high[part]

        put(pl.ds(1 + (j ^ k) * rows, rows), slice(0, rows))
        pl.when((j ^ k) == 0)(functools.partial(put, 0, rows))
        pl.when((j ^ k) == QUAD - 1)(functools.partial(put, held.shape[0] - 1, rows))

    tall, width, depth, q = held.shape
    width -= 2
    cells = tall * width * depth
    part = q // RING
    small = part // RING
    place = lax.broadcasted_iota(jnp.int32, (q, q), 0)
    source = lax.broadcasted_iota(jnp.int32, (q, q), 1)
    xpart = lax.rem(lax.div(place, part) + x, RING)
    ypart = lax.rem(lax.div(lax.rem(place, part), small) + y_place(), RING)
    base = ypart * part + xpart * small + lax.rem(place, small)
    order = jnp.where(source == base, 1.0, 0.0).astype(BF16)
    z = lax.rem(lax.broadcasted_iota(jnp.int32, (q, cells), 1), depth)
    for b in (-1, 0, 1):
        moved = held[:, 1 - b:1 - b + width].reshape(cells, q)
        value = lax.dot_general(
            order, moved, (((1,), (1,)), ((), ())), preferred_element_type=F32
        )
        high = zero_at(pltpu.roll(value, cells - 1, 1), z, depth - 1)
        low = zero_at(pltpu.roll(value, 1, 1), z, 0)
        for c, v in enumerate((high, value, low)):
            at = ((b + 1) * 3 + c) * q
            out[at:at + q] = v.astype(BF16)


def turn(quarters, even, odd):
    rows, width, depth, q = quarters[0].shape
    width += 2
    tall = QUAD * (rows - 1) + 2
    return pl.pallas_call(
        turn_kernel,
        out_shape=[
            jax.ShapeDtypeStruct((tall, width, depth, q), BF16),
            jax.ShapeDtypeStruct((9 * q, tall * (width - 2) * depth), BF16),
        ],
        in_specs=[VMEM] * (QUAD + 2),
        out_specs=[VMEM] * 2,
        compiler_params=params(),
        cost_estimate=small_cost(),
    )(*quarters, even, odd)


def run_copies(pairs, sem):
    copies = [pltpu.make_async_copy(s, d, sem.at[n]) for n, (s, d) in enumerate(pairs)]
    for c in copies:
        c.start()
    return copies


def weight_kernel(norm, own_act, near, far, across, cot, *refs):
    groups, held, sem = (refs[:5], refs[5:10]), *refs[10:]
    j = quad_place()
    rows, width, depth, chan = own_act.shape
    pairs = []
    for k, piece in enumerate((own_act, near, far, across)):
        pairs.append((piece, held.at[pl.ds((j ^ k) * rows, rows)]))
    for c in run_copies(pairs, sem):
        c.wait()
    row = width * depth
    cells = QUAD * rows * row
    act = held[...].reshape(cells, chan)
    q = cot.shape[0] // 9
    small = q // RING // RING
    for n in range(9):
        a, b = n // 3 - 1, n % 3
        moved = cot[3 * b * q:3 * (b + 1) * q, (1 - a) * row:(1 - a) * row + cells]
        term = jnp.dot(moved, act, preferred_element_type=F32) * norm
        for c in range(3):
            tap = 3 * n + c
            by_y = tap >= XTAPS
            up, down, keep_up, keep_down, own = groups[by_y]
            tap -= XTAPS * by_y

            def block(r, h):
                spots = [(2 * h, r), (2 * h + 1, r)] if by_y else [(r, 2 * h), (r, 2 * h + 1)]
                starts = [c * q + (xr * RING + yr) * small for xr, yr in spots]
                return jnp.concatenate([term[at:at + small] for at in starts], axis=0)

            up[0, tap] = block(2, 0).astype(BF16)
            down[0, tap] = block(2, 1).astype(BF16)
            keep_up[tap] = block(1, 0)
            up[1, tap] = block(1, 1).astype(BF16)
            down[1, tap] = block(3, 0).astype(BF16)
            keep_down[tap] = block(3, 1)
            own[0, tap] = block(0, 0)
            own[1, tap] = block(0, 1)


def weight_terms(norm, acts, cot):
    rows, width, depth, chan = acts[0].shape
    q = chan // QUAD
    cells = QUAD * rows * width * depth
    shapes = []
    for taps in (XTAPS, 27 - XTAPS):
        shape = (taps, q // RING // 2, chan)
        shapes += [jax.ShapeDtypeStruct((2,) + shape, BF16)] * 2
        shapes += [jax.ShapeDtypeStruct(shape, F32)] * 2
        shapes += [jax.ShapeDtypeStruct((2,) + shape, F32)]
    return pl.pallas_call(
        functools.partial(weight_kernel, norm),
        out_shape=shapes,
        in_specs=[ANY] * 4 + [VMEM],
        out_specs=[VMEM] * 10,
        scratch_shapes=[
            pltpu.VMEM((QUAD * rows, width, depth, chan), BF16),
            pltpu.SemaphoreType.DMA((4,)),
        ],
        compiler_params=params(),
        cost_estimate=pl.CostEstimate(
            flops=2 * 27 * q * cells * chan, bytes_accessed=10_000_000, transcendentals=0
        ),
    )(*acts, cot)


def input_kernel(held, own, above, across_low, across_high, below, *refs):
    send, keep, pass_on, weights, sem = refs
    j = quad_place()
    y = y_place()
    part = own.shape[1]
    low = across_low.shape[0]

    def at(s):
        return pl.ds(pl.multiple_of(lax.rem(y + s, RING) * part, part), part)

    pairs = [
        (own, weights.at[:, at(0)]),
        (above, weights.at[:, at(1)]),
        (across_low, weights.at[pl.ds(0, low), at(2)]),
        (across_high, weights.at[pl.ds(low, 27 - low), at(2)]),
        (below, weights.at[:, at(3)]),
    ]
    for c in run_copies(pairs, sem):
        c.wait()
    rows, width, depth, chan = keep.shape
    cells = rows * width * depth
    q = held.shape[3]
    taps = weights[...].reshape(9, 3, q, chan)
    for k, out in ((1, send.at[0]), (3, send.at[1]), (2, pass_on), (0, keep)):
        first = (j ^ k) * rows
        moved = []
        for n in range(9):
            a, b = n // 3 - 1, n % 3 - 1
            block = held[pl.ds(first + 1 - a, rows), 1 - b:1 - b + width]
            moved.append(block.reshape(cells, q))
        moved = jnp.concatenate(moved, axis=1)
        z = lax.rem(lax.broadcasted_iota(jnp.int32, (cells, chan), 0), depth)

        def term(c):
            return jnp.dot(moved, taps[:, c].reshape(9 * q, chan), preferred_element_type=F32)

        grad = term(1)
        grad = grad + zero_at(pltpu.roll(term(0), cells - 1, 0), z, depth - 1)
        grad = grad + zero_at(pltpu.roll(term(2), 1, 0), z, 0)
        out[...] = grad.reshape(rows, width, depth, chan)


def input_terms(held, parts):
    tall, width, depth, q = held.shape
    chan = QUAD * q
    block = ((tall - 2) // QUAD, width - 2, depth, chan)
    return pl.pallas_call(
        input_kernel,
        out_shape=[
            jax.ShapeDtypeStruct((2,) + block, F32),
            jax.ShapeDtypeStruct(block, F32),
            jax.ShapeDtypeStruct(block, F32),
        ],
        in_specs=[VMEM] + [ANY] * 5,
        out_specs=[VMEM] * 3,
        scratch_shapes=[pltpu.VMEM((27, q, chan), BF16), pltpu.SemaphoreType.DMA((5,))],
        compiler_params=params(),
        cost_estimate=pl.CostEstimate(
            flops=2 * 27 * tall * width * depth * q * chan, bytes_accessed=10_000_000, transcendentals=0
        ),
    )(held, *parts)


def finish_kernel(pre, keep, near, far, out):
    value = pre[...].astype(F32)
    s = jax.nn.sigmoid(value)
    grad = keep[...] + near[0] + far[...].astype(F32)
    out[...] = (grad * s * (1.0 + value * (1.0 - s))).astype(BF16)


def finish(pre_act, keep, near, far):
    return pl.pallas_call(
        finish_kernel,
        out_shape=jax.ShapeDtypeStruct(pre_act.shape, BF16),
        in_specs=[VMEM] * 4,
        out_specs=VMEM,
        compiler_params=params(),
    )(pre_act, keep, near, far)


def next_kernel(*refs):
    for n, out in enumerate(refs[8:]):
        came, keep = refs[2 * n:2 * n + 2]
        out[...] = (came[0].astype(F32) + keep[...]).astype(BF16)


def next_step(*parts):
    keeps = parts[1::2]
    return pl.pallas_call(
        next_kernel,
        out_shape=[jax.ShapeDtypeStruct(k.shape, BF16) for k in keeps],
        in_specs=[VMEM] * 8,
        out_specs=[VMEM] * 4,
        compiler_params=params(),
    )(*parts)


def split_kernel(*refs):
    for group in range(2):
        own, from_low, from_high, last_low, last_high = refs[5 * group:5 * group + 5]
        outs = refs[10 + 4 * group:14 + 4 * group]
        size = own.shape[2] // 2
        low = own[0] + from_high[1].astype(F32) + last_low[...].astype(F32)
        high = own[1] + from_low[1].astype(F32) + last_high[...].astype(F32)
        blocks = (low[:, :size], low[:, size:], high[:, :size], high[:, size:])
        for block, out in zip(blocks, outs):
            out[...] = block.astype(out.dtype)


def split(*parts):
    shapes = []
    for own in parts[::5]:
        _, taps, rows, chan = own.shape
        shape = (taps, rows // 2, chan)
        shapes += [jax.ShapeDtypeStruct(shape, F32)] + [jax.ShapeDtypeStruct(shape, BF16)] * 3
    return pl.pallas_call(
        split_kernel,
        out_shape=shapes,
        in_specs=[VMEM] * 10,
        out_specs=[VMEM] * 8,
        compiler_params=params(),
    )(*parts)


def join_kernel(*refs):
    out = refs[-1]
    x = x_place()
    size = refs[0].shape[1]
    low = refs[0].shape[0]
    for piece, part, k in zip(refs, (0, 1) * RING, (0, 0, 3, 3, 1, 1, 2, 2)):
        at = pl.ds(pl.multiple_of(lax.rem(x + k, RING) * size, size), size)
        first = part * low
        out[first:first + piece.shape[0], at] = piece[...].astype(F32)


def gather_x(low, high):
    low_below, high_above = along_x(low.astype(BF16), 1), along_x(high.astype(BF16), -1)
    high_below, low_above = along_x(high, 1), along_x(low, -1)
    low_far, high_far = along_x(low_below, 1), along_x(high_above, -1)
    return low, high, low_below, high_below, low_above, high_above, low_far, high_far


def join(pieces):
    _, size, chan = pieces[0].shape
    return pl.pallas_call(
        join_kernel,
        out_shape=jax.ShapeDtypeStruct((27, RING * size, chan), F32),
        in_specs=[VMEM] * 8,
        out_specs=VMEM,
        compiler_params=params(),
    )(*pieces)


def body(pre_act, cot, weight):
    rows, width, depth, chan = pre_act.shape
    norm = 1.0 / math.sqrt(rows * lax.axis_size("gy") * width * lax.axis_size("gx") * depth)
    j = quad_place()
    barrier = lax.optimization_barrier

    count = lax.axis_size("gy")
    pairs = [(g, g + 1) for g in range(QUAD - 1, count - 1, QUAD)]
    pairs = pairs + [(t, s) for s, t in pairs]
    extra = lax.ppermute(jnp.where(j == 0, cot[0], cot[rows - 1]), "gy", pairs)
    act = jax.nn.silu(pre_act.astype(F32)).astype(BF16)
    far = swap(act, 2)
    near = swap(act, 1)
    own_quarters = quarters_of(own_kernel, rows, cot)
    extra, near, own_quarters = barrier((extra, near, own_quarters))
    quarters = quarters_of(extra_kernel, rows + 1, extra, *own_quarters)
    quarters, weight = barrier((quarters, weight))
    above = along_y(weight, -1, True)
    below = along_y(weight, 1, True)
    quarters = [quarters[0]] + [swap(quarters[k], k) for k in (1, 2, 3)]
    quarters, far = barrier((quarters, far))
    acts = [act, near, far, swap(far, 1)]
    even, odd = sides(quarters)
    even, odd = swap_x(even, 0), swap_x(odd, 1)
    even, odd, above, below = barrier((even, odd, above, below))
    taps = XTAPS
    parts = [weight, above, along_y(below[:taps], 1, True), along_y(above[taps:], -1, True), below]
    held, turned = turn(quarters, even, odd)

    terms = weight_terms(norm, acts, turned)
    held, terms = barrier((held, terms))
    xup, xdown, xkeep_up, xkeep_down, xown = terms[:5]
    yup, ydown, ykeep_up, ykeep_down, yown = terms[5:]
    xlow, xhigh = along_x(xup, 1), along_x(xdown, -1)
    ylow, yhigh = along_y(yup, 1, True), along_y(ydown, -1, True)
    grads = input_terms(held, parts)
    grads, xlow, xhigh, ylow, yhigh = barrier((grads, xlow, xhigh, ylow, yhigh))
    send, keep, pass_on = grads
    got = swap(send, 1)
    xup, xdown, yup, ydown = next_step(
        xlow, xkeep_up, xhigh, xkeep_down, ylow, ykeep_up, yhigh, ykeep_down
    )
    xlast = along_x(xup, 1), along_x(xdown, -1)
    ylast = along_y(yup, 1, True), along_y(ydown, -1, True)
    xlast, ylast, got = barrier((xlast, ylast, got))
    blocks = split(xown, xlow, xhigh, *xlast, yown, ylow, yhigh, *ylast)

    low, high = blocks[0], blocks[4]
    lows = [along_y(block, r, True) for r, block in zip((1, 2, 3), blocks[1:4])]
    highs = [along_x(block, r) for r, block in zip((1, 2, 3), blocks[5:])]
    for other in lows:
        low = low + other.astype(F32)
    for other in highs:
        high = high + other.astype(F32)
    count = lax.axis_size("gx")
    mine = jnp.concatenate([low.astype(BF16), high.astype(BF16)])
    other = lax.ppermute(mine, "gx", [(g, g ^ 1) for g in range(count)])
    other, passed = barrier((other, (pass_on + got[1]).astype(BF16)))
    far_grad = swap(passed, 2)
    low, high = low + other[:taps].astype(F32), high + other[taps:].astype(F32)
    pieces = gather_x(low, high)
    grad_pre = finish(pre_act, keep, got, far_grad)
    grad_pre, pieces = barrier((grad_pre, pieces))
    return (grad_pre, join(pieces))


def solution(mesh):
    return jax.shard_map(
        body,
        mesh=mesh,
        in_specs=(P("gy", "gx", None, None), P("gy", "gx", None, None), P(None, "gy", None)),
        out_specs=(P("gy", "gx", None, None), P(None, "gy", None)),
        check_vma=False,
    )
```

```python
import functools
import math

import jax
import jax.numpy as jnp
from jax import lax
from jax.experimental import pallas as pl
from jax.experimental.pallas import tpu as pltpu
from jax.sharding import PartitionSpec as P

QUAD = 4
RING = 4
XTAPS = 13
F32 = jnp.float32
BF16 = jnp.bfloat16
ANY = pl.BlockSpec(memory_space=pl.ANY)
VMEM = pl.BlockSpec(memory_space=pltpu.VMEM)
LIMIT = 24 * 1024 * 1024


def params():
    return pltpu.CompilerParams(vmem_limit_bytes=LIMIT)


def small_cost():
    return pl.CostEstimate(flops=1000, bytes_accessed=1000, transcendentals=0)


def quad_place():
    return lax.rem(lax.axis_index("gy"), QUAD)


def x_place():
    return lax.div(lax.axis_index("gx"), 2)


def y_place():
    return lax.div(lax.axis_index("gy"), QUAD)


def swap(block, k):
    count = lax.axis_size("gy")
    return lax.ppermute(block, "gy", [(g, g ^ k) for g in range(count)])


def along_y(block, step, ring):
    count = lax.axis_size("gy")
    pairs = [(g, g + QUAD * step) for g in range(count)]
    if ring:
        pairs = [(s, t % count) for s, t in pairs]
    return lax.ppermute(block, "gy", [(s, t) for s, t in pairs if 0 <= t < count])


def along_x(block, step):
    count = lax.axis_size("gx")
    return lax.ppermute(block, "gx", [(g, (g + 2 * step) % count) for g in range(count)])


def swap_x(block, first):
    count = lax.axis_size("gx")
    pairs = [(g, g + 1) for g in range(first, count - 1, 2)]
    return lax.ppermute(block, "gx", pairs + [(t, s) for s, t in pairs])


def zero_at(value, z, edge):
    return jnp.where(z == edge, 0.0, value)


def pick(block, k):
    chan = block.shape[-1]
    q = chan // QUAD
    part = q // RING
    source = lax.broadcasted_iota(jnp.int32, (chan, q), 0)
    place = lax.broadcasted_iota(jnp.int32, (chan, q), 1)
    base = lax.div(place, part) * q + lax.rem(place, part) + (quad_place() ^ k) * part
    matrix = jnp.where(source == base, 1.0, 0.0).astype(BF16)
    got = jnp.dot(block.reshape(-1, chan), matrix, preferred_element_type=F32)
    return got.astype(BF16).reshape(block.shape[:-1] + (q,))


def own_kernel(cot, *quarters):
    for k, out in enumerate(quarters):
        out[...] = pick(cot[...], k)


def extra_kernel(extra, q0, q1, q2, q3, *quarters):
    for k, (own, out) in enumerate(zip((q0, q1, q2, q3), quarters)):
        rows = own.shape[0]
        out[0:rows] = own[...]
        out[rows] = pick(extra[...], k)


def quarters_of(kernel, rows, *ins):
    width, depth, chan = ins[0].shape[-3:]
    quarter = jax.ShapeDtypeStruct((rows, width, depth, chan // QUAD), BF16)
    return pl.pallas_call(
        kernel,
        out_shape=[quarter] * QUAD,
        in_specs=[VMEM] * len(ins),
        out_specs=[VMEM] * QUAD,
        compiler_params=params(),
        cost_estimate=pl.CostEstimate(
            flops=1000, bytes_accessed=40_000_000 if kernel is own_kernel else 1000, transcendentals=0
        ),
    )(*ins)


def side_kernel(p0, p1, p2, p3, even, odd):
    width = p0.shape[1]
    is_odd = lax.rem(lax.axis_index("gx"), 2) == 1
    for k, p in enumerate((p0, p1, p2, p3)):
        first, last = p[:, 0], p[:, width - 1]
        even[k] = jnp.where(is_odd, first, last)
        odd[k] = jnp.where(is_odd, last, first)


def sides(quarters):
    rows, _, depth, q = quarters[0].shape
    return pl.pallas_call(
        side_kernel,
        out_shape=[jax.ShapeDtypeStruct((QUAD, rows, depth, q), BF16)] * 2,
        in_specs=[VMEM] * QUAD,
        out_specs=[VMEM] * 2,
        compiler_params=params(),
        cost_estimate=small_cost(),
    )(*quarters)


def turn_kernel(p0, p1, p2, p3, even, odd, held, out):
    j, x = quad_place(), x_place()
    is_odd = lax.rem(lax.axis_index("gx"), 2) == 1
    for k, p in enumerate((p0, p1, p2, p3)):
        rows, width = p.shape[0] - 1, p.shape[1]
        low = jnp.where(is_odd, even[k], odd[k])
        high = jnp.where(is_odd, odd[k], even[k])

        def put(at, part):
            held[at, 1:width + 1] = p[part]
            held[at, 0] = low[part]
            held[at, width + 1] = high[part]

        put(pl.ds(1 + (j ^ k) * rows, rows), slice(0, rows))
        pl.when((j ^ k) == 0)(functools.partial(put, 0, rows))
        pl.when((j ^ k) == QUAD - 1)(functools.partial(put, held.shape[0] - 1, rows))

    tall, width, depth, q = held.shape
    width -= 2
    cells = tall * width * depth
    part = q // RING
    small = part // RING
    place = lax.broadcasted_iota(jnp.int32, (q, q), 0)
    source = lax.broadcasted_iota(jnp.int32, (q, q), 1)
    xpart = lax.rem(lax.div(place, part) + x, RING)
    ypart = lax.rem(lax.div(lax.rem(place, part), small) + y_place(), RING)
    base = ypart * part + xpart * small + lax.rem(place, small)
    order = jnp.where(source == base, 1.0, 0.0).astype(BF16)
    z = lax.rem(lax.broadcasted_iota(jnp.int32, (q, cells), 1), depth)
    for b in (-1, 0, 1):
        moved = held[:, 1 - b:1 - b + width].reshape(cells, q)
        value = lax.dot_general(
            order, moved, (((1,), (1,)), ((), ())), preferred_element_type=F32
        )
        high = zero_at(pltpu.roll(value, cells - 1, 1), z, depth - 1)
        low = zero_at(pltpu.roll(value, 1, 1), z, 0)
        for c, v in enumerate((high, value, low)):
            at = ((b + 1) * 3 + c) * q
            out[at:at + q] = v.astype(BF16)


def turn(quarters, even, odd):
    rows, width, depth, q = quarters[0].shape
    width += 2
    tall = QUAD * (rows - 1) + 2
    return pl.pallas_call(
        turn_kernel,
        out_shape=[
            jax.ShapeDtypeStruct((tall, width, depth, q), BF16),
            jax.ShapeDtypeStruct((9 * q, tall * (width - 2) * depth), BF16),
        ],
        in_specs=[VMEM] * (QUAD + 2),
        out_specs=[VMEM] * 2,
        compiler_params=params(),
        cost_estimate=small_cost(),
    )(*quarters, even, odd)


def run_copies(pairs, sem):
    copies = [pltpu.make_async_copy(s, d, sem.at[n]) for n, (s, d) in enumerate(pairs)]
    for c in copies:
        c.start()
    return copies


def weight_kernel(norm, own_act, near, far, across, cot, *refs):
    groups, held, sem = (refs[:5], refs[5:10]), *refs[10:]
    j = quad_place()
    rows, width, depth, chan = own_act.shape
    pairs = []
    for k, piece in enumerate((own_act, near, far, across)):
        pairs.append((piece, held.at[pl.ds((j ^ k) * rows, rows)]))
    for c in run_copies(pairs, sem):
        c.wait()
    row = width * depth
    cells = QUAD * rows * row
    act = held[...].reshape(cells, chan)
    q = cot.shape[0] // 9
    small = q // RING // RING
    for n in range(9):
        a, b = n // 3 - 1, n % 3
        moved = cot[3 * b * q:3 * (b + 1) * q, (1 - a) * row:(1 - a) * row + cells]
        term = jnp.dot(moved, act, preferred_element_type=F32) * norm
        for c in range(3):
            tap = 3 * n + c
            by_y = tap >= XTAPS
            up, down, keep_up, keep_down, own = groups[by_y]
            tap -= XTAPS * by_y

            def block(r, h):
                spots = [(2 * h, r), (2 * h + 1, r)] if by_y else [(r, 2 * h), (r, 2 * h + 1)]
                starts = [c * q + (xr * RING + yr) * small for xr, yr in spots]
                return jnp.concatenate([term[at:at + small] for at in starts], axis=0)

            up[0, tap] = block(2, 0).astype(BF16)
            down[0, tap] = block(2, 1).astype(BF16)
            keep_up[tap] = block(1, 0)
            up[1, tap] = block(1, 1).astype(BF16)
            down[1, tap] = block(3, 0).astype(BF16)
            keep_down[tap] = block(3, 1)
            own[0, tap] = block(0, 0)
            own[1, tap] = block(0, 1)


def weight_terms(norm, acts, cot):
    rows, width, depth, chan = acts[0].shape
    q = chan // QUAD
    cells = QUAD * rows * width * depth
    shapes = []
    for taps in (XTAPS, 27 - XTAPS):
        shape = (taps, q // RING // 2, chan)
        shapes += [jax.ShapeDtypeStruct((2,) + shape, BF16)] * 2
        shapes += [jax.ShapeDtypeStruct(shape, F32)] * 2
        shapes += [jax.ShapeDtypeStruct((2,) + shape, F32)]
    return pl.pallas_call(
        functools.partial(weight_kernel, norm),
        out_shape=shapes,
        in_specs=[ANY] * 4 + [VMEM],
        out_specs=[VMEM] * 10,
        scratch_shapes=[
            pltpu.VMEM((QUAD * rows, width, depth, chan), BF16),
            pltpu.SemaphoreType.DMA((4,)),
        ],
        compiler_params=params(),
        cost_estimate=pl.CostEstimate(
            flops=2 * 27 * q * cells * chan, bytes_accessed=10_000_000, transcendentals=0
        ),
    )(*acts, cot)


def input_kernel(held, own, above, across_low, across_high, below, *refs):
    send, keep, pass_on, weights, sem = refs
    j = quad_place()
    y = y_place()
    part = own.shape[1]
    low = across_low.shape[0]

    def at(s):
        return pl.ds(pl.multiple_of(lax.rem(y + s, RING) * part, part), part)

    pairs = [
        (own, weights.at[:, at(0)]),
        (above, weights.at[:, at(1)]),
        (across_low, weights.at[pl.ds(0, low), at(2)]),
        (across_high, weights.at[pl.ds(low, 27 - low), at(2)]),
        (below, weights.at[:, at(3)]),
    ]
    for c in run_copies(pairs, sem):
        c.wait()
    rows, width, depth, chan = keep.shape
    cells = rows * width * depth
    q = held.shape[3]
    taps = weights[...].reshape(9, 3, q, chan)
    for k, out in ((1, send.at[0]), (3, send.at[1]), (2, pass_on), (0, keep)):
        first = (j ^ k) * rows
        moved = []
        for n in range(9):
            a, b = n // 3 - 1, n % 3 - 1
            block = held[pl.ds(first + 1 - a, rows), 1 - b:1 - b + width]
            moved.append(block.reshape(cells, q))
        moved = jnp.concatenate(moved, axis=1)
        z = lax.rem(lax.broadcasted_iota(jnp.int32, (cells, chan), 0), depth)

        def term(c):
            return jnp.dot(moved, taps[:, c].reshape(9 * q, chan), preferred_element_type=F32)

        grad = term(1)
        grad = grad + zero_at(pltpu.roll(term(0), cells - 1, 0), z, depth - 1)
        grad = grad + zero_at(pltpu.roll(term(2), 1, 0), z, 0)
        out[...] = grad.reshape(rows, width, depth, chan)


def input_terms(held, parts):
    tall, width, depth, q = held.shape
    chan = QUAD * q
    block = ((tall - 2) // QUAD, width - 2, depth, chan)
    return pl.pallas_call(
        input_kernel,
        out_shape=[
            jax.ShapeDtypeStruct((2,) + block, F32),
            jax.ShapeDtypeStruct(block, F32),
            jax.ShapeDtypeStruct(block, F32),
        ],
        in_specs=[VMEM] + [ANY] * 5,
        out_specs=[VMEM] * 3,
        scratch_shapes=[pltpu.VMEM((27, q, chan), BF16), pltpu.SemaphoreType.DMA((5,))],
        compiler_params=params(),
        cost_estimate=pl.CostEstimate(
            flops=2 * 27 * tall * width * depth * q * chan, bytes_accessed=10_000_000, transcendentals=0
        ),
    )(held, *parts)


def finish_kernel(pre, keep, near, far, out):
    value = pre[...].astype(F32)
    s = jax.nn.sigmoid(value)
    grad = keep[...] + near[0] + far[...].astype(F32)
    out[...] = (grad * s * (1.0 + value * (1.0 - s))).astype(BF16)


def finish(pre_act, keep, near, far):
    return pl.pallas_call(
        finish_kernel,
        out_shape=jax.ShapeDtypeStruct(pre_act.shape, BF16),
        in_specs=[VMEM] * 4,
        out_specs=VMEM,
        compiler_params=params(),
    )(pre_act, keep, near, far)


def next_kernel(*refs):
    for n, out in enumerate(refs[8:]):
        came, keep = refs[2 * n:2 * n + 2]
        out[...] = (came[0].astype(F32) + keep[...]).astype(BF16)


def next_step(*parts):
    keeps = parts[1::2]
    return pl.pallas_call(
        next_kernel,
        out_shape=[jax.ShapeDtypeStruct(k.shape, BF16) for k in keeps],
        in_specs=[VMEM] * 8,
        out_specs=[VMEM] * 4,
        compiler_params=params(),
    )(*parts)


def split_kernel(*refs):
    for group in range(2):
        own, from_low, from_high, last_low, last_high = refs[5 * group:5 * group + 5]
        outs = refs[10 + 4 * group:14 + 4 * group]
        size = own.shape[2] // 2
        low = own[0] + from_high[1].astype(F32) + last_low[...].astype(F32)
        high = own[1] + from_low[1].astype(F32) + last_high[...].astype(F32)
        blocks = (low[:, :size], low[:, size:], high[:, :size], high[:, size:])
        for block, out in zip(blocks, outs):
            out[...] = block.astype(out.dtype)


def split(*parts):
    shapes = []
    for own in parts[::5]:
        _, taps, rows, chan = own.shape
        shape = (taps, rows // 2, chan)
        shapes += [jax.ShapeDtypeStruct(shape, F32)] + [jax.ShapeDtypeStruct(shape, BF16)] * 3
    return pl.pallas_call(
        split_kernel,
        out_shape=shapes,
        in_specs=[VMEM] * 10,
        out_specs=[VMEM] * 8,
        compiler_params=params(),
    )(*parts)


def join_kernel(*refs):
    out = refs[-1]
    x = x_place()
    size = refs[0].shape[1]
    low = refs[0].shape[0]
    for piece, part, k in zip(refs, (0, 1) * RING, (0, 0, 3, 3, 1, 1, 2, 2)):
        at = pl.ds(pl.multiple_of(lax.rem(x + k, RING) * size, size), size)
        first = part * low
        out[first:first + piece.shape[0], at] = piece[...].astype(F32)


def gather_x(low, high):
    low_below, high_above = along_x(low.astype(BF16), 1), along_x(high.astype(BF16), -1)
    high_below, low_above = along_x(high, 1), along_x(low, -1)
    low_far, high_far = along_x(low_below, 1), along_x(high_above, -1)
    return low, high, low_below, high_below, low_above, high_above, low_far, high_far


def join(pieces):
    _, size, chan = pieces[0].shape
    return pl.pallas_call(
        join_kernel,
        out_shape=jax.ShapeDtypeStruct((27, RING * size, chan), F32),
        in_specs=[VMEM] * 8,
        out_specs=VMEM,
        compiler_params=params(),
    )(*pieces)


def body(pre_act, cot, weight):
    rows, width, depth, chan = pre_act.shape
    norm = 1.0 / math.sqrt(rows * lax.axis_size("gy") * width * lax.axis_size("gx") * depth)
    j = quad_place()
    barrier = lax.optimization_barrier

    count = lax.axis_size("gy")
    pairs = [(g, g + 1) for g in range(QUAD - 1, count - 1, QUAD)]
    pairs = pairs + [(t, s) for s, t in pairs]
    extra = lax.ppermute(jnp.where(j == 0, cot[0], cot[rows - 1]), "gy", pairs)
    act = jax.nn.silu(pre_act.astype(F32)).astype(BF16)
    far = swap(act, 2)
    near = swap(act, 1)
    own_quarters = quarters_of(own_kernel, rows, cot)
    extra, near, own_quarters = barrier((extra, near, own_quarters))
    quarters = quarters_of(extra_kernel, rows + 1, extra, *own_quarters)
    quarters, weight = barrier((quarters, weight))
    above = along_y(weight, -1, True)
    below = along_y(weight, 1, True)
    quarters = [quarters[0]] + [swap(quarters[k], k) for k in (1, 2, 3)]
    quarters, far = barrier((quarters, far))
    acts = [act, near, far, swap(far, 1)]
    even, odd = sides(quarters)
    odd, even = swap_x(odd, 1), swap_x(even, 0)
    odd, even, above, below = barrier((odd, even, above, below))
    taps = XTAPS
    parts = [weight, above, along_y(below[:taps], 1, True), along_y(above[taps:], -1, True), below]
    held, turned = turn(quarters, even, odd)

    terms = weight_terms(norm, acts, turned)
    held, terms = barrier((held, terms))
    xup, xdown, xkeep_up, xkeep_down, xown = terms[:5]
    yup, ydown, ykeep_up, ykeep_down, yown = terms[5:]
    xlow, xhigh = along_x(xup, 1), along_x(xdown, -1)
    ylow, yhigh = along_y(yup, 1, True), along_y(ydown, -1, True)
    grads = input_terms(held, parts)
    grads, xlow, xhigh, ylow, yhigh = barrier((grads, xlow, xhigh, ylow, yhigh))
    send, keep, pass_on = grads
    got = swap(send, 1)
    xup, xdown, yup, ydown = next_step(
        xlow, xkeep_up, xhigh, xkeep_down, ylow, ykeep_up, yhigh, ykeep_down
    )
    xlast = along_x(xup, 1), along_x(xdown, -1)
    ylast = along_y(yup, 1, True), along_y(ydown, -1, True)
    xlast, ylast, got = barrier((xlast, ylast, got))
    blocks = split(xown, xlow, xhigh, *xlast, yown, ylow, yhigh, *ylast)

    low, high = blocks[0], blocks[4]
    lows = [along_y(block, r, True) for r, block in zip((1, 2, 3), blocks[1:4])]
    highs = [along_x(block, r) for r, block in zip((1, 2, 3), blocks[5:])]
    for other in lows:
        low = low + other.astype(F32)
    for other in highs:
        high = high + other.astype(F32)
    count = lax.axis_size("gx")
    mine = jnp.concatenate([low.astype(BF16), high.astype(BF16)])
    other = lax.ppermute(mine, "gx", [(g, g ^ 1) for g in range(count)])
    other, passed = barrier((other, (pass_on + got[1]).astype(BF16)))
    far_grad = swap(passed, 2)
    low, high = low + other[:taps].astype(F32), high + other[taps:].astype(F32)
    pieces = gather_x(low, high)
    grad_pre = finish(pre_act, keep, got, far_grad)
    grad_pre, pieces = barrier((grad_pre, pieces))
    return (grad_pre, join(pieces))


def solution(mesh):
    return jax.shard_map(
        body,
        mesh=mesh,
        in_specs=(P("gy", "gx", None, None), P("gy", "gx", None, None), P(None, "gy", None)),
        out_specs=(P("gy", "gx", None, None), P(None, "gy", None)),
        check_vma=False,
    )
```

```python
import functools
import math

import jax
import jax.numpy as jnp
from jax import lax
from jax.experimental import pallas as pl
from jax.experimental.pallas import tpu as pltpu
from jax.sharding import PartitionSpec as P

QUAD = 4
RING = 4
XTAPS = 13
F32 = jnp.float32
BF16 = jnp.bfloat16
ANY = pl.BlockSpec(memory_space=pl.ANY)
VMEM = pl.BlockSpec(memory_space=pltpu.VMEM)
LIMIT = 24 * 1024 * 1024


def params():
    return pltpu.CompilerParams(vmem_limit_bytes=LIMIT)


def small_cost():
    return pl.CostEstimate(flops=1000, bytes_accessed=1000, transcendentals=0)


def quad_place():
    return lax.rem(lax.axis_index("gy"), QUAD)


def x_place():
    return lax.div(lax.axis_index("gx"), 2)


def y_place():
    return lax.div(lax.axis_index("gy"), QUAD)


def swap(block, k):
    count = lax.axis_size("gy")
    return lax.ppermute(block, "gy", [(g, g ^ k) for g in range(count)])


def along_y(block, step, ring):
    count = lax.axis_size("gy")
    pairs = [(g, g + QUAD * step) for g in range(count)]
    if ring:
        pairs = [(s, t % count) for s, t in pairs]
    return lax.ppermute(block, "gy", [(s, t) for s, t in pairs if 0 <= t < count])


def along_x(block, step):
    count = lax.axis_size("gx")
    return lax.ppermute(block, "gx", [(g, (g + 2 * step) % count) for g in range(count)])


def swap_x(block, first):
    count = lax.axis_size("gx")
    pairs = [(g, g + 1) for g in range(first, count - 1, 2)]
    return lax.ppermute(block, "gx", pairs + [(t, s) for s, t in pairs])


def zero_at(value, z, edge):
    return jnp.where(z == edge, 0.0, value)


def pick(block, k):
    chan = block.shape[-1]
    q = chan // QUAD
    part = q // RING
    source = lax.broadcasted_iota(jnp.int32, (chan, q), 0)
    place = lax.broadcasted_iota(jnp.int32, (chan, q), 1)
    base = lax.div(place, part) * q + lax.rem(place, part) + (quad_place() ^ k) * part
    matrix = jnp.where(source == base, 1.0, 0.0).astype(BF16)
    got = jnp.dot(block.reshape(-1, chan), matrix, preferred_element_type=F32)
    return got.astype(BF16).reshape(block.shape[:-1] + (q,))


def own_kernel(cot, *quarters):
    for k, out in enumerate(quarters):
        out[...] = pick(cot[...], k)


def extra_kernel(extra, q0, q1, q2, q3, *quarters):
    for k, (own, out) in enumerate(zip((q0, q1, q2, q3), quarters)):
        rows = own.shape[0]
        out[0:rows] = own[...]
        out[rows] = pick(extra[...], k)


def quarters_of(kernel, rows, *ins):
    width, depth, chan = ins[0].shape[-3:]
    quarter = jax.ShapeDtypeStruct((rows, width, depth, chan // QUAD), BF16)
    return pl.pallas_call(
        kernel,
        out_shape=[quarter] * QUAD,
        in_specs=[VMEM] * len(ins),
        out_specs=[VMEM] * QUAD,
        compiler_params=params(),
        cost_estimate=pl.CostEstimate(
            flops=1000, bytes_accessed=40_000_000 if kernel is own_kernel else 1000, transcendentals=0
        ),
    )(*ins)


def side_kernel(p0, p1, p2, p3, even, odd):
    width = p0.shape[1]
    is_odd = lax.rem(lax.axis_index("gx"), 2) == 1
    for k, p in enumerate((p0, p1, p2, p3)):
        first, last = p[:, 0], p[:, width - 1]
        even[k] = jnp.where(is_odd, first, last)
        odd[k] = jnp.where(is_odd, last, first)


def sides(quarters):
    rows, _, depth, q = quarters[0].shape
    return pl.pallas_call(
        side_kernel,
        out_shape=[jax.ShapeDtypeStruct((QUAD, rows, depth, q), BF16)] * 2,
        in_specs=[VMEM] * QUAD,
        out_specs=[VMEM] * 2,
        compiler_params=params(),
        cost_estimate=small_cost(),
    )(*quarters)


def turn(p0, p1, p2, p3, even, odd, held, out):
    j, x = quad_place(), x_place()
    is_odd = lax.rem(lax.axis_index("gx"), 2) == 1
    for k, p in enumerate((p0, p1, p2, p3)):
        rows, width = p.shape[0] - 1, p.shape[1]
        low = jnp.where(is_odd, even[k], odd[k])
        high = jnp.where(is_odd, odd[k], even[k])

        def put(at, part):
            held[at, 1:width + 1] = p[part]
            held[at, 0] = low[part]
            held[at, width + 1] = high[part]

        put(pl.ds(1 + (j ^ k) * rows, rows), slice(0, rows))
        pl.when((j ^ k) == 0)(functools.partial(put, 0, rows))
        pl.when((j ^ k) == QUAD - 1)(functools.partial(put, held.shape[0] - 1, rows))

    tall, width, depth, q = held.shape
    width -= 2
    cells = tall * width * depth
    part = q // RING
    small = part // RING
    place = lax.broadcasted_iota(jnp.int32, (q, q), 0)
    source = lax.broadcasted_iota(jnp.int32, (q, q), 1)
    xpart = lax.rem(lax.div(place, part) + x, RING)
    ypart = lax.rem(lax.div(lax.rem(place, part), small) + y_place(), RING)
    base = ypart * part + xpart * small + lax.rem(place, small)
    order = jnp.where(source == base, 1.0, 0.0).astype(BF16)
    z = lax.rem(lax.broadcasted_iota(jnp.int32, (q, cells), 1), depth)
    for b in (-1, 0, 1):
        moved = held[:, 1 - b:1 - b + width].reshape(cells, q)
        value = lax.dot_general(
            order, moved, (((1,), (1,)), ((), ())), preferred_element_type=F32
        )
        high = zero_at(pltpu.roll(value, cells - 1, 1), z, depth - 1)
        low = zero_at(pltpu.roll(value, 1, 1), z, 0)
        for c, v in enumerate((high, value, low)):
            at = ((b + 1) * 3 + c) * q
            out[at:at + q] = v.astype(BF16)


def run_copies(pairs, sem):
    copies = [pltpu.make_async_copy(s, d, sem.at[n]) for n, (s, d) in enumerate(pairs)]
    for c in copies:
        c.start()
    return copies


def weight_kernel(norm, own_act, near, far, across, *refs):
    quarters, cells_out, groups = refs[:6], refs[6], (refs[7:12], refs[12:17])
    held, cot, sem = refs[17:]
    j = quad_place()
    rows, width, depth, chan = own_act.shape
    pairs = []
    for k, piece in enumerate((own_act, near, far, across)):
        pairs.append((piece, held.at[pl.ds((j ^ k) * rows, rows)]))
    copies = run_copies(pairs, sem)
    turn(*quarters, cells_out, cot)
    for c in copies:
        c.wait()
    row = width * depth
    cells = QUAD * rows * row
    act = held[...].reshape(cells, chan)
    q = cot.shape[0] // 9
    small = q // RING // RING
    for n in range(9):
        a, b = n // 3 - 1, n % 3
        moved = cot[3 * b * q:3 * (b + 1) * q, (1 - a) * row:(1 - a) * row + cells]
        term = jnp.dot(moved, act, preferred_element_type=F32) * norm
        for c in range(3):
            tap = 3 * n + c
            by_y = tap >= XTAPS
            up, down, keep_up, keep_down, own = groups[by_y]
            tap -= XTAPS * by_y

            def block(r, h):
                spots = [(2 * h, r), (2 * h + 1, r)] if by_y else [(r, 2 * h), (r, 2 * h + 1)]
                starts = [c * q + (xr * RING + yr) * small for xr, yr in spots]
                return jnp.concatenate([term[at:at + small] for at in starts], axis=0)

            up[0, tap] = block(2, 0).astype(BF16)
            down[0, tap] = block(2, 1).astype(BF16)
            keep_up[tap] = block(1, 0)
            up[1, tap] = block(1, 1).astype(BF16)
            down[1, tap] = block(3, 0).astype(BF16)
            keep_down[tap] = block(3, 1)
            own[0, tap] = block(0, 0)
            own[1, tap] = block(0, 1)


def weight_terms(norm, acts, quarters):
    rows, width, depth, chan = acts[0].shape
    q = chan // QUAD
    cells = QUAD * rows * width * depth
    tall = QUAD * rows + 2
    shapes = [jax.ShapeDtypeStruct((tall, width + 2, depth, q), BF16)]
    for taps in (XTAPS, 27 - XTAPS):
        shape = (taps, q // RING // 2, chan)
        shapes += [jax.ShapeDtypeStruct((2,) + shape, BF16)] * 2
        shapes += [jax.ShapeDtypeStruct(shape, F32)] * 2
        shapes += [jax.ShapeDtypeStruct((2,) + shape, F32)]
    return pl.pallas_call(
        functools.partial(weight_kernel, norm),
        out_shape=shapes,
        in_specs=[ANY] * 4 + [VMEM] * 6,
        out_specs=[VMEM] * 11,
        scratch_shapes=[
            pltpu.VMEM((QUAD * rows, width, depth, chan), BF16),
            pltpu.VMEM((9 * q, tall * width * depth), BF16),
            pltpu.SemaphoreType.DMA((4,)),
        ],
        compiler_params=params(),
        cost_estimate=pl.CostEstimate(
            flops=2 * 27 * q * cells * chan, bytes_accessed=10_000_000, transcendentals=0
        ),
    )(*acts, *quarters)


def input_kernel(held, own, above, across_low, across_high, below, *refs):
    send, keep, pass_on, weights, sem = refs
    j = quad_place()
    y = y_place()
    part = own.shape[1]
    low = across_low.shape[0]

    def at(s):
        return pl.ds(pl.multiple_of(lax.rem(y + s, RING) * part, part), part)

    pairs = [
        (own, weights.at[:, at(0)]),
        (above, weights.at[:, at(1)]),
        (across_low, weights.at[pl.ds(0, low), at(2)]),
        (across_high, weights.at[pl.ds(low, 27 - low), at(2)]),
        (below, weights.at[:, at(3)]),
    ]
    for c in run_copies(pairs, sem):
        c.wait()
    rows, width, depth, chan = keep.shape
    cells = rows * width * depth
    q = held.shape[3]
    taps = weights[...].reshape(9, 3, q, chan)
    for k, out in ((1, send.at[0]), (3, send.at[1]), (2, pass_on), (0, keep)):
        first = (j ^ k) * rows
        moved = []
        for n in range(9):
            a, b = n // 3 - 1, n % 3 - 1
            block = held[pl.ds(first + 1 - a, rows), 1 - b:1 - b + width]
            moved.append(block.reshape(cells, q))
        moved = jnp.concatenate(moved, axis=1)
        z = lax.rem(lax.broadcasted_iota(jnp.int32, (cells, chan), 0), depth)

        def term(c):
            return jnp.dot(moved, taps[:, c].reshape(9 * q, chan), preferred_element_type=F32)

        grad = term(1)
        grad = grad + zero_at(pltpu.roll(term(0), cells - 1, 0), z, depth - 1)
        grad = grad + zero_at(pltpu.roll(term(2), 1, 0), z, 0)
        out[...] = grad.reshape(rows, width, depth, chan)


def input_terms(held, parts):
    tall, width, depth, q = held.shape
    chan = QUAD * q
    block = ((tall - 2) // QUAD, width - 2, depth, chan)
    return pl.pallas_call(
        input_kernel,
        out_shape=[
            jax.ShapeDtypeStruct((2,) + block, F32),
            jax.ShapeDtypeStruct(block, F32),
            jax.ShapeDtypeStruct(block, F32),
        ],
        in_specs=[VMEM] + [ANY] * 5,
        out_specs=[VMEM] * 3,
        scratch_shapes=[pltpu.VMEM((27, q, chan), BF16), pltpu.SemaphoreType.DMA((5,))],
        compiler_params=params(),
        cost_estimate=pl.CostEstimate(
            flops=2 * 27 * tall * width * depth * q * chan, bytes_accessed=10_000_000, transcendentals=0
        ),
    )(held, *parts)


def finish_kernel(pre, keep, near, far, out):
    value = pre[...].astype(F32)
    s = jax.nn.sigmoid(value)
    grad = keep[...] + near[0] + far[...].astype(F32)
    out[...] = (grad * s * (1.0 + value * (1.0 - s))).astype(BF16)


def finish(pre_act, keep, near, far):
    return pl.pallas_call(
        finish_kernel,
        out_shape=jax.ShapeDtypeStruct(pre_act.shape, BF16),
        in_specs=[VMEM] * 4,
        out_specs=VMEM,
        compiler_params=params(),
    )(pre_act, keep, near, far)


def next_kernel(*refs):
    for n, out in enumerate(refs[8:]):
        came, keep = refs[2 * n:2 * n + 2]
        out[...] = (came[0].astype(F32) + keep[...]).astype(BF16)


def next_step(*parts):
    keeps = parts[1::2]
    return pl.pallas_call(
        next_kernel,
        out_shape=[jax.ShapeDtypeStruct(k.shape, BF16) for k in keeps],
        in_specs=[VMEM] * 8,
        out_specs=[VMEM] * 4,
        compiler_params=params(),
    )(*parts)


def split_kernel(*refs):
    for group in range(2):
        own, from_low, from_high, last_low, last_high = refs[5 * group:5 * group + 5]
        outs = refs[10 + 4 * group:14 + 4 * group]
        size = own.shape[2] // 2
        low = own[0] + from_high[1].astype(F32) + last_low[...].astype(F32)
        high = own[1] + from_low[1].astype(F32) + last_high[...].astype(F32)
        blocks = (low[:, :size], low[:, size:], high[:, :size], high[:, size:])
        for block, out in zip(blocks, outs):
            out[...] = block.astype(out.dtype)


def split(*parts):
    shapes = []
    for own in parts[::5]:
        _, taps, rows, chan = own.shape
        shape = (taps, rows // 2, chan)
        shapes += [jax.ShapeDtypeStruct(shape, F32)] + [jax.ShapeDtypeStruct(shape, BF16)] * 3
    return pl.pallas_call(
        split_kernel,
        out_shape=shapes,
        in_specs=[VMEM] * 10,
        out_specs=[VMEM] * 8,
        compiler_params=params(),
    )(*parts)


def join_kernel(*refs):
    out = refs[-1]
    x = x_place()
    size = refs[0].shape[1]
    low = refs[0].shape[0]
    for piece, part, k in zip(refs, (0, 1) * RING, (0, 0, 3, 3, 1, 1, 2, 2)):
        at = pl.ds(pl.multiple_of(lax.rem(x + k, RING) * size, size), size)
        first = part * low
        out[first:first + piece.shape[0], at] = piece[...].astype(F32)


def gather_x(low, high):
    low_below, high_above = along_x(low.astype(BF16), 1), along_x(high.astype(BF16), -1)
    high_below, low_above = along_x(high, 1), along_x(low, -1)
    low_far, high_far = along_x(low_below, 1), along_x(high_above, -1)
    return low, high, low_below, high_below, low_above, high_above, low_far, high_far


def join(pieces):
    _, size, chan = pieces[0].shape
    return pl.pallas_call(
        join_kernel,
        out_shape=jax.ShapeDtypeStruct((27, RING * size, chan), F32),
        in_specs=[VMEM] * 8,
        out_specs=VMEM,
        compiler_params=params(),
    )(*pieces)


def body(pre_act, cot, weight):
    rows, width, depth, chan = pre_act.shape
    norm = 1.0 / math.sqrt(rows * lax.axis_size("gy") * width * lax.axis_size("gx") * depth)
    j = quad_place()
    barrier = lax.optimization_barrier

    count = lax.axis_size("gy")
    pairs = [(g, g + 1) for g in range(QUAD - 1, count - 1, QUAD)]
    pairs = pairs + [(t, s) for s, t in pairs]
    extra = lax.ppermute(jnp.where(j == 0, cot[0], cot[rows - 1]), "gy", pairs)
    act = jax.nn.silu(pre_act.astype(F32)).astype(BF16)
    far = swap(act, 2)
    near = swap(act, 1)
    own_quarters = quarters_of(own_kernel, rows, cot)
    extra, near, own_quarters = barrier((extra, near, own_quarters))
    quarters = quarters_of(extra_kernel, rows + 1, extra, *own_quarters)
    quarters, weight = barrier((quarters, weight))
    above = along_y(weight, -1, True)
    below = along_y(weight, 1, True)
    quarters = [quarters[0]] + [swap(quarters[k], k) for k in (1, 2, 3)]
    quarters, far = barrier((quarters, far))
    acts = [act, near, far, swap(far, 1)]
    even, odd = sides(quarters)
    even, odd = swap_x(even, 0), swap_x(odd, 1)
    even, odd, above, below = barrier((even, odd, above, below))
    taps = XTAPS
    parts = [weight, above, along_y(below[:taps], 1, True), along_y(above[taps:], -1, True), below]

    held, *terms = weight_terms(norm, acts, [*quarters, even, odd])
    held, terms = barrier((held, terms))
    xup, xdown, xkeep_up, xkeep_down, xown = terms[:5]
    yup, ydown, ykeep_up, ykeep_down, yown = terms[5:]
    xlow, xhigh = along_x(xup, 1), along_x(xdown, -1)
    ylow, yhigh = along_y(yup, 1, True), along_y(ydown, -1, True)
    grads = input_terms(held, parts)
    grads, xlow, xhigh, ylow, yhigh = barrier((grads, xlow, xhigh, ylow, yhigh))
    send, keep, pass_on = grads
    got = swap(send, 1)
    xup, xdown, yup, ydown = next_step(
        xlow, xkeep_up, xhigh, xkeep_down, ylow, ykeep_up, yhigh, ykeep_down
    )
    xlast = along_x(xup, 1), along_x(xdown, -1)
    ylast = along_y(yup, 1, True), along_y(ydown, -1, True)
    xlast, ylast, got = barrier((xlast, ylast, got))
    blocks = split(xown, xlow, xhigh, *xlast, yown, ylow, yhigh, *ylast)

    low, high = blocks[0], blocks[4]
    lows = [along_y(block, r, True) for r, block in zip((1, 2, 3), blocks[1:4])]
    highs = [along_x(block, r) for r, block in zip((1, 2, 3), blocks[5:])]
    for other in lows:
        low = low + other.astype(F32)
    for other in highs:
        high = high + other.astype(F32)
    count = lax.axis_size("gx")
    mine = jnp.concatenate([low.astype(BF16), high.astype(BF16)])
    other = lax.ppermute(mine, "gx", [(g, g ^ 1) for g in range(count)])
    other, passed = barrier((other, (pass_on + got[1]).astype(BF16)))
    far_grad = swap(passed, 2)
    low, high = low + other[:taps].astype(F32), high + other[taps:].astype(F32)
    pieces = gather_x(low, high)
    grad_pre = finish(pre_act, keep, got, far_grad)
    grad_pre, pieces = barrier((grad_pre, pieces))
    return (grad_pre, join(pieces))


def solution(mesh):
    return jax.shard_map(
        body,
        mesh=mesh,
        in_specs=(P("gy", "gx", None, None), P("gy", "gx", None, None), P(None, "gy", None)),
        out_specs=(P("gy", "gx", None, None), P(None, "gy", None)),
        check_vma=False,
    )
```

```python
import functools
import math

import jax
import jax.numpy as jnp
from jax import lax
from jax.experimental import pallas as pl
from jax.experimental.pallas import tpu as pltpu
from jax.sharding import PartitionSpec as P

QUAD = 4
RING = 4
XTAPS = 14
F32 = jnp.float32
BF16 = jnp.bfloat16
ANY = pl.BlockSpec(memory_space=pl.ANY)
VMEM = pl.BlockSpec(memory_space=pltpu.VMEM)
LIMIT = 24 * 1024 * 1024


def params():
    return pltpu.CompilerParams(vmem_limit_bytes=LIMIT)


def small_cost():
    return pl.CostEstimate(flops=1000, bytes_accessed=1000, transcendentals=0)


def quad_place():
    return lax.rem(lax.axis_index("gy"), QUAD)


def x_place():
    return lax.div(lax.axis_index("gx"), 2)


def y_place():
    return lax.div(lax.axis_index("gy"), QUAD)


def swap(block, k):
    count = lax.axis_size("gy")
    return lax.ppermute(block, "gy", [(g, g ^ k) for g in range(count)])


def along_y(block, step, ring):
    count = lax.axis_size("gy")
    pairs = [(g, g + QUAD * step) for g in range(count)]
    if ring:
        pairs = [(s, t % count) for s, t in pairs]
    return lax.ppermute(block, "gy", [(s, t) for s, t in pairs if 0 <= t < count])


def along_x(block, step):
    count = lax.axis_size("gx")
    return lax.ppermute(block, "gx", [(g, (g + 2 * step) % count) for g in range(count)])


def swap_x(block, first):
    count = lax.axis_size("gx")
    pairs = [(g, g + 1) for g in range(first, count - 1, 2)]
    return lax.ppermute(block, "gx", pairs + [(t, s) for s, t in pairs])


def zero_at(value, z, edge):
    return jnp.where(z == edge, 0.0, value)


def pick(block, k):
    chan = block.shape[-1]
    q = chan // QUAD
    part = q // RING
    source = lax.broadcasted_iota(jnp.int32, (chan, q), 0)
    place = lax.broadcasted_iota(jnp.int32, (chan, q), 1)
    base = lax.div(place, part) * q + lax.rem(place, part) + (quad_place() ^ k) * part
    matrix = jnp.where(source == base, 1.0, 0.0).astype(BF16)
    got = jnp.dot(block.reshape(-1, chan), matrix, preferred_element_type=F32)
    return got.astype(BF16).reshape(block.shape[:-1] + (q,))


def own_kernel(cot, *quarters):
    for k, out in enumerate(quarters):
        out[...] = pick(cot[...], k)


def extra_kernel(extra, q0, q1, q2, q3, *quarters):
    for k, (own, out) in enumerate(zip((q0, q1, q2, q3), quarters)):
        rows = own.shape[0]
        out[0:rows] = own[...]
        out[rows] = pick(extra[...], k)


def quarters_of(kernel, rows, *ins):
    width, depth, chan = ins[0].shape[-3:]
    quarter = jax.ShapeDtypeStruct((rows, width, depth, chan // QUAD), BF16)
    return pl.pallas_call(
        kernel,
        out_shape=[quarter] * QUAD,
        in_specs=[VMEM] * len(ins),
        out_specs=[VMEM] * QUAD,
        compiler_params=params(),
        cost_estimate=pl.CostEstimate(
            flops=1000, bytes_accessed=40_000_000 if kernel is own_kernel else 1000, transcendentals=0
        ),
    )(*ins)


def side_kernel(p0, p1, p2, p3, even, odd):
    width = p0.shape[1]
    is_odd = lax.rem(lax.axis_index("gx"), 2) == 1
    for k, p in enumerate((p0, p1, p2, p3)):
        first, last = p[:, 0], p[:, width - 1]
        even[k] = jnp.where(is_odd, first, last)
        odd[k] = jnp.where(is_odd, last, first)


def sides(quarters):
    rows, _, depth, q = quarters[0].shape
    return pl.pallas_call(
        side_kernel,
        out_shape=[jax.ShapeDtypeStruct((QUAD, rows, depth, q), BF16)] * 2,
        in_specs=[VMEM] * QUAD,
        out_specs=[VMEM] * 2,
        compiler_params=params(),
        cost_estimate=small_cost(),
    )(*quarters)


def turn_kernel(p0, p1, p2, p3, even, odd, held, out):
    j, x = quad_place(), x_place()
    is_odd = lax.rem(lax.axis_index("gx"), 2) == 1
    for k, p in enumerate((p0, p1, p2, p3)):
        rows, width = p.shape[0] - 1, p.shape[1]
        low = jnp.where(is_odd, even[k], odd[k])
        high = jnp.where(is_odd, odd[k], even[k])

        def put(at, part):
            held[at, 1:width + 1] = p[part]
            held[at, 0] = low[part]
            held[at, width + 1] = high[part]

        put(pl.ds(1 + (j ^ k) * rows, rows), slice(0, rows))
        pl.when((j ^ k) == 0)(functools.partial(put, 0, rows))
        pl.when((j ^ k) == QUAD - 1)(functools.partial(put, held.shape[0] - 1, rows))

    tall, width, depth, q = held.shape
    width -= 2
    cells = tall * width * depth
    part = q // RING
    small = part // RING
    place = lax.broadcasted_iota(jnp.int32, (q, q), 0)
    source = lax.broadcasted_iota(jnp.int32, (q, q), 1)
    xpart = lax.rem(lax.div(place, part) + x, RING)
    ypart = lax.rem(lax.div(lax.rem(place, part), small) + y_place(), RING)
    base = ypart * part + xpart * small + lax.rem(place, small)
    order = jnp.where(source == base, 1.0, 0.0).astype(BF16)
    z = lax.rem(lax.broadcasted_iota(jnp.int32, (q, cells), 1), depth)
    for b in (-1, 0, 1):
        moved = held[:, 1 - b:1 - b + width].reshape(cells, q)
        value = lax.dot_general(
            order, moved, (((1,), (1,)), ((), ())), preferred_element_type=F32
        )
        high = zero_at(pltpu.roll(value, cells - 1, 1), z, depth - 1)
        low = zero_at(pltpu.roll(value, 1, 1), z, 0)
        for c, v in enumerate((high, value, low)):
            at = ((b + 1) * 3 + c) * q
            out[at:at + q] = v.astype(BF16)


def turn(quarters, even, odd):
    rows, width, depth, q = quarters[0].shape
    width += 2
    tall = QUAD * (rows - 1) + 2
    return pl.pallas_call(
        turn_kernel,
        out_shape=[
            jax.ShapeDtypeStruct((tall, width, depth, q), BF16),
            jax.ShapeDtypeStruct((9 * q, tall * (width - 2) * depth), BF16),
        ],
        in_specs=[VMEM] * (QUAD + 2),
        out_specs=[VMEM] * 2,
        compiler_params=params(),
        cost_estimate=small_cost(),
    )(*quarters, even, odd)


def run_copies(pairs, sem):
    copies = [pltpu.make_async_copy(s, d, sem.at[n]) for n, (s, d) in enumerate(pairs)]
    for c in copies:
        c.start()
    return copies


def weight_kernel(norm, own_act, near, far, across, cot, *refs):
    groups, held, sem = (refs[:5], refs[5:10]), *refs[10:]
    j = quad_place()
    rows, width, depth, chan = own_act.shape
    pairs = []
    for k, piece in enumerate((own_act, near, far, across)):
        pairs.append((piece, held.at[pl.ds((j ^ k) * rows, rows)]))
    for c in run_copies(pairs, sem):
        c.wait()
    row = width * depth
    cells = QUAD * rows * row
    act = held[...].reshape(cells, chan)
    q = cot.shape[0] // 9
    small = q // RING // RING
    for n in range(9):
        a, b = n // 3 - 1, n % 3
        moved = cot[3 * b * q:3 * (b + 1) * q, (1 - a) * row:(1 - a) * row + cells]
        term = jnp.dot(moved, act, preferred_element_type=F32) * norm
        for c in range(3):
            tap = 3 * n + c
            by_y = tap >= XTAPS
            up, down, keep_up, keep_down, own = groups[by_y]
            tap -= XTAPS * by_y

            def block(r, h):
                spots = [(2 * h, r), (2 * h + 1, r)] if by_y else [(r, 2 * h), (r, 2 * h + 1)]
                starts = [c * q + (xr * RING + yr) * small for xr, yr in spots]
                return jnp.concatenate([term[at:at + small] for at in starts], axis=0)

            up[0, tap] = block(2, 0).astype(BF16)
            down[0, tap] = block(2, 1).astype(BF16)
            keep_up[tap] = block(1, 0)
            up[1, tap] = block(1, 1).astype(BF16)
            down[1, tap] = block(3, 0).astype(BF16)
            keep_down[tap] = block(3, 1)
            own[0, tap] = block(0, 0)
            own[1, tap] = block(0, 1)


def weight_terms(norm, acts, cot):
    rows, width, depth, chan = acts[0].shape
    q = chan // QUAD
    cells = QUAD * rows * width * depth
    shapes = []
    for taps in (XTAPS, 27 - XTAPS):
        shape = (taps, q // RING // 2, chan)
        shapes += [jax.ShapeDtypeStruct((2,) + shape, BF16)] * 2
        shapes += [jax.ShapeDtypeStruct(shape, F32)] * 2
        shapes += [jax.ShapeDtypeStruct((2,) + shape, F32)]
    return pl.pallas_call(
        functools.partial(weight_kernel, norm),
        out_shape=shapes,
        in_specs=[ANY] * 4 + [VMEM],
        out_specs=[VMEM] * 10,
        scratch_shapes=[
            pltpu.VMEM((QUAD * rows, width, depth, chan), BF16),
            pltpu.SemaphoreType.DMA((4,)),
        ],
        compiler_params=params(),
        cost_estimate=pl.CostEstimate(
            flops=2 * 27 * q * cells * chan, bytes_accessed=10_000_000, transcendentals=0
        ),
    )(*acts, cot)


def input_kernel(held, own, above, across_low, across_high, below, *refs):
    send, keep, pass_on, weights, sem = refs
    j = quad_place()
    y = y_place()
    part = own.shape[1]
    low = across_low.shape[0]

    def at(s):
        return pl.ds(pl.multiple_of(lax.rem(y + s, RING) * part, part), part)

    pairs = [
        (own, weights.at[:, at(0)]),
        (above, weights.at[:, at(1)]),
        (across_low, weights.at[pl.ds(0, low), at(2)]),
        (across_high, weights.at[pl.ds(low, 27 - low), at(2)]),
        (below, weights.at[:, at(3)]),
    ]
    for c in run_copies(pairs, sem):
        c.wait()
    rows, width, depth, chan = keep.shape
    cells = rows * width * depth
    q = held.shape[3]
    taps = weights[...].reshape(9, 3, q, chan)
    for k, out in ((1, send.at[0]), (3, send.at[1]), (2, pass_on), (0, keep)):
        first = (j ^ k) * rows
        moved = []
        for n in range(9):
            a, b = n // 3 - 1, n % 3 - 1
            block = held[pl.ds(first + 1 - a, rows), 1 - b:1 - b + width]
            moved.append(block.reshape(cells, q))
        moved = jnp.concatenate(moved, axis=1)
        z = lax.rem(lax.broadcasted_iota(jnp.int32, (cells, chan), 0), depth)

        def term(c):
            return jnp.dot(moved, taps[:, c].reshape(9 * q, chan), preferred_element_type=F32)

        grad = term(1)
        grad = grad + zero_at(pltpu.roll(term(0), cells - 1, 0), z, depth - 1)
        grad = grad + zero_at(pltpu.roll(term(2), 1, 0), z, 0)
        out[...] = grad.reshape(rows, width, depth, chan)


def input_terms(held, parts):
    tall, width, depth, q = held.shape
    chan = QUAD * q
    block = ((tall - 2) // QUAD, width - 2, depth, chan)
    return pl.pallas_call(
        input_kernel,
        out_shape=[
            jax.ShapeDtypeStruct((2,) + block, F32),
            jax.ShapeDtypeStruct(block, F32),
            jax.ShapeDtypeStruct(block, F32),
        ],
        in_specs=[VMEM] + [ANY] * 5,
        out_specs=[VMEM] * 3,
        scratch_shapes=[pltpu.VMEM((27, q, chan), BF16), pltpu.SemaphoreType.DMA((5,))],
        compiler_params=params(),
        cost_estimate=pl.CostEstimate(
            flops=2 * 27 * tall * width * depth * q * chan, bytes_accessed=10_000_000, transcendentals=0
        ),
    )(held, *parts)


def finish_kernel(pre, keep, near, far, out):
    value = pre[...].astype(F32)
    s = jax.nn.sigmoid(value)
    grad = keep[...] + near[0] + far[...].astype(F32)
    out[...] = (grad * s * (1.0 + value * (1.0 - s))).astype(BF16)


def finish(pre_act, keep, near, far):
    return pl.pallas_call(
        finish_kernel,
        out_shape=jax.ShapeDtypeStruct(pre_act.shape, BF16),
        in_specs=[VMEM] * 4,
        out_specs=VMEM,
        compiler_params=params(),
    )(pre_act, keep, near, far)


def next_kernel(*refs):
    for n, out in enumerate(refs[8:]):
        came, keep = refs[2 * n:2 * n + 2]
        out[...] = (came[0].astype(F32) + keep[...]).astype(BF16)


def next_step(*parts):
    keeps = parts[1::2]
    return pl.pallas_call(
        next_kernel,
        out_shape=[jax.ShapeDtypeStruct(k.shape, BF16) for k in keeps],
        in_specs=[VMEM] * 8,
        out_specs=[VMEM] * 4,
        compiler_params=params(),
    )(*parts)


def split_kernel(*refs):
    for group in range(2):
        own, from_low, from_high, last_low, last_high = refs[5 * group:5 * group + 5]
        outs = refs[10 + 4 * group:14 + 4 * group]
        size = own.shape[2] // 2
        low = own[0] + from_high[1].astype(F32) + last_low[...].astype(F32)
        high = own[1] + from_low[1].astype(F32) + last_high[...].astype(F32)
        blocks = (low[:, :size], low[:, size:], high[:, :size], high[:, size:])
        for block, out in zip(blocks, outs):
            out[...] = block.astype(out.dtype)


def split(*parts):
    shapes = []
    for own in parts[::5]:
        _, taps, rows, chan = own.shape
        shape = (taps, rows // 2, chan)
        shapes += [jax.ShapeDtypeStruct(shape, F32)] + [jax.ShapeDtypeStruct(shape, BF16)] * 3
    return pl.pallas_call(
        split_kernel,
        out_shape=shapes,
        in_specs=[VMEM] * 10,
        out_specs=[VMEM] * 8,
        compiler_params=params(),
    )(*parts)


def join_kernel(*refs):
    out = refs[-1]
    x = x_place()
    size = refs[0].shape[1]
    low = refs[0].shape[0]
    for piece, part, k in zip(refs, (0, 1) * RING, (0, 0, 3, 3, 1, 1, 2, 2)):
        at = pl.ds(pl.multiple_of(lax.rem(x + k, RING) * size, size), size)
        first = part * low
        out[first:first + piece.shape[0], at] = piece[...].astype(F32)


def gather_x(low, high):
    low_below, high_above = along_x(low.astype(BF16), 1), along_x(high.astype(BF16), -1)
    high_below, low_above = along_x(high, 1), along_x(low, -1)
    low_far, high_far = along_x(low_below, 1), along_x(high_above, -1)
    return low, high, low_below, high_below, low_above, high_above, low_far, high_far


def join(pieces):
    _, size, chan = pieces[0].shape
    return pl.pallas_call(
        join_kernel,
        out_shape=jax.ShapeDtypeStruct((27, RING * size, chan), F32),
        in_specs=[VMEM] * 8,
        out_specs=VMEM,
        compiler_params=params(),
    )(*pieces)


def body(pre_act, cot, weight):
    rows, width, depth, chan = pre_act.shape
    norm = 1.0 / math.sqrt(rows * lax.axis_size("gy") * width * lax.axis_size("gx") * depth)
    j = quad_place()
    barrier = lax.optimization_barrier

    count = lax.axis_size("gy")
    pairs = [(g, g + 1) for g in range(QUAD - 1, count - 1, QUAD)]
    pairs = pairs + [(t, s) for s, t in pairs]
    extra = lax.ppermute(jnp.where(j == 0, cot[0], cot[rows - 1]), "gy", pairs)
    act = jax.nn.silu(pre_act.astype(F32)).astype(BF16)
    far = swap(act, 2)
    near = swap(act, 1)
    own_quarters = quarters_of(own_kernel, rows, cot)
    extra, near, own_quarters = barrier((extra, near, own_quarters))
    quarters = quarters_of(extra_kernel, rows + 1, extra, *own_quarters)
    quarters, weight = barrier((quarters, weight))
    above = along_y(weight, -1, True)
    below = along_y(weight, 1, True)
    quarters = [quarters[0]] + [swap(quarters[k], k) for k in (1, 2, 3)]
    quarters, far = barrier((quarters, far))
    acts = [act, near, far, swap(far, 1)]
    even, odd = sides(quarters)
    even, odd = swap_x(even, 0), swap_x(odd, 1)
    even, odd, above, below = barrier((even, odd, above, below))
    taps = XTAPS
    parts = [weight, above, along_y(below[:taps], 1, True), along_y(above[taps:], -1, True), below]
    held, turned = turn(quarters, even, odd)

    terms = weight_terms(norm, acts, turned)
    held, terms = barrier((held, terms))
    xup, xdown, xkeep_up, xkeep_down, xown = terms[:5]
    yup, ydown, ykeep_up, ykeep_down, yown = terms[5:]
    xlow, xhigh = along_x(xup, 1), along_x(xdown, -1)
    ylow, yhigh = along_y(yup, 1, True), along_y(ydown, -1, True)
    grads = input_terms(held, parts)
    grads, xlow, xhigh, ylow, yhigh = barrier((grads, xlow, xhigh, ylow, yhigh))
    send, keep, pass_on = grads
    got = swap(send, 1)
    xup, xdown, yup, ydown = next_step(
        xlow, xkeep_up, xhigh, xkeep_down, ylow, ykeep_up, yhigh, ykeep_down
    )
    xlast = along_x(xup, 1), along_x(xdown, -1)
    ylast = along_y(yup, 1, True), along_y(ydown, -1, True)
    xlast, ylast, got = barrier((xlast, ylast, got))
    blocks = split(xown, xlow, xhigh, *xlast, yown, ylow, yhigh, *ylast)

    low, high = blocks[0], blocks[4]
    lows = [along_y(block, r, True) for r, block in zip((1, 2, 3), blocks[1:4])]
    highs = [along_x(block, r) for r, block in zip((1, 2, 3), blocks[5:])]
    for other in lows:
        low = low + other.astype(F32)
    for other in highs:
        high = high + other.astype(F32)
    count = lax.axis_size("gx")
    mine = jnp.concatenate([low.astype(BF16), high.astype(BF16)])
    other = lax.ppermute(mine, "gx", [(g, g ^ 1) for g in range(count)])
    other, passed = barrier((other, (pass_on + got[1]).astype(BF16)))
    far_grad = swap(passed, 2)
    low, high = low + other[:taps].astype(F32), high + other[taps:].astype(F32)
    pieces = gather_x(low, high)
    grad_pre = finish(pre_act, keep, got, far_grad)
    grad_pre, pieces = barrier((grad_pre, pieces))
    return (grad_pre, join(pieces))


def solution(mesh):
    return jax.shard_map(
        body,
        mesh=mesh,
        in_specs=(P("gy", "gx", None, None), P("gy", "gx", None, None), P(None, "gy", None)),
        out_specs=(P("gy", "gx", None, None), P(None, "gy", None)),
        check_vma=False,
    )
```
